32 devices in a mesh: dp: 8 (over y, x, core), tensor: 4 (over z).
Axes of the slice: x: 2, y: 2, z: 4, core: 2. Of those that a mesh axis runs over, the one named last changes fastest.
Arguments:
- inputs: bfloat16 [8192, 2048], P('dp'), may hold values from -6 to 6
- cotangent: bfloat16 [8192, 2048], P('dp'), may hold values from -6 to 6
- segments: int32 [8, 1024], P('dp'), may hold values from 0 to 3, never falling along the last dimension, each value on 1 to 512 neighbouring positions
- subsets: int32 [8], P('dp'), may hold values from 0 to 21
- ln1_gain: float32 [2048], replicated, may hold values from 0.5 to 1.5
- ln1_bias: float32 [2048], replicated, may hold values from -2 to 2
- qkv_weight: bfloat16 [2048, 6144], P(None, 'tensor'), may hold values from -0.125 to 0.125
- qkv_bias: float32 [6144], P('tensor'), may hold values from -2 to 2
- dense_weight: bfloat16 [2048, 2048], P('tensor'), may hold values from -0.5 to 0.5
- dense_bias: float32 [2048], replicated, may hold values from -3 to 3
- ln2_gain: float32 [2048], replicated, may hold values from 0.5 to 1.5
- ln2_bias: float32 [2048], replicated, may hold values from -2 to 2
- up_weight: bfloat16 [2048, 8192], P(None, 'tensor'), may hold values from -0.125 to 0.125
- up_bias: float32 [8192], P('tensor'), may hold values from -3 to 3
- down_weight: bfloat16 [8192, 2048], P('tensor'), may hold values from -0.0625 to 0.0625
- down_bias: float32 [2048], replicated, may hold values from -3 to 3
Outputs:
- out: bfloat16 [8192, 2048], P('dp')
- input_grad: bfloat16 [8192, 2048], P('dp')
- ln1_gain_grad: float32 [2048], replicated
- ln1_bias_grad: float32 [2048], replicated
- qkv_weight_grad: float32 [2048, 6144], P('dp', 'tensor')
- qkv_bias_grad: float32 [6144], P('tensor')
- dense_weight_grad: float32 [2048, 2048], P('tensor', 'dp')
- dense_bias_grad: float32 [2048], replicated
- ln2_gain_grad: float32 [2048], replicated
- ln2_bias_grad: float32 [2048], replicated
- up_weight_grad: float32 [2048, 8192], P('dp', 'tensor')
- up_bias_grad: float32 [8192], P('tensor')
- down_weight_grad: float32 [8192, 2048], P('tensor', 'dp')
- down_bias_grad: float32 [2048], replicated
- subset_rms: float32 [22, 2], replicated
The draws below stay inside these ranges and needn't reach their ends.
Inputs may be any that keep to these rules, and one draw needn't show every extreme that they name: `segments`: within each sequence the document numbers never fall; every document has 1 to 512 tokens and one has exactly 512.
All inputs are finite; a program needn't handle non-finite values.
Results may differ from the reference program's by a relative error of at most 0.0094.
Values sent between devices are 32-bit elements; how exact they have to be, the bound alone decides.
A program may use at most 256 MiB of HBM per device.

```python
import math
import jax
import jax.numpy as jnp
import numpy as np
from jax import lax

D = 2048
HEADS = 8
HS = 256
ROT = 64
FF = 8192
SUBSETS = 22
LEN = 1024
DOCS = 4
DOC_MOST = 512
SEQS = 8
TOKENS = 8192


def set_ends(drawn, own_key, low, largest):
    shape = drawn.shape
    index_at = [jax.random.randint(jax.random.fold_in(own_key, axis), (), 0, shape[axis]) for axis in range(len(shape))]
    drawn = drawn.at[tuple(index_at)].set(low)
    longest = shape.index(max(shape))
    index_at[longest] = (index_at[longest] + 1) % shape[longest]
    return drawn.at[tuple(index_at)].set(largest)


def block_scale(own_key, dims, split, low, largest):
    def one(dim, blocks):
        draws = jax.random.uniform(jax.random.fold_in(jax.random.fold_in(own_key, 6), dim), (blocks,), jnp.float32, low / len(split), largest / len(split))
        return jnp.repeat(jnp.exp(draws), dims[dim] // blocks).reshape((-1,) + (1,) * (len(dims) - dim - 1))

    factor_of = one(*split[0])
    for cut in split[1:]:
        factor_of = factor_of * one(*cut)
    return factor_of


def length_profile(amount, total, reach, skew):
    portions = [(1 << 20) // math.isqrt(rank ** skew) + 1 for rank in range(2, amount + 1)]
    spare, holding = total - reach - (amount - 1), [1] * (amount - 1)
    while spare > 0:
        free = [i for i in range(amount - 1) if holding[i] < reach]
        mass, remaining = sum([portions[i] for i in free]), spare
        for i in free:
            extra = min(reach - holding[i], max(1, remaining * portions[i] // mass), spare)
            holding[i] = holding[i] + extra
            spare = spare - extra
    return np.array([reach] + holding)


def ragged_sizes(rng, count, total, reach, skew):
    if count == 2:
        one = jax.random.randint(rng, (), max(1, total - reach), min(reach, total - 1) + 1)
        return jnp.stack([one, total - one])
    lengths = jnp.asarray(length_profile(count, total, reach, skew), jnp.int32)
    couples = (count - 1) // 2
    donor, taker = lengths[1:1 + 2 * couples:2], lengths[2:2 + 2 * couples:2]
    slack = jnp.minimum(donor - 1, reach - taker)
    shifted = jax.random.randint(jax.random.fold_in(rng, 1), (couples,), 0, 1 << 20) % (slack + 1)
    lengths = lengths.at[1:1 + 2 * couples:2].set(donor - shifted).at[2:2 + 2 * couples:2].set(taker + shifted)
    return lengths[jax.random.permutation(jax.random.fold_in(rng, 2), count)]


def gaussian(stream_key, dims, scale, most, cuts=(), kind=jnp.bfloat16):
    level = block_scale(stream_key, dims, cuts, -0.22, 0.18) if cuts else 1.0
    values = jax.random.normal(stream_key, dims, jnp.float32) * scale * level
    return jnp.minimum(jnp.maximum(values, -most), most).astype(kind)


def setup_inputs(seed: int = 0) -> dict:
    key_of = jax.random.split(jax.random.key(seed), 17)
    return {
        "inputs": gaussian(key_of[0], (TOKENS, D), 1.0, 6.0, ((0, 8),)),
        "cotangent": gaussian(key_of[1], (TOKENS, D), 1.0, 6.0, ((0, 8),)),
        "segments": jax.vmap(lambda own: jnp.searchsorted(jnp.cumsum(ragged_sizes(own, DOCS, LEN, DOC_MOST, 1)), jnp.arange(LEN), side="right"))(jax.random.split(key_of[2], SEQS)).reshape((SEQS, LEN)).astype(jnp.int32),
        "subsets": set_ends(jax.random.randint(key_of[3], (SEQS,), 0, SUBSETS), jax.random.fold_in(key_of[3], 1), 0, SUBSETS - 1).astype(jnp.int32),
        "ln1_gain": jnp.clip(1.0 + 0.1 * jax.random.normal(key_of[4], (D,), jnp.float32), 0.5, 1.5),
        "ln1_bias": gaussian(key_of[5], (D,), 0.3, 2.0, (), jnp.float32),
        "qkv_weight": gaussian(key_of[6], (D, 3 * HEADS * HS), D ** -0.5, 0.125, ((1, 4),)),
        "qkv_bias": gaussian(key_of[7], (3 * HEADS * HS,), 0.3, 2.0, ((0, 4),), jnp.float32),
        "dense_weight": gaussian(key_of[8], (HEADS * HS, D), (HEADS * HS // 16) ** -0.5, 0.5, ((0, 4),)),
        "dense_bias": gaussian(key_of[9], (D,), 0.5, 3.0, (), jnp.float32),
        "ln2_gain": jnp.clip(1.0 + 0.1 * jax.random.normal(key_of[10], (D,), jnp.float32), 0.5, 1.5),
        "ln2_bias": gaussian(key_of[11], (D,), 0.3, 2.0, (), jnp.float32),
        "up_weight": gaussian(key_of[12], (D, FF), D ** -0.5, 0.125, ((1, 4),)),
        "up_bias": gaussian(key_of[13], (FF,), 0.5, 3.0, ((0, 4),), jnp.float32),
        "down_weight": gaussian(key_of[14], (FF, D), FF ** -0.5, 0.0625, ((0, 4),)),
        "down_bias": gaussian(key_of[15], (D,), 0.5, 3.0, (), jnp.float32),
    }


@jax.custom_vjp
def low(v):
    return lax.optimization_barrier(v.astype(jnp.bfloat16)).astype(jnp.float32)

@jax.custom_vjp
def low_back(v):
    return v

def low_keep(v):
    return (low(v), None)

def low_pass(kept, grad):
    return (grad,)

def back_keep(v):
    return (v, None)

def back_low(kept, grad):
    return (low(grad),)
low.defvjp(low_keep, low_pass)
low_back.defvjp(back_keep, back_low)
HIGHEST_PRECISION = lax.Precision.HIGHEST
EPSILON = 1e-05
MASKED_SCORE = -1000000000.0

def matmul(left, right):
    return jnp.dot(left, right, precision=HIGHEST_PRECISION)

def layer_norm(resid, norm_gain, norm_bias):
    centre = resid - lax.optimization_barrier(jnp.mean(resid, axis=-1, keepdims=True))
    variance = lax.optimization_barrier(jnp.mean(centre * centre, axis=-1, keepdims=True))
    return centre * lax.rsqrt(variance + EPSILON) * norm_gain + norm_bias

def rotary_tables(length):
    half_rot = ROT // 2
    frequency = 10000.0 ** (-(2.0 * jnp.arange(half_rot, dtype=jnp.float32)) / ROT)
    angles = jnp.arange(length, dtype=jnp.float32)[:, None] * frequency[None, :]
    angles = jnp.concatenate([angles, angles], axis=1)
    return (jnp.cos(angles), jnp.sin(angles))

def rotate(heads_in, cosine, sine_table):
    rot_part = heads_in[..., :ROT]
    turned = jnp.concatenate([-rot_part[..., ROT // 2:], rot_part[..., :ROT // 2]], axis=-1)
    rot_part = rot_part * cosine[:, None, :] + turned * sine_table[:, None, :]
    return jnp.concatenate([rot_part, heads_in[..., ROT:]], axis=-1)

def block_forward(resid, segment_row, ln1_gain, ln1_bias, qkv_weight, qkv_bias, dense_weight, dense_bias, ln2_gain, ln2_bias, up_weight, up_bias, down_weight, down_bias):
    length = resid.shape[0]
    first_norm = low(layer_norm(resid, ln1_gain, ln1_bias))
    joined = low_back(matmul(first_norm, qkv_weight) + qkv_bias).reshape(length, HEADS, 3, HS)
    cosine, sine_table = rotary_tables(length)
    queries = low(rotate(joined[:, :, 0], cosine, sine_table))
    key_rows = low(rotate(joined[:, :, 1], cosine, sine_table))
    values = low(joined[:, :, 2])
    scores = jnp.einsum('qhd,khd->hqk', queries, key_rows, precision=HIGHEST_PRECISION) * HS ** (-0.5)
    places = jnp.arange(length)
    allowed = (segment_row[:, None] == segment_row[None, :]) & (places[None, :] <= places[:, None])
    scores = low_back(jnp.where(allowed[None], scores, MASKED_SCORE))
    attn_probs = low(jax.nn.softmax(scores, axis=-1))
    context = jnp.einsum('hqk,khd->qhd', attn_probs, values, precision=HIGHEST_PRECISION).reshape(length, HEADS * HS)
    attn_part = matmul(low(low_back(context)), dense_weight)
    second_norm = low(layer_norm(resid, ln2_gain, ln2_bias))
    hidden = low_back(matmul(second_norm, up_weight) + up_bias)
    active = jax.nn.gelu(hidden, approximate=False)
    mlp_part = matmul(low(active), down_weight)
    result = resid + attn_part + mlp_part + dense_bias + down_bias
    return (result, (context, active))

def reference(inputs, cotangent, segments, subsets, ln1_gain, ln1_bias, qkv_weight, qkv_bias, dense_weight, dense_bias, ln2_gain, ln2_bias, up_weight, up_bias, down_weight, down_bias):
    params = tuple((weight_arg.astype(jnp.float32) for weight_arg in (ln1_gain, ln1_bias, qkv_weight, qkv_bias, dense_weight, dense_bias, ln2_gain, ln2_bias, up_weight, up_bias, down_weight, down_bias)))
    resid_all = inputs.astype(jnp.float32).reshape(SEQS, LEN, D)
    grad_all = cotangent.astype(jnp.float32).reshape(SEQS, LEN, D)

    def per_sequence(running, seq_item):
        resid, grad_out, segment_row, subset_id = seq_item

        def forward(resid_in, *weights_in):
            return block_forward(resid_in, segment_row, *weights_in)
        result, pull_back, aux_pair = jax.vjp(forward, resid, *params, has_aux=True)
        context, active = aux_pair
        grads = pull_back(grad_out)
        grad_sums, stats = running
        grad_sums = tuple((total_grad + new_grad for total_grad, new_grad in zip(grad_sums, grads[1:])))
        subset_pick = (jnp.arange(SUBSETS) == subset_id).astype(jnp.float32)
        seq_stats = jnp.stack([jnp.sum(context * context), jnp.sum(active * active), jnp.sum(jnp.ones_like(active[:, 0]))])
        stats = stats + subset_pick[:, None] * seq_stats[None, :]
        return ((grad_sums, stats), (result.astype(jnp.bfloat16), grads[0].astype(jnp.bfloat16)))
    start_sums = tuple((jnp.zeros(weight_arg.shape, jnp.float32) for weight_arg in params))
    start_stats = jnp.zeros((SUBSETS, 3), jnp.float32)
    final_state, row_outputs = lax.scan(per_sequence, (start_sums, start_stats), (resid_all, grad_all, segments, subsets))
    grad_sums, stats = final_state
    out_rows, grad_rows = row_outputs
    ln1_gain_grad, ln1_bias_grad, qkv_weight_grad, qkv_bias_grad, dense_weight_grad, dense_bias_grad, ln2_gain_grad, ln2_bias_grad, up_weight_grad, up_bias_grad, down_weight_grad, down_bias_grad = grad_sums
    widths = jnp.array([HEADS * HS, FF], jnp.float32)
    subset_rms = jnp.sqrt(stats[:, :2] / (jnp.maximum(stats[:, 2:3], 1.0) * widths[None, :]))
    return (out_rows.reshape(TOKENS, D), grad_rows.reshape(TOKENS, D), ln1_gain_grad, ln1_bias_grad, qkv_weight_grad, qkv_bias_grad, dense_weight_grad, dense_bias_grad, ln2_gain_grad, ln2_bias_grad, up_weight_grad, up_bias_grad, down_weight_grad, down_bias_grad, subset_rms)
```

```python
import functools
import jax
import jax.numpy as jnp
from jax import lax
from jax.experimental import pallas as pl
from jax.experimental.pallas import tpu as pltpu
from jax.sharding import PartitionSpec as P

HEADS = 8
HS = 256
ROT = 64
FF = 8192
SUBSETS = 22
LEN = 1024


EPSILON = 1e-05
MASKED_SCORE = -1000000000.0

MESH=pl.DeviceIdType.MESH
CH=32; W=8; H=4
def line_kernel(n, p_ref, o_ref, near_in, far_in, own, low, s1, r1, s2, r2, lp, lo):
    d=lax.axis_index("dp"); t=lax.axis_index("tensor")
    near=t+1-2*lax.rem(t,2); far=3-t
    mid=(t==1)|(t==2)
    bar=pltpu.get_barrier_semaphore()
    pl.semaphore_signal(bar,inc=1,device_id=(d,near),device_id_type=MESH)
    @pl.when(mid)
    def _():
        pl.semaphore_signal(bar,inc=1,device_id=(d,far),device_id_type=MESH)
        pl.semaphore_wait(bar,2)
    @pl.when(jnp.logical_not(mid))
    def _():
        pl.semaphore_wait(bar,1)
    def rows(k): return pl.ds(pl.multiple_of(k*CH,CH),CH)
    def slot(k): return lax.rem(k,W)
    def send_part(k):
        return pltpu.make_async_remote_copy(src_ref=p_ref.at[rows(k)],dst_ref=near_in.at[slot(k)],send_sem=s1.at[slot(k)],recv_sem=r1.at[slot(k)],device_id=(d,near),device_id_type=MESH)
    def swap(k):
        return pltpu.make_async_remote_copy(src_ref=near_in.at[slot(k)],dst_ref=far_in.at[slot(k)],send_sem=s2.at[slot(k)],recv_sem=r2.at[slot(k)],device_id=(d,far),device_id_type=MESH)
    def send_sum(k):
        return pltpu.make_async_remote_copy(src_ref=far_in.at[slot(k)],dst_ref=near_in.at[slot(k)],send_sem=s1.at[slot(k)],recv_sem=r1.at[slot(k)],device_id=(d,near),device_id_type=MESH)
    def load_own(k):
        return pltpu.make_async_copy(p_ref.at[rows(k)],own.at[lax.rem(k,2)],lp.at[lax.rem(k,2)])
    def store(k):
        return pltpu.make_async_copy(low.at[lax.rem(k,2)],o_ref.at[rows(k)],lo.at[lax.rem(k,2)])
    def emit(k,ref):
        @pl.when(k>=2)
        def _(): store(k-2).wait()
        low[lax.rem(k,2)]=ref[slot(k)].astype(jnp.bfloat16)
        store(k).start()
    @pl.when(jnp.logical_not(mid))
    def _():
        @pl.loop(0,W)
        def _(k): send_part(k).start()
        @pl.loop(0,n)
        def _(k):
            send_sum(k).wait_recv()
            send_part(k).wait_send()
            emit(k,near_in)
            @pl.when(k+W<n)
            def _(): send_part(k+W).start()
    @pl.when(mid)
    def _():
        load_own(0).start(); load_own(1).start()
        @pl.loop(0,n+1)
        def _(k):
            @pl.when(k<n)
            def _():
                send_part(k).wait_recv()
                load_own(k).wait()
                near_in[slot(k)]=near_in[slot(k)]+own[lax.rem(k,2)]
                @pl.when(k>=H)
                def _(): send_sum(k-H).wait_send()
                swap(k).start()
                @pl.when(k+2<n)
                def _(): load_own(k+2).start()
            @pl.when(k>=1)
            def _():
                j=k-1
                swap(j).wait()
                far_in[slot(j)]=near_in[slot(j)]+far_in[slot(j)]
                send_sum(j).start()
                emit(j,far_in)
        @pl.loop(n-H,n)
        def _(k): send_sum(k).wait_send()
    store(n-2).wait(); store(n-1).wait()
def line_sum(p, cid=0):
    rows,cols=p.shape
    return pl.pallas_call(functools.partial(line_kernel,rows//CH),
        out_shape=jax.ShapeDtypeStruct((rows,cols),jnp.bfloat16),
        in_specs=[pl.BlockSpec(memory_space=pl.ANY)],out_specs=pl.BlockSpec(memory_space=pl.ANY),
        scratch_shapes=[pltpu.VMEM((W,CH,cols),jnp.float32),pltpu.VMEM((W,CH,cols),jnp.float32),pltpu.VMEM((2,CH,cols),jnp.float32),pltpu.VMEM((2,CH,cols),jnp.bfloat16),
          pltpu.SemaphoreType.DMA((W,)),pltpu.SemaphoreType.DMA((W,)),pltpu.SemaphoreType.DMA((W,)),pltpu.SemaphoreType.DMA((W,)),pltpu.SemaphoreType.DMA((2,)),pltpu.SemaphoreType.DMA((2,))],
        compiler_params=pltpu.CompilerParams(collective_id=cid,has_side_effects=True,vmem_limit_bytes=40*2**20),name="line_sum")(p)


def layer_norm(resid, norm_gain, norm_bias):
    centre = resid - jnp.mean(resid, axis=-1, keepdims=True)
    variance = jnp.mean(centre * centre, axis=-1, keepdims=True)
    return centre * lax.rsqrt(variance + EPSILON) * norm_gain + norm_bias


def rotary_tables(length):
    half_rot = ROT // 2
    frequency = 10000.0 ** (-(2.0 * jnp.arange(half_rot, dtype=jnp.float32)) / ROT)
    angles = jnp.arange(length, dtype=jnp.float32)[:, None] * frequency[None, :]
    angles = jnp.concatenate([angles, angles], axis=1)
    return (jnp.cos(angles), jnp.sin(angles))


def rotate(heads_in, cosine, sine_table):
    rot_part = heads_in[..., :ROT]
    turned = jnp.concatenate([-rot_part[..., ROT // 2 :], rot_part[..., : ROT // 2]], axis=-1)
    rot_part = rot_part * cosine[:, None, :] + turned * sine_table[:, None, :]
    return jnp.concatenate([rot_part, heads_in[..., ROT:]], axis=-1)


def gelu_exact(hidden):
    return jax.nn.gelu(hidden, approximate=False)


def dot_rows(left, right):
    return lax.dot_general(
        left, right, (((0,), (0,)), ((), ())), preferred_element_type=jnp.float32
    )


def dot_cols(left, right):
    return lax.dot_general(
        left, right, (((1,), (1,)), ((), ())), preferred_element_type=jnp.float32
    )


def masked_scores(query_block, key_rows, segment_row, row_start, score_scale):
    scores = (
        jnp.einsum("qhd,khd->hqk", query_block, key_rows, preferred_element_type=jnp.float32)
        * score_scale
    )
    query_places = row_start + jnp.arange(query_block.shape[0])
    key_places = jnp.arange(key_rows.shape[0])
    query_segs = lax.dynamic_slice_in_dim(segment_row, row_start, query_block.shape[0], 0)
    allowed = (query_segs[:, None] == segment_row[None, :]) & (
        key_places[None, :] <= query_places[:, None]
    )
    return jnp.where(allowed[None], scores, MASKED_SCORE)


def on_device(
    inputs,
    cotangent,
    segments,
    subsets,
    ln1_gain,
    ln1_bias,
    qkv_weight,
    qkv_bias,
    dense_weight,
    dense_bias,
    ln2_gain,
    ln2_bias,
    up_weight,
    up_bias,
    down_weight,
    down_bias,
):
    rows_here = inputs.shape[0]
    seqs_here = segments.shape[0]
    heads_here = dense_weight.shape[0] // HS
    block_rows = min(512, LEN)
    score_scale = HS ** (-0.5)
    resid = inputs.astype(jnp.float32)
    first_full, pull_first = jax.vjp(layer_norm, resid, ln1_gain, ln1_bias)
    first_norm = first_full.astype(jnp.bfloat16)
    joined = jnp.dot(first_norm, qkv_weight, preferred_element_type=jnp.float32) + qkv_bias
    joined = joined.reshape(seqs_here, LEN, heads_here, 3, HS)
    cosine, sine_table = rotary_tables(LEN)

    def turn(heads_in):
        return rotate(heads_in, cosine, sine_table)

    query_full, pull_turn = jax.vjp(turn, joined[:, :, :, 0])
    queries = query_full.astype(jnp.bfloat16)
    key_rows = turn(joined[:, :, :, 1]).astype(jnp.bfloat16)
    values = joined[:, :, :, 2].astype(jnp.bfloat16)

    def attend(seq_item):
        query_seq, key_seq, value_seq, segment_row = seq_item
        out_blocks = []
        total_blocks = []
        for row_start in range(0, LEN, block_rows):
            query_block = query_seq[row_start : row_start + block_rows]
            scores = masked_scores(query_block, key_seq, segment_row, row_start, score_scale)
            score_peak = jnp.max(scores, axis=-1, keepdims=True)
            weights = jnp.exp(scores - score_peak)
            weight_total = jnp.sum(weights, axis=-1, keepdims=True)
            attn_probs = (weights / weight_total).astype(jnp.bfloat16)
            out_blocks.append(
                jnp.einsum(
                    "hqk,khd->qhd", attn_probs, value_seq, preferred_element_type=jnp.float32
                )
            )
            total_blocks.append(score_peak + jnp.log(weight_total))
        return (jnp.concatenate(out_blocks, axis=0), jnp.concatenate(total_blocks, axis=1))

    context, log_totals = lax.map(attend, (queries, key_rows, values, segments))
    context_low = context.reshape(rows_here, heads_here * HS).astype(jnp.bfloat16)
    attn_part = jnp.dot(context_low, dense_weight, preferred_element_type=jnp.float32)
    second_full, pull_second = jax.vjp(layer_norm, resid, ln2_gain, ln2_bias)
    second_norm = second_full.astype(jnp.bfloat16)
    hidden = jnp.dot(second_norm, up_weight, preferred_element_type=jnp.float32) + up_bias
    active, pull_active = jax.vjp(gelu_exact, hidden)
    active_low = active.astype(jnp.bfloat16)
    branch_terms = attn_part + jnp.dot(active_low, down_weight, preferred_element_type=jnp.float32)
    first_here = lax.axis_index("tensor") == 1
    out_terms = branch_terms + jnp.where(first_here, resid + (dense_bias + down_bias), 0.0)
    context_seq = jnp.sum((context * context).reshape(seqs_here, -1), axis=1)
    active_seq = jnp.sum((active * active).reshape(seqs_here, -1), axis=1)
    count_seq = jnp.where(lax.axis_index("tensor") == 0, float(LEN), 0.0) * jnp.ones_like(
        context_seq
    )
    subset_pick = (subsets[:, None] == jnp.arange(SUBSETS)[None, :]).astype(jnp.float32)
    per_seq = jnp.stack([context_seq, active_seq, count_seq], axis=1)
    stats_local = jnp.sum(subset_pick[:, :, None] * per_seq[:, None, :], axis=0)
    stats_total = lax.psum(stats_local, ("dp", "tensor"))
    grad_full = cotangent.astype(jnp.float32)
    out_bias_grad = jnp.sum(grad_full, axis=0)
    down_grad = dot_rows(active_low, cotangent)
    dense_grad = dot_rows(context_low, cotangent)
    d_active = dot_cols(cotangent, down_weight)
    d_hidden = pull_active(d_active)[0].astype(jnp.bfloat16)
    up_bias_grad = jnp.sum(d_hidden, axis=0, dtype=jnp.float32)
    d_second = dot_cols(d_hidden, up_weight)
    dx_second, dgain_second, dbias_second = pull_second(d_second)
    d_context = dot_cols(cotangent, dense_weight).astype(jnp.bfloat16)
    d_context = d_context.reshape(seqs_here, LEN, heads_here, HS)

    def attend_back(seq_item):
        query_seq, key_seq, value_seq, segment_row, total_seq, dout_seq = seq_item
        query_grads = []
        key_grad = jnp.zeros(key_seq.shape, jnp.float32)
        value_grad = jnp.zeros(value_seq.shape, jnp.float32)
        for row_start in range(0, LEN, block_rows):
            query_block = query_seq[row_start : row_start + block_rows]
            dout_block = dout_seq[row_start : row_start + block_rows]
            scores = masked_scores(query_block, key_seq, segment_row, row_start, score_scale)
            attn_probs = jnp.exp(scores - total_seq[:, row_start : row_start + block_rows])
            d_probs = jnp.einsum(
                "qhd,khd->hqk", dout_block, value_seq, preferred_element_type=jnp.float32
            )
            inner = jnp.sum(attn_probs * d_probs, axis=-1, keepdims=True)
            d_scores = (attn_probs * (d_probs - inner)).astype(jnp.bfloat16)
            query_grads.append(
                jnp.einsum("hqk,khd->qhd", d_scores, key_seq, preferred_element_type=jnp.float32)
                * score_scale
            )
            key_grad = (
                key_grad
                + jnp.einsum(
                    "hqk,qhd->khd", d_scores, query_block, preferred_element_type=jnp.float32
                )
                * score_scale
            )
            value_grad = value_grad + jnp.einsum(
                "hqk,qhd->khd",
                attn_probs.astype(jnp.bfloat16),
                dout_block,
                preferred_element_type=jnp.float32,
            )
        return (jnp.concatenate(query_grads, axis=0), key_grad, value_grad)

    query_grad, key_grad, value_grad = lax.map(
        attend_back, (queries, key_rows, values, segments, log_totals, d_context)
    )
    d_joined = jnp.stack([pull_turn(query_grad)[0], pull_turn(key_grad)[0], value_grad], axis=3)
    d_joined = d_joined.reshape(rows_here, 3 * heads_here * HS).astype(jnp.bfloat16)
    qkv_bias_grad = jnp.sum(d_joined, axis=0, dtype=jnp.float32)
    d_first = dot_cols(d_joined, qkv_weight)
    dx_first, dgain_first, dbias_first = pull_first(d_first)
    qkv_part, dense_part, up_part, down_part = (
        lax.psum_scatter(dot_rows(first_norm, d_joined), "dp", scatter_dimension=0, tiled=True),
        lax.psum_scatter(dense_grad, "dp", scatter_dimension=1, tiled=True),
        lax.psum_scatter(dot_rows(second_norm, d_hidden), "dp", scatter_dimension=0, tiled=True),
        lax.psum_scatter(down_grad, "dp", scatter_dimension=1, tiled=True),
    )
    norm_part = jnp.stack([dgain_first, dbias_first, dgain_second, dbias_second], axis=0)
    grad_terms = dx_first + dx_second + jnp.where(first_here, grad_full, 0.0)
    sums = line_sum(jnp.concatenate([out_terms, grad_terms], axis=0))
    out, input_grad = sums[:rows_here], sums[rows_here:]
    norm_group = lax.psum(norm_part, "tensor")
    bias_qkv, bias_up, bias_out, norm_total = lax.psum(
        (qkv_bias_grad, up_bias_grad, out_bias_grad, norm_group), "dp"
    )
    widths = jnp.array([HEADS * HS, FF], jnp.float32)
    subset_rms = jnp.sqrt(
        stats_total[:, :2] / (jnp.maximum(stats_total[:, 2:3], 1.0) * widths[None, :])
    )
    return (
        out,
        input_grad,
        norm_total[0],
        norm_total[1],
        qkv_part,
        bias_qkv,
        dense_part,
        bias_out,
        norm_total[2],
        norm_total[3],
        up_part,
        bias_up,
        down_part,
        bias_out,
        subset_rms,
    )


def solution(mesh):
    placed = (
        P("dp", None),
        P("dp", None),
        P("dp", None),
        P("dp"),
        P(),
        P(),
        P(None, "tensor"),
        P("tensor"),
        P("tensor", None),
        P(),
        P(),
        P(),
        P(None, "tensor"),
        P("tensor"),
        P("tensor", None),
        P(),
    )
    return jax.shard_map(
        on_device,
        mesh=mesh,
        in_specs=placed,
        out_specs=(
            P("dp", None),
            P("dp", None),
            P(),
            P(),
            P("dp", "tensor"),
            P("tensor"),
            P("tensor", "dp"),
            P(),
            P(),
            P(),
            P("dp", "tensor"),
            P("tensor"),
            P("tensor", "dp"),
            P(),
            P(),
        ),
        check_vma=False,
    )
```

```python
import functools
import jax
import jax.numpy as jnp
from jax import lax
from jax.experimental import pallas as pl
from jax.experimental.pallas import tpu as pltpu
from jax.sharding import PartitionSpec as P

HEADS = 8
HS = 256
ROT = 64
FF = 8192
SUBSETS = 22
LEN = 1024


EPSILON = 1e-05
MASKED_SCORE = -1000000000.0
VMEM_ASK = 64 * 2**20

MESH = pl.DeviceIdType.MESH
F32 = jnp.float32
LOW = jnp.bfloat16
BLOCK = 256
CH = 32
PER = BLOCK // CH
WINDOW = 8
HELD = 4
TILE = 512
RSQRT2 = 0.7071067811865476
RSQRT2PI = 0.3989422804014327
SV = 8
S_GAIN1, S_BIAS1, S_GAIN2, S_BIAS2, S_STATS, S_UP, S_QKV, S_OUT = range(SV)
V_UP, V_GAIN1, V_GAIN2, V_BIAS2, V_OUT, V_PICK = range(6)


def dot_nn(left, right):
    return lax.dot_general(left, right, (((1,), (0,)), ((), ())), preferred_element_type=F32)


def dot_nt(left, right):
    return lax.dot_general(left, right, (((1,), (1,)), ((), ())), preferred_element_type=F32)


def at_tile(index, width):
    return pl.ds(pl.multiple_of(index * width, width), width)


def layer_kernel(
    ndp,
    vec, sv0, x_h, cot_h, n1_h, ctx_h, dq_h, up_h, down_h, dense_h, qkv_h,
    o_h, sv_o, gd_h, gu_h, p_h, n2_h, ad_h, au_h, bd_h, bu_h,
    a_t, cot_v, dh_v, dq_v, ctx_v, sv_v, sq_v, svd, svz,
    near_in, far_in, own, low,
    s1, r1, s2, r2, lp, lo, lsem, wsem, psem, nsem,
    ssv, rsv, ssz, rsz, sa, ra, sb, rb, ssem,
):
    d = lax.axis_index("dp")
    t = lax.axis_index("tensor")
    rows, cols = x_h.shape
    ff = up_h.shape[1]
    att = ctx_h.shape[1]
    qw = dq_h.shape[1]
    width = cols // ndp
    half = ndp // 2
    steps = rows // BLOCK
    chunks = 2 * rows // CH
    near = t + 1 - 2 * lax.rem(t, 2)
    far = 3 - t
    mid = (t == 1) | (t == 2)
    end = jnp.logical_not(mid)
    parity = lax.rem(d, 2)
    mate = d + 1 - 2 * parity
    here = lax.div(d, 2)
    add_here = jnp.where(t == 1, 1.0, 0.0).astype(F32)

    bar = pltpu.get_barrier_semaphore()
    for k in range(1, 4):
        pl.semaphore_signal(bar, inc=1, device_id=(d, lax.rem(t + k, 4)), device_id_type=MESH)

    @pl.loop(1, ndp)
    def _(k):
        pl.semaphore_signal(bar, inc=1, device_id=(lax.rem(d + k, ndp), t), device_id_type=MESH)

    def slot(k):
        return lax.rem(k, WINDOW)

    def send_part(k):
        return pltpu.make_async_remote_copy(
            src_ref=p_h.at[k], dst_ref=near_in.at[slot(k)], send_sem=s1.at[slot(k)],
            recv_sem=r1.at[slot(k)], device_id=(d, near), device_id_type=MESH)

    def swap(k):
        return pltpu.make_async_remote_copy(
            src_ref=near_in.at[slot(k)], dst_ref=far_in.at[slot(k)], send_sem=s2.at[slot(k)],
            recv_sem=r2.at[slot(k)], device_id=(d, far), device_id_type=MESH)

    def send_sum(k):
        return pltpu.make_async_remote_copy(
            src_ref=far_in.at[slot(k)], dst_ref=near_in.at[slot(k)], send_sem=s1.at[slot(k)],
            recv_sem=r1.at[slot(k)], device_id=(d, near), device_id_type=MESH)

    def load_own(k):
        return pltpu.make_async_copy(p_h.at[k], own.at[lax.rem(k, 2)], lp.at[lax.rem(k, 2)])

    def store(k):
        return pltpu.make_async_copy(low.at[lax.rem(k, 2)], o_h.at[k], lo.at[lax.rem(k, 2)])

    def emit(k, ref):
        @pl.when(k >= 2)
        def _():
            store(k - 2).wait()

        low[lax.rem(k, 2)] = ref[slot(k)].astype(LOW)
        store(k).start()

    LAG = 3

    def prime():
        @pl.when(end)
        def _():
            @pl.loop(0, WINDOW)
            def _(k):
                send_part(k).start()

        @pl.when(mid)
        def _():
            load_own(0).start()
            load_own(1).start()

    def tick(k):
        @pl.when(end & (k >= LAG) & (k < chunks + LAG))
        def _():
            j = k - LAG
            send_sum(j).wait_recv()
            send_part(j).wait_send()
            emit(j, near_in)

            @pl.when(j + WINDOW < chunks)
            def _():
                send_part(j + WINDOW).start()

        @pl.when(mid & (k < chunks))
        def _():
            send_part(k).wait_recv()
            load_own(k).wait()
            near_in[slot(k)] = near_in[slot(k)] + own[lax.rem(k, 2)]

            @pl.when(k >= HELD)
            def _():
                send_sum(k - HELD).wait_send()

            swap(k).start()

            @pl.when(k + 2 < chunks)
            def _():
                load_own(k + 2).start()

        @pl.when(mid & (k >= 1) & (k < chunks + 1))
        def _():
            j = k - 1
            swap(j).wait()
            far_in[slot(j)] = near_in[slot(j)] + far_in[slot(j)]
            send_sum(j).start()
            emit(j, far_in)

    def load_cot(r):
        return pltpu.make_async_copy(cot_h.at[at_tile(r, BLOCK)], cot_v.at[at_tile(r, BLOCK)], lsem.at[r])

    load_ctx = pltpu.make_async_copy(ctx_h, ctx_v, lsem.at[steps])
    load_dq = pltpu.make_async_copy(dq_h, dq_v, lsem.at[steps + 1])

    sv_v[...] = sv0[...]
    sq_v[...] = jnp.zeros_like(sq_v)

    def row_phase(up_v, down_v, dense_v, qkv_v, xs, pst, xhat, n2c, actc, rstd, m1, m2, xsem):
        ntile = ff // TILE
        dtile = cols // TILE

        def load_x(r):
            return pltpu.make_async_copy(x_h.at[at_tile(r, BLOCK)], xs.at[lax.rem(r, 2)], xsem.at[lax.rem(r, 2)])

        def load_up(j):
            return pltpu.make_async_copy(up_h.at[:, at_tile(j, TILE)], up_v.at[:, at_tile(j, TILE)], wsem.at[2 * j])

        def load_down(j):
            return pltpu.make_async_copy(down_h.at[at_tile(j, TILE)], down_v.at[at_tile(j, TILE)], wsem.at[2 * j + 1])

        load_dense = pltpu.make_async_copy(dense_h, dense_v, wsem.at[2 * ntile])
        load_qkv = pltpu.make_async_copy(qkv_h, qkv_v, wsem.at[2 * ntile + 1])
        load_x(0).start()
        for j in range(ntile):
            load_up(j).start()
            if j == 0:
                load_cot(0).start()
            load_down(j).start()
        load_ctx.start()
        load_dense.start()
        load_dq.start()
        load_qkv.start()
        for r in range(1, steps):
            load_cot(r).start()
        pl.semaphore_wait(bar, 3 + ndp - 1)

        def put_p(r, which):
            return pltpu.make_async_copy(pst, p_h.at[pl.ds((2 * r + which) * PER, PER)], psem)

        def put_n2(r):
            return pltpu.make_async_copy(n2c, n2_h.at[at_tile(r, BLOCK)], nsem)

        @pl.loop(0, steps)
        def _(r):
            rds = at_tile(r, BLOCK)
            xcur = xs.at[lax.rem(r, 2)]
            load_x(r).wait()
            load_cot(r).wait()

            @pl.when(r + 1 < steps)
            def _():
                load_x(r + 1).start()

            @pl.when(r > 0)
            def _():
                put_n2(r - 1).wait()

            @pl.loop(0, BLOCK // CH)
            def _(s):
                sds = at_tile(s, CH)
                xf = xcur[sds, :].astype(F32)
                centre = xf - jnp.mean(xf, axis=-1, keepdims=True)
                inv = lax.rsqrt(jnp.mean(centre * centre, axis=-1, keepdims=True) + EPSILON)
                xh = centre * inv
                xhat[sds, :] = xh
                rstd[sds, :] = jnp.broadcast_to(inv, (CH, 128))
                n2c[sds, :] = (xh * vec[V_GAIN2 : V_GAIN2 + 1, :] + vec[V_BIAS2 : V_BIAS2 + 1, :]).astype(LOW)

            put_n2(r).start()

            @pl.loop(0, ntile)
            def _(j):
                jds = at_tile(j, TILE)

                @pl.when(r == 0)
                def _():
                    load_up(j).wait()
                    load_down(j).wait()

                hidden = dot_nn(n2c[...], up_v[:, jds]) + vec[V_UP : V_UP + 1, jds]
                cum = 0.5 * (1.0 + lax.erf(hidden * RSQRT2))
                active = hidden * cum
                slope = cum + hidden * jnp.exp(-0.5 * hidden * hidden) * RSQRT2PI
                act_low = active.astype(LOW)
                actc[:, jds] = act_low
                a_t[jds, rds] = act_low.T
                sq_v[...] += jnp.sum((active * active).reshape(BLOCK // 8, 8, TILE), axis=0)
                d_hid = (dot_nt(cot_v[rds, :], down_v[jds, :]) * slope).astype(LOW)
                dh_v[rds, jds] = d_hid
                sv_v[S_UP : S_UP + 1, jds] += jnp.sum(d_hid.astype(F32), axis=0, keepdims=True)

            @pl.when(r > 0)
            def _():
                tick(3 * r - 2)
                put_p(r - 1, 1).wait()

            @pl.when(r == 0)
            def _():
                load_ctx.wait()
                load_dense.wait()

            a_t[pl.ds(ff, att), rds] = ctx_v[rds, :].T

            @pl.loop(0, dtile)
            def _(j):
                jds = at_tile(j, TILE)
                cot_tile = cot_v[rds, jds].astype(F32)
                sv_v[S_OUT : S_OUT + 1, jds] += jnp.sum(cot_tile, axis=0, keepdims=True)
                term = dot_nn(actc[...], down_v[:, jds]) + dot_nn(ctx_v[rds, :], dense_v[:, jds])
                term = term + add_here * (xcur[:, jds].astype(F32) + vec[V_OUT : V_OUT + 1, jds])
                pst[:, :, jds] = term.reshape(PER, CH, TILE)

            put_p(r, 0).start()

            @pl.when(r == 0)
            def _():
                load_dq.wait()
                load_qkv.wait()

            put_p(r, 0).wait()

            @pl.when(r == 0)
            def _():
                prime()

            @pl.when(r > 0)
            def _():
                tick(3 * r - 1)

            m1[...] = jnp.zeros_like(m1)
            m2[...] = jnp.zeros_like(m2)
            sv_v[S_QKV : S_QKV + 1, pl.ds(0, qw)] += jnp.sum(dq_v[rds, :].astype(F32), axis=0, keepdims=True)

            @pl.loop(0, dtile)
            def _(j):
                jds = at_tile(j, TILE)
                xh = xhat[:, jds]
                second = dot_nt(dh_v[rds, :], up_v[jds, :])
                sv_v[S_GAIN2 : S_GAIN2 + 1, jds] += jnp.sum(second * xh, axis=0, keepdims=True)
                sv_v[S_BIAS2 : S_BIAS2 + 1, jds] += jnp.sum(second, axis=0, keepdims=True)
                first = dot_nt(dq_v[rds, :], qkv_v[jds, :])
                sv_v[S_GAIN1 : S_GAIN1 + 1, jds] += jnp.sum(first * xh, axis=0, keepdims=True)
                sv_v[S_BIAS1 : S_BIAS1 + 1, jds] += jnp.sum(first, axis=0, keepdims=True)
                scaled = second * vec[V_GAIN2 : V_GAIN2 + 1, jds] + first * vec[V_GAIN1 : V_GAIN1 + 1, jds]
                pst[:, :, jds] = scaled.reshape(PER, CH, TILE)
                with_xh = scaled * xh
                for q in range(TILE // 128):
                    m1[...] += scaled[:, q * 128 : (q + 1) * 128]
                    m2[...] += with_xh[:, q * 128 : (q + 1) * 128]

            @pl.loop(0, PER)
            def _(s):
                sds = at_tile(s, CH)
                mean1 = jnp.sum(m1[sds, :], axis=-1, keepdims=True) * (1.0 / cols)
                mean2 = jnp.sum(m2[sds, :], axis=-1, keepdims=True) * (1.0 / cols)
                grad = rstd[sds, 0:1] * (pst[s] - mean1 - xhat[sds, :] * mean2)
                cot_rows = cot_v[pl.ds(pl.multiple_of(r * BLOCK + s * CH, CH), CH), :].astype(F32)
                pst[s] = grad + add_here * cot_rows

            put_p(r, 1).start()
            tick(3 * r)

        put_p(steps - 1, 1).wait()
        put_n2(steps - 1).wait()

    pl.run_scoped(
        row_phase,
        pltpu.VMEM((cols, ff), LOW), pltpu.VMEM((ff, cols), LOW), pltpu.VMEM((att, cols), LOW), pltpu.VMEM((cols, qw), LOW),
        pltpu.VMEM((2, BLOCK, cols), LOW), pltpu.VMEM((PER, CH, cols), F32), pltpu.VMEM((BLOCK, cols), F32),
        pltpu.VMEM((BLOCK, cols), LOW), pltpu.VMEM((BLOCK, ff), LOW), pltpu.VMEM((BLOCK, 128), F32),
        pltpu.VMEM((BLOCK, 128), F32), pltpu.VMEM((BLOCK, 128), F32), pltpu.SemaphoreType.DMA((2,)),
    )
    done = 3 * (steps - 1) + 1

    sv_v[S_STATS : S_STATS + 1, :] += jnp.sum(sq_v[...]) * vec[V_PICK : V_PICK + 1, :]
    svd[d] = sv_v[...]

    def give_dp(k):
        return pltpu.make_async_remote_copy(
            src_ref=sv_v, dst_ref=svd.at[d], send_sem=ssv.at[k], recv_sem=rsv.at[d],
            device_id=(lax.rem(d + k, ndp), t), device_id_type=MESH)

    def get_dp(k):
        other = lax.rem(d + k, ndp)
        return pltpu.make_async_remote_copy(
            src_ref=sv_v, dst_ref=svd.at[other], send_sem=ssv.at[k], recv_sem=rsv.at[other],
            device_id=(other, t), device_id_type=MESH)

    @pl.loop(1, ndp)
    def _(k):
        give_dp(k).start()

    def grad_phase(n1_v, n2_v, sd, su, gsem):
        load_n1 = pltpu.make_async_copy(n1_h, n1_v, gsem.at[0])
        load_n2 = pltpu.make_async_copy(n2_h, n2_v, gsem.at[1])
        load_n1.start()
        load_n2.start()

        def lanes(ref, e):
            if width % 128 == 0:
                return ref[:, at_tile(e, width)]
            pair = ref[:, at_tile(lax.div(e, 2), 2 * width)]
            odd = lax.rem(e, 2) == 1
            return jnp.where(odd, pair[:, width:].astype(F32), pair[:, :width].astype(F32)).astype(LOW)

        def give_d(i):
            return pltpu.make_async_remote_copy(
                src_ref=sd.at[0], dst_ref=ad_h.at[i], send_sem=sa.at[0], recv_sem=ra.at[i],
                device_id=(mate, t), device_id_type=MESH)

        def give_u(i):
            return pltpu.make_async_remote_copy(
                src_ref=su.at[0], dst_ref=au_h.at[i], send_sem=sa.at[1], recv_sem=ra.at[half + i],
                device_id=(mate, t), device_id_type=MESH)

        def slice_d(e, into, add):
            right = lanes(cot_v, e)

            @pl.loop(0, (ff + att) // TILE)
            def _(j):
                part = dot_nn(a_t[at_tile(j, TILE), :], right)
                if add:
                    part = part + into[at_tile(j, TILE), :]
                into[at_tile(j, TILE), :] = part

        def slice_u(e, into, add):
            left = lanes(n2_v, e).T

            @pl.loop(0, ff // TILE)
            def _(j):
                part = dot_nn(left, dh_v[:, at_tile(j, TILE)])
                if add:
                    part = part + into[:, at_tile(j, TILE)]
                into[:, at_tile(j, TILE)] = part

            left1 = lanes(n1_v, e).T

            @pl.loop(0, qw // TILE)
            def _(j):
                part = dot_nn(left1, dq_v[:, at_tile(j, TILE)])
                there = pl.ds(pl.multiple_of(ff + j * TILE, TILE), TILE)
                if add:
                    part = part + into[:, there]
                into[:, there] = part

        def own_slice(i, into, got, keep, out, first, compute):
            e = 2 * i + parity
            fetch = pltpu.make_async_copy(got.at[i], into, ssem)
            fetch.start()
            fetch.wait()
            compute(e, into, True)
            put = pltpu.make_async_copy(into, keep.at[i], ssem)
            put.start()
            put.wait()

            @pl.when(e == d)
            def _():
                stay = pltpu.make_async_copy(into, out.at[here], ssem)
                stay.start()
                stay.wait()

            @pl.when(e != d)
            def _():
                pltpu.make_async_remote_copy(
                    src_ref=keep.at[i], dst_ref=out.at[here], send_sem=sb.at[first + i],
                    recv_sem=rb.at[first + here], device_id=(e, t), device_id_type=MESH).start()

        @pl.loop(0, half + 1)
        def _(i):
            base = done + 3 * i

            @pl.when(i < half)
            def _():
                e = 2 * i + 1 - parity

                @pl.when(i > 0)
                def _():
                    give_d(i - 1).wait_send()

                slice_d(e, sd.at[0], False)
                give_d(i).start()

            tick(base)

            @pl.when(i == 0)
            def _():
                load_n1.wait()
                load_n2.wait()

            @pl.when(i < half)
            def _():
                e = 2 * i + 1 - parity

                @pl.when(i > 0)
                def _():
                    give_u(i - 1).wait_send()

                slice_u(e, su.at[0], False)
                give_u(i).start()

            tick(base + 1)

            @pl.when(i > 0)
            def _():
                give_d(i - 1).wait_recv()
                own_slice(i - 1, sd.at[1], ad_h, bd_h, gd_h, 0, slice_d)
                give_u(i - 1).wait_recv()
                own_slice(i - 1, su.at[1], au_h, bu_h, gu_h, half, slice_u)

            tick(base + 2)

        give_d(half - 1).wait_send()
        give_u(half - 1).wait_send()

    pl.run_scoped(
        grad_phase,
        pltpu.VMEM((rows, cols), LOW), pltpu.VMEM((rows, cols), LOW),
        pltpu.VMEM((2, ff + att, width), F32), pltpu.VMEM((2, width, ff + qw), F32), pltpu.SemaphoreType.DMA((2,)),
    )
    done2 = done + 3 * (half + 1)

    @pl.loop(1, ndp)
    def _(k):
        get_dp(k).wait_recv()
        give_dp(k).wait_send()

    total = svd[0]
    for i in range(1, ndp):
        total = total + svd[i]
    sv_o[0] = total
    svz[t] = total

    def give_z(k):
        return pltpu.make_async_remote_copy(
            src_ref=sv_o.at[0], dst_ref=svz.at[t], send_sem=ssz.at[k], recv_sem=rsz.at[t],
            device_id=(d, lax.rem(t + k, 4)), device_id_type=MESH)

    def get_z(k):
        other = lax.rem(t + k, 4)
        return pltpu.make_async_remote_copy(
            src_ref=sv_o.at[0], dst_ref=svz.at[other], send_sem=ssz.at[k], recv_sem=rsz.at[other],
            device_id=(d, other), device_id_type=MESH)

    for k in range(1, 4):
        give_z(k).start()

    @pl.loop(done2, chunks + LAG)
    def _(k):
        tick(k)

    for k in range(1, 4):
        get_z(k).wait_recv()
        give_z(k).wait_send()
    sv_o[1] = svz[0] + svz[1] + svz[2] + svz[3]

    @pl.when(mid)
    def _():
        @pl.loop(chunks - HELD, chunks)
        def _(k):
            send_sum(k).wait_send()

    store(chunks - 2).wait()
    store(chunks - 1).wait()

    @pl.loop(0, half)
    def _(i):
        @pl.when(i != here)
        def _():
            for keep, out, first in ((bd_h, gd_h, 0), (bu_h, gu_h, half)):
                sent = pltpu.make_async_remote_copy(
                    src_ref=keep.at[i], dst_ref=out.at[i], send_sem=sb.at[first + i],
                    recv_sem=rb.at[first + i], device_id=(2 * i + parity, t), device_id_type=MESH)
                sent.wait_send()
                sent.wait_recv()


def layer(ndp, vec, sv0, x, cot, n1, ctx, dq, up_w, down_w, dense_w, qkv_w):
    rows, cols = x.shape
    ff, att, qw = up_w.shape[1], ctx.shape[1], dq.shape[1]
    width, half, steps, chunks = cols // ndp, ndp // 2, rows // BLOCK, 2 * rows // CH
    any_spec = pl.BlockSpec(memory_space=pl.ANY)
    vmem_spec = pl.BlockSpec(memory_space=pltpu.VMEM)
    sem = pltpu.SemaphoreType.DMA
    return pl.pallas_call(
        functools.partial(layer_kernel, ndp),
        out_shape=[
            jax.ShapeDtypeStruct((chunks, CH, cols), LOW),
            jax.ShapeDtypeStruct((2, SV, cols), F32),
            jax.ShapeDtypeStruct((half, ff + att, width), F32),
            jax.ShapeDtypeStruct((half, width, ff + qw), F32),
            jax.ShapeDtypeStruct((chunks, CH, cols), F32),
            jax.ShapeDtypeStruct((rows, cols), LOW),
            jax.ShapeDtypeStruct((half, ff + att, width), F32),
            jax.ShapeDtypeStruct((half, width, ff + qw), F32),
            jax.ShapeDtypeStruct((half, ff + att, width), F32),
            jax.ShapeDtypeStruct((half, width, ff + qw), F32),
        ],
        in_specs=[vmem_spec, vmem_spec] + [any_spec] * 9,
        out_specs=[any_spec, vmem_spec] + [any_spec] * 8,
        scratch_shapes=[
            pltpu.VMEM((ff + att, rows), LOW), pltpu.VMEM((rows, cols), LOW), pltpu.VMEM((rows, ff), LOW),
            pltpu.VMEM((rows, qw), LOW), pltpu.VMEM((rows, att), LOW), pltpu.VMEM((SV, cols), F32),
            pltpu.VMEM((8, TILE), F32), pltpu.VMEM((ndp, SV, cols), F32), pltpu.VMEM((4, SV, cols), F32),
            pltpu.VMEM((WINDOW, CH, cols), F32), pltpu.VMEM((WINDOW, CH, cols), F32),
            pltpu.VMEM((2, CH, cols), F32), pltpu.VMEM((2, CH, cols), LOW),
            sem((WINDOW,)), sem((WINDOW,)), sem((WINDOW,)), sem((WINDOW,)), sem((2,)), sem((2,)),
            sem((steps + 2,)), sem((2 * (ff // TILE) + 2,)), sem, sem,
            sem((ndp,)), sem((ndp,)), sem((4,)), sem((4,)),
            sem((2,)), sem((2 * half,)), sem((2 * half,)), sem((2 * half,)), sem,
        ],
        compiler_params=pltpu.CompilerParams(
            collective_id=0, has_side_effects=True, vmem_limit_bytes=VMEM_ASK),
        cost_estimate=pl.CostEstimate(flops=10**11, bytes_accessed=2 * 10**8, transcendentals=0),
        name="layer",
    )(vec, sv0, x, cot, n1, ctx, dq, up_w, down_w, dense_w, qkv_w)


def layer_norm(resid, norm_gain, norm_bias):
    centre = resid - jnp.mean(resid, axis=-1, keepdims=True)
    variance = jnp.mean(centre * centre, axis=-1, keepdims=True)
    return centre * lax.rsqrt(variance + EPSILON) * norm_gain + norm_bias


def rotary_tables(length):
    half_rot = ROT // 2
    frequency = 10000.0 ** (-(2.0 * jnp.arange(half_rot, dtype=jnp.float32)) / ROT)
    angles = jnp.arange(length, dtype=jnp.float32)[:, None] * frequency[None, :]
    angles = jnp.concatenate([angles, angles], axis=1)
    return (jnp.cos(angles), jnp.sin(angles))


def rotate(heads_in, cosine, sine_table):
    rot_part = heads_in[..., :ROT]
    turned = jnp.concatenate([-rot_part[..., ROT // 2 :], rot_part[..., : ROT // 2]], axis=-1)
    rot_part = rot_part * cosine[:, None, :] + turned * sine_table[:, None, :]
    return jnp.concatenate([rot_part, heads_in[..., ROT:]], axis=-1)


def gelu_exact(hidden):
    return jax.nn.gelu(hidden, approximate=False)


def dot_rows(left, right):
    return lax.dot_general(
        left, right, (((0,), (0,)), ((), ())), preferred_element_type=jnp.float32
    )


def dot_cols(left, right):
    return lax.dot_general(
        left, right, (((1,), (1,)), ((), ())), preferred_element_type=jnp.float32
    )


def masked_scores(query_block, key_rows, segment_row, row_start, score_scale):
    scores = (
        jnp.einsum("qhd,khd->hqk", query_block, key_rows, preferred_element_type=jnp.float32)
        * score_scale
    )
    query_places = row_start + jnp.arange(query_block.shape[0])
    key_places = jnp.arange(key_rows.shape[0])
    query_segs = lax.dynamic_slice_in_dim(segment_row, row_start, query_block.shape[0], 0)
    allowed = (query_segs[:, None] == segment_row[None, :]) & (
        key_places[None, :] <= query_places[:, None]
    )
    return jnp.where(allowed[None], scores, MASKED_SCORE)


def on_device(
    ndp,
    inputs,
    cotangent,
    segments,
    subsets,
    ln1_gain,
    ln1_bias,
    qkv_weight,
    qkv_bias,
    dense_weight,
    dense_bias,
    ln2_gain,
    ln2_bias,
    up_weight,
    up_bias,
    down_weight,
    down_bias,
):
    rows_here = inputs.shape[0]
    seqs_here = segments.shape[0]
    heads_here = dense_weight.shape[0] // HS
    block_rows = min(512, LEN)
    score_scale = HS ** (-0.5)
    resid = inputs.astype(jnp.float32)
    first_full, pull_first = jax.vjp(layer_norm, resid, ln1_gain, ln1_bias)
    first_norm = first_full.astype(jnp.bfloat16)
    joined = jnp.dot(first_norm, qkv_weight, preferred_element_type=jnp.float32) + qkv_bias
    joined = joined.reshape(seqs_here, LEN, heads_here, 3, HS)
    cosine, sine_table = rotary_tables(LEN)

    def turn(heads_in):
        return rotate(heads_in, cosine, sine_table)

    query_full, pull_turn = jax.vjp(turn, joined[:, :, :, 0])
    queries = query_full.astype(jnp.bfloat16)
    key_rows = turn(joined[:, :, :, 1]).astype(jnp.bfloat16)
    values = joined[:, :, :, 2].astype(jnp.bfloat16)

    def attend(seq_item):
        query_seq, key_seq, value_seq, segment_row = seq_item
        out_blocks = []
        total_blocks = []
        for row_start in range(0, LEN, block_rows):
            query_block = query_seq[row_start : row_start + block_rows]
            scores = masked_scores(query_block, key_seq, segment_row, row_start, score_scale)
            score_peak = jnp.max(scores, axis=-1, keepdims=True)
            weights = jnp.exp(scores - score_peak)
            weight_total = jnp.sum(weights, axis=-1, keepdims=True)
            attn_probs = (weights / weight_total).astype(jnp.bfloat16)
            out_blocks.append(
                jnp.einsum(
                    "hqk,khd->qhd", attn_probs, value_seq, preferred_element_type=jnp.float32
                )
            )
            total_blocks.append(score_peak + jnp.log(weight_total))
        return (jnp.concatenate(out_blocks, axis=0), jnp.concatenate(total_blocks, axis=1))

    context, log_totals = lax.map(attend, (queries, key_rows, values, segments))
    context_low = context.reshape(rows_here, heads_here * HS).astype(jnp.bfloat16)
    context_sq = jnp.sum(context * context)
    d_context = dot_cols(cotangent, dense_weight).astype(jnp.bfloat16)
    d_context = d_context.reshape(seqs_here, LEN, heads_here, HS)

    def attend_back(seq_item):
        query_seq, key_seq, value_seq, segment_row, total_seq, dout_seq = seq_item
        query_grads = []
        key_grad = jnp.zeros(key_seq.shape, jnp.float32)
        value_grad = jnp.zeros(value_seq.shape, jnp.float32)
        for row_start in range(0, LEN, block_rows):
            query_block = query_seq[row_start : row_start + block_rows]
            dout_block = dout_seq[row_start : row_start + block_rows]
            scores = masked_scores(query_block, key_seq, segment_row, row_start, score_scale)
            attn_probs = jnp.exp(scores - total_seq[:, row_start : row_start + block_rows])
            d_probs = jnp.einsum(
                "qhd,khd->hqk", dout_block, value_seq, preferred_element_type=jnp.float32
            )
            inner = jnp.sum(attn_probs * d_probs, axis=-1, keepdims=True)
            d_scores = (attn_probs * (d_probs - inner)).astype(jnp.bfloat16)
            query_grads.append(
                jnp.einsum("hqk,khd->qhd", d_scores, key_seq, preferred_element_type=jnp.float32)
                * score_scale
            )
            key_grad = (
                key_grad
                + jnp.einsum(
                    "hqk,qhd->khd", d_scores, query_block, preferred_element_type=jnp.float32
                )
                * score_scale
            )
            value_grad = value_grad + jnp.einsum(
                "hqk,qhd->khd",
                attn_probs.astype(jnp.bfloat16),
                dout_block,
                preferred_element_type=jnp.float32,
            )
        return (jnp.concatenate(query_grads, axis=0), key_grad, value_grad)

    query_grad, key_grad, value_grad = lax.map(
        attend_back, (queries, key_rows, values, segments, log_totals, d_context)
    )
    d_joined = jnp.stack([pull_turn(query_grad)[0], pull_turn(key_grad)[0], value_grad], axis=3)
    d_joined = d_joined.reshape(rows_here, 3 * heads_here * HS).astype(jnp.bfloat16)
    model = inputs.shape[1]
    hidden_here = up_weight.shape[1]
    lane = jnp.arange(model)
    slot_of = 3 * subsets[0]
    count = jnp.where(lax.axis_index("tensor") == 0, float(LEN), 0.0)
    stats_row = jnp.where(lane == slot_of, context_sq, 0.0) + jnp.where(lane == slot_of + 2, count, 0.0)
    sv0 = jnp.zeros((SV, model), F32).at[S_STATS].set(stats_row)
    pick = (lane == slot_of + 1).astype(F32)
    blank = jnp.zeros((model,), F32)
    up_row = jnp.pad(up_bias, (0, model - hidden_here)) if hidden_here < model else up_bias
    vec = jnp.stack([up_row, ln1_gain, ln2_gain, ln2_bias, dense_bias + down_bias, pick, blank, blank])
    done = layer(
        ndp, vec, sv0, inputs, cotangent, first_norm, context_low, d_joined, up_weight, down_weight, dense_weight, qkv_weight)
    sums, small, grads_d, grads_u = done[:4]
    sums = sums.reshape(rows_here // BLOCK, 2, BLOCK, model)
    out = sums[:, 0].reshape(rows_here, model)
    input_grad = sums[:, 1].reshape(rows_here, model)
    down_part = jnp.sum(grads_d[:, :hidden_here], axis=0)
    dense_part = jnp.sum(grads_d[:, hidden_here:], axis=0)
    up_part = jnp.sum(grads_u[:, :, :hidden_here], axis=0)
    qkv_part = jnp.sum(grads_u[:, :, hidden_here:], axis=0)
    stats_total = small[1, S_STATS, : 3 * SUBSETS].reshape(SUBSETS, 3)
    widths = jnp.array([HEADS * HS, FF], jnp.float32)
    subset_rms = jnp.sqrt(
        stats_total[:, :2] / (jnp.maximum(stats_total[:, 2:3], 1.0) * widths[None, :])
    )
    bias_out = small[0, S_OUT]
    return (
        out,
        input_grad,
        small[1, S_GAIN1],
        small[1, S_BIAS1],
        qkv_part,
        small[0, S_QKV, : qkv_bias.shape[0]],
        dense_part,
        bias_out,
        small[1, S_GAIN2],
        small[1, S_BIAS2],
        up_part,
        small[0, S_UP, :hidden_here],
        down_part,
        bias_out,
        subset_rms,
    )


def solution(mesh):
    placed = (
        P("dp", None),
        P("dp", None),
        P("dp", None),
        P("dp"),
        P(),
        P(),
        P(None, "tensor"),
        P("tensor"),
        P("tensor", None),
        P(),
        P(),
        P(),
        P(None, "tensor"),
        P("tensor"),
        P("tensor", None),
        P(),
    )
    return jax.shard_map(
        functools.partial(on_device, mesh.shape["dp"]),
        mesh=mesh,
        in_specs=placed,
        out_specs=(
            P("dp", None),
            P("dp", None),
            P(),
            P(),
            P("dp", "tensor"),
            P("tensor"),
            P("tensor", "dp"),
            P(),
            P(),
            P(),
            P("dp", "tensor"),
            P("tensor"),
            P("tensor", "dp"),
            P(),
            P(),
        ),
        check_vma=False,
    )
```

```python
import functools

import jax
import jax.numpy as jnp
import numpy as np
from jax import lax
from jax.experimental import pallas as pl
from jax.experimental.pallas import tpu as pltpu
from jax.sharding import PartitionSpec as P

HEADS = 8
HS = 256
ROT = 64
FF = 8192
SUBSETS = 22
LEN = 1024


EPSILON = 1e-05
MASKED_SCORE = -1000000000.0


VMEM_ASK = 64 * 2**20

MESH = pl.DeviceIdType.MESH
F32 = jnp.float32
LOW = jnp.bfloat16
BLOCK = 256
REACH = 3
CH = 32
PER = BLOCK // CH
WINDOW = 8
HELD = 4
LAG = 5
PACED = 4
TILE = 512
SUB = 16
RSQRT2 = 0.7071067811865476
RSQRT2PI = 0.3989422804014327
SV = 8
S_GAIN1, S_BIAS1, S_GAIN2, S_BIAS2, S_STATS, S_UP, S_QKV, S_OUT = range(SV)
VROWS = 16
V_UP, V_GAIN1, V_BIAS1, V_GAIN2, V_BIAS2, V_OUT, V_QKV, V_CTX, V_ACT, V_COUNT = range(10)


def dot_nn(left, right):
    return lax.dot_general(left, right, (((1,), (0,)), ((), ())), preferred_element_type=F32)


def dot_nt(left, right):
    return lax.dot_general(left, right, (((1,), (1,)), ((), ())), preferred_element_type=F32)


def at_tile(index, width):
    return pl.ds(pl.multiple_of(index * width, width), width)


def turn_tables(packed):
    lane = lax.broadcasted_iota(jnp.int32, packed.shape, 1)
    half_rot = ROT // 2
    sine = pltpu.roll(packed, 64, 1)
    cosine = jnp.where(lane < ROT, packed, 1.0)
    from_upper = jnp.where(lane < half_rot, -sine, 0.0)
    from_lower = jnp.where((lane >= half_rot) & (lane < ROT), sine, 0.0)
    return cosine, from_upper, from_lower


def turn(head, tables, sign):
    cosine, from_upper, from_lower = tables
    low_part = head[:, :128]
    moved = pltpu.roll(low_part, 128 - ROT // 2, 1) * from_upper + pltpu.roll(low_part, ROT // 2, 1) * from_lower
    low_part = low_part * cosine + moved if sign > 0 else low_part * cosine - moved
    return jnp.concatenate([low_part, head[:, 128:]], axis=1)


def layer_kernel(
    ndp,
    vec, seg, x_h, cot_h, rot_h, up_h, down_h, dense_h, qkv_h,
    o_h, sv_o, gd_h, gu_h, gq_h, p_h, n1_h, n2_h, ad_h, au_h, aq_h, bd_h, bu_h, bq_h,
    a_t, cot_v, dh_v, dq_v, q_v, k_v, v_v, do_v, lse_v, rot_v, sv_v, sq_v, csq_v, svd, svz,
    near_in, far_in, own, low,
    s1, r1, s2, r2, lp, lo, lsem, wsem, psem, nsem,
    ssv, rsv, ssz, rsz, sa, ra, sb, rb, ssem,
):
    d = lax.axis_index("dp")
    t = lax.axis_index("tensor")
    rows, cols = x_h.shape
    ff = up_h.shape[1]
    att = dense_h.shape[0]
    heads = att // HS
    qw = qkv_h.shape[1]
    width = cols // ndp
    half = ndp // 2
    steps = rows // BLOCK
    chunks = 2 * rows // CH
    near = t + 1 - 2 * lax.rem(t, 2)
    far = 3 - t
    mid = (t == 1) | (t == 2)
    end = jnp.logical_not(mid)
    parity = lax.rem(d, 2)
    mate = d + 1 - 2 * parity
    here = lax.div(d, 2)
    add_here = jnp.where(t == 1, 1.0, 0.0).astype(F32)

    bar = pltpu.get_barrier_semaphore()
    for k in range(1, 4):
        pl.semaphore_signal(bar, inc=1, device_id=(d, lax.rem(t + k, 4)), device_id_type=MESH)

    @pl.loop(1, ndp)
    def _(k):
        pl.semaphore_signal(bar, inc=1, device_id=(lax.rem(d + k, ndp), t), device_id_type=MESH)

    def slot(k):
        return lax.rem(k, WINDOW)

    def send_part(k):
        return pltpu.make_async_remote_copy(
            src_ref=p_h.at[k], dst_ref=near_in.at[slot(k)], send_sem=s1.at[slot(k)],
            recv_sem=r1.at[slot(k)], device_id=(d, near), device_id_type=MESH)

    def swap(k):
        return pltpu.make_async_remote_copy(
            src_ref=near_in.at[slot(k)], dst_ref=far_in.at[slot(k)], send_sem=s2.at[slot(k)],
            recv_sem=r2.at[slot(k)], device_id=(d, far), device_id_type=MESH)

    def send_sum(k):
        return pltpu.make_async_remote_copy(
            src_ref=far_in.at[slot(k)], dst_ref=near_in.at[slot(k)], send_sem=s1.at[slot(k)],
            recv_sem=r1.at[slot(k)], device_id=(d, near), device_id_type=MESH)

    def load_own(k):
        return pltpu.make_async_copy(p_h.at[k], own.at[lax.rem(k, 2)], lp.at[lax.rem(k, 2)])

    def store(k):
        return pltpu.make_async_copy(low.at[lax.rem(k, 2)], o_h.at[k], lo.at[lax.rem(k, 2)])

    def emit(k, ref):
        @pl.when(k >= 2)
        def _():
            store(k - 2).wait()

        low[lax.rem(k, 2)] = ref[slot(k)].astype(LOW)
        store(k).start()

    def prime():
        @pl.when(end)
        def _():
            @pl.loop(0, WINDOW)
            def _(k):
                send_part(k).start()

        @pl.when(mid)
        def _():
            load_own(0).start()
            load_own(1).start()

    def tick(k):
        @pl.when(end & (k >= LAG) & (k < chunks + LAG))
        def _():
            j = k - LAG
            send_sum(j).wait_recv()
            send_part(j).wait_send()
            emit(j, near_in)

            @pl.when(j + WINDOW < chunks)
            def _():
                send_part(j + WINDOW).start()

        @pl.when(mid & (k < chunks))
        def _():
            send_part(k).wait_recv()
            load_own(k).wait()
            near_in[slot(k)] = near_in[slot(k)] + own[lax.rem(k, 2)]

            @pl.when(k >= HELD)
            def _():
                send_sum(k - HELD).wait_send()

            swap(k).start()

            @pl.when(k + 2 < chunks)
            def _():
                load_own(k + 2).start()

        @pl.when(mid & (k >= 1) & (k < chunks + 1))
        def _():
            j = k - 1
            swap(j).wait()
            far_in[slot(j)] = near_in[slot(j)] + far_in[slot(j)]
            send_sum(j).start()
            emit(j, far_in)

    ntile, dtile = ff // TILE, cols // TILE

    def load_cot(r):
        return pltpu.make_async_copy(cot_h.at[at_tile(r, BLOCK)], cot_v.at[at_tile(r, BLOCK)], lsem.at[r])

    def load_x(r, xs, xsem):
        return pltpu.make_async_copy(x_h.at[at_tile(r, BLOCK)], xs.at[lax.rem(r, 2)], xsem.at[lax.rem(r, 2)])

    def put_p(r, which, pst):
        first = pl.multiple_of(which * (chunks // 2) + r * PER, PER)
        return pltpu.make_async_copy(pst, p_h.at[pl.ds(first, PER)], psem)

    def seen(r):
        return pl.ds(pl.multiple_of(jnp.maximum(r - (REACH - 1), 0) * BLOCK, BLOCK), REACH * BLOCK)

    def allowed(r):
        keys = REACH * BLOCK
        first = jnp.maximum(r - (REACH - 1), 0) * BLOCK
        query_at = lax.broadcasted_iota(jnp.int32, (BLOCK, keys), 0) + r * BLOCK
        key_at = lax.broadcasted_iota(jnp.int32, (BLOCK, keys), 1) + first
        query_seg = jnp.broadcast_to(seg[0:1, at_tile(r, BLOCK)], (8, BLOCK)).T[:, 0:1]
        return (query_seg == seg[0:1, seen(r)]) & (key_at <= query_at)

    sv_v[...] = jnp.zeros_like(sv_v)
    sq_v[...] = jnp.zeros_like(sq_v)
    csq_v[...] = jnp.zeros_like(csq_v)
    score_scale = HS ** (-0.5)

    def with_inputs(up_v, qkv_v):
        def load_up(j):
            return pltpu.make_async_copy(up_h.at[:, at_tile(j, TILE)], up_v.at[:, at_tile(j, TILE)], wsem.at[2 * j])

        load_qkv = pltpu.make_async_copy(qkv_h, qkv_v, wsem.at[2 * ntile + 1])
        load_rot = pltpu.make_async_copy(rot_h, rot_v, lsem.at[steps])

        def forward_phase(down_v, dense_v, xs, pst, n1c, n2c, actc, slope, ctxc, xsem):
            def load_down(j):
                return pltpu.make_async_copy(down_h.at[at_tile(j, TILE)], down_v.at[at_tile(j, TILE)], wsem.at[2 * j + 1])

            load_dense = pltpu.make_async_copy(dense_h, dense_v, wsem.at[2 * ntile])
            load_x(0, xs, xsem).start()
            load_qkv.start()
            load_rot.start()
            load_cot(0).start()
            load_dense.start()
            for j in range(ntile):
                load_up(j).start()
            for j in range(ntile):
                load_down(j).start()
            for r in range(1, steps):
                load_cot(r).start()
            k_v[...] = jnp.zeros_like(k_v)
            v_v[...] = jnp.zeros_like(v_v)
            pl.semaphore_wait(bar, 3 + ndp - 1)

            def put_n(r):
                return (
                    pltpu.make_async_copy(n1c, n1_h.at[at_tile(r, BLOCK)], nsem.at[0]),
                    pltpu.make_async_copy(n2c, n2_h.at[at_tile(r, BLOCK)], nsem.at[1]),
                )

            @pl.loop(0, steps)
            def _(r):
                rds = at_tile(r, BLOCK)
                xcur = xs.at[lax.rem(r, 2)]
                load_x(r, xs, xsem).wait()

                @pl.when(r + 1 < steps)
                def _():
                    load_x(r + 1, xs, xsem).start()

                @pl.when(r > 0)
                def _():
                    for copy in put_n(r - 1):
                        copy.wait()

                @pl.loop(0, BLOCK // SUB, unroll=2)
                def _(s):
                    sds = at_tile(s, SUB)
                    xf = xcur[sds, :].astype(F32)
                    centre = xf - jnp.mean(xf, axis=-1, keepdims=True)
                    xh = centre * lax.rsqrt(jnp.mean(centre * centre, axis=-1, keepdims=True) + EPSILON)
                    n1c[sds, :] = (xh * vec[V_GAIN1 : V_GAIN1 + 1, :] + vec[V_BIAS1 : V_BIAS1 + 1, :]).astype(LOW)
                    n2c[sds, :] = (xh * vec[V_GAIN2 : V_GAIN2 + 1, :] + vec[V_BIAS2 : V_BIAS2 + 1, :]).astype(LOW)

                for copy in put_n(r):
                    copy.start()

                @pl.when(r == 0)
                def _():
                    load_qkv.wait()
                    load_rot.wait()

                tables = turn_tables(rot_v[rds, :])
                for h in range(heads):
                    for part in range(3):
                        at = pl.ds((3 * h + part) * HS, HS)
                        head = dot_nn(n1c[...], qkv_v[:, at]) + vec[V_QKV : V_QKV + 1, at]
                        if part < 2:
                            head = turn(head, tables, 1)
                        (q_v, k_v, v_v)[part][h, rds, :] = head.astype(LOW)

                load_cot(r).wait()

                @pl.when(r == 0)
                def _():
                    load_dense.wait()

                do_v[rds, :] = dot_nt(cot_v[rds, :], dense_v[...]).astype(LOW)

                ok = allowed(r)
                for h in range(heads):
                    scores = dot_nt(q_v[h, rds, :], k_v[h, seen(r), :]) * score_scale
                    scores = jnp.where(ok, scores, MASKED_SCORE)
                    peak = jnp.max(scores, axis=-1, keepdims=True)
                    weights = jnp.exp(scores - peak)
                    total = jnp.sum(weights, axis=-1, keepdims=True)
                    lse_v[rds, h * 64 : h * 64 + 64] = jnp.broadcast_to(peak + jnp.log(total), (BLOCK, 64))
                    context = dot_nn((weights / total).astype(LOW), v_v[h, seen(r), :])
                    csq_v[...] += jnp.sum((context * context).reshape(BLOCK // 8, 8, HS), axis=0)
                    context = context.astype(LOW)
                    ctxc[:, h * HS : (h + 1) * HS] = context
                    a_t[pl.ds(ff + h * HS, HS), rds] = context.T

                @pl.when(r > 0)
                def _():
                    tick(4 * r - 3)

                @pl.loop(0, ntile)
                def _(j):
                    jds = at_tile(j, TILE)

                    @pl.when(r == 0)
                    def _():
                        load_up(j).wait()

                    hidden = dot_nn(n2c[...], up_v[:, jds]) + vec[V_UP : V_UP + 1, jds]
                    cum = 0.5 * (1.0 + lax.erf(hidden * RSQRT2))
                    active = hidden * cum
                    slope[:, jds] = cum + hidden * jnp.exp(-0.5 * hidden * hidden) * RSQRT2PI
                    act_low = active.astype(LOW)
                    actc[:, jds] = act_low
                    sq_v[...] += jnp.sum((active * active).reshape(BLOCK // 8, 8, TILE), axis=0)

                @pl.when(r > 0)
                def _():
                    tick(4 * r - 2)

                @pl.when(r == 0)
                def _():
                    @pl.loop(0, ntile)
                    def _(j):
                        load_down(j).wait()

                @pl.loop(0, dtile)
                def _(j):
                    jds = at_tile(j, TILE)
                    term = dot_nn(actc[...], down_v[:, jds]) + dot_nn(ctxc[...], dense_v[:, jds])
                    term = term + add_here * (xcur[:, jds].astype(F32) + vec[V_OUT : V_OUT + 1, jds])
                    pst[:, :, jds] = term.reshape(PER, CH, TILE)

                put_p(r, 0, pst).start()

                @pl.loop(0, ntile)
                def _(j):
                    jds = at_tile(j, TILE)
                    a_t[jds, rds] = actc[:, jds].T

                put_p(r, 0, pst).wait()

                @pl.when(r == 0)
                def _():
                    prime()

                @pl.when(r > 0)
                def _():
                    tick(4 * r - 1)

                @pl.loop(0, ntile)
                def _(j):
                    jds = at_tile(j, TILE)
                    d_hid = (dot_nt(cot_v[rds, :], down_v[jds, :]) * slope[:, jds]).astype(LOW)
                    dh_v[rds, jds] = d_hid
                    sv_v[S_UP : S_UP + 1, jds] += jnp.sum(d_hid.astype(F32), axis=0, keepdims=True)

                tick(4 * r)

            for copy in put_n(steps - 1):
                copy.wait()

        pl.run_scoped(
            forward_phase,
            pltpu.VMEM((ff, cols), LOW), pltpu.VMEM((att, cols), LOW),
            pltpu.VMEM((2, BLOCK, cols), LOW), pltpu.VMEM((PER, CH, cols), F32),
            pltpu.VMEM((BLOCK, cols), LOW), pltpu.VMEM((BLOCK, cols), LOW), pltpu.VMEM((BLOCK, ff), LOW),
            pltpu.VMEM((BLOCK, ff), F32), pltpu.VMEM((BLOCK, att), LOW), pltpu.SemaphoreType.DMA((2,)),
        )
        done = 4 * (steps - 1) + 1

        def lanes(ref, e):
            if width % 128 == 0:
                return ref[:, at_tile(e, width)]
            pair = ref[:, at_tile(lax.div(e, 2), 2 * width)]
            odd = lax.rem(e, 2) == 1
            return jnp.where(odd, pair[:, width:].astype(F32), pair[:, :width].astype(F32)).astype(LOW)

        def by_rows(right_ref):
            def compute(e, into, add):
                right = lanes(right_ref, e)

                @pl.loop(0, (ff + att) // TILE)
                def _(j):
                    part = dot_nn(a_t[at_tile(j, TILE), :], right)
                    if add:
                        part = part + into[at_tile(j, TILE), :]
                    into[at_tile(j, TILE), :] = part

            return compute

        def by_columns(left_ref, right_ref):
            def compute(e, into, add):
                left = lanes(left_ref, e).T

                @pl.loop(0, right_ref.shape[1] // TILE)
                def _(j):
                    part = dot_nn(left, right_ref[:, at_tile(j, TILE)])
                    if add:
                        part = part + into[:, at_tile(j, TILE)]
                    into[:, at_tile(j, TILE)] = part

            return compute

        def give(group, i, buf, got):
            return pltpu.make_async_remote_copy(
                src_ref=buf.at[0], dst_ref=got.at[i], send_sem=sa.at[group], recv_sem=ra.at[group * half + i],
                device_id=(mate, t), device_id_type=MESH)

        def mate_slice(group, i, buf, got, compute, again):
            @pl.when(again)
            def _():
                give(group, i, buf, got).wait_send()

            compute(2 * i + 1 - parity, buf.at[0], False)
            give(group, i, buf, got).start()

        def fetch(group, i, buf, got):
            return pltpu.make_async_copy(got.at[i], buf.at[1], ssem.at[group])

        def get_slice(group, i, buf, got):
            give(group, i, buf, got).wait_recv()
            fetch(group, i, buf, got).start()

        def put(group, i, buf, there):
            return pltpu.make_async_copy(buf.at[1], there.at[i], ssem.at[3 + group])

        def own_slice(group, i, buf, got, keep, out, compute):
            fetch(group, i, buf, got).wait()
            compute(2 * i + parity, buf.at[1], True)

            @pl.when(i == here)
            def _():
                put(group, i, buf, out).start()

            @pl.when(i != here)
            def _():
                put(group, i, buf, keep).start()

        def pass_slice(group, i, buf, keep, out):
            put(group, i, buf, keep).wait()

            @pl.when(i != here)
            def _():
                pltpu.make_async_remote_copy(
                    src_ref=keep.at[i], dst_ref=out.at[here], send_sem=sb.at[group * half + i],
                    recv_sem=rb.at[group * half + here], device_id=(2 * i + parity, t), device_id_type=MESH).start()

        def turn_of(i):
            return lax.rem(here + 1 + i, half)

        def first_grads(n2_v, sd, su, gsem):
            load_n2 = pltpu.make_async_copy(n2_h, n2_v, gsem)
            load_n2.start()
            rows_of, columns_of = by_rows(cot_v), by_columns(n2_v, dh_v)

            @pl.loop(0, half + 1)
            def _(i):
                now, before = turn_of(i), turn_of(i + half - 1)

                @pl.when(i > 0)
                def _():
                    get_slice(0, before, sd, ad_h)

                @pl.when(i < half)
                def _():
                    mate_slice(0, now, sd, ad_h, rows_of, i > 0)

                @pl.when(i < PACED)
                def _():
                    tick(done + jnp.maximum(3 * i - 1, 0))

                @pl.when(i > 0)
                def _():
                    own_slice(0, before, sd, ad_h, bd_h, gd_h, rows_of)
                    get_slice(1, before, su, au_h)

                @pl.when(i == 0)
                def _():
                    load_n2.wait()

                @pl.when(i < half)
                def _():
                    mate_slice(1, now, su, au_h, columns_of, i > 0)

                @pl.when(i < PACED)
                def _():
                    tick(done + jnp.maximum(3 * i, 1))

                @pl.when(i > 0)
                def _():
                    pass_slice(0, before, sd, bd_h, gd_h)
                    own_slice(1, before, su, au_h, bu_h, gu_h, columns_of)

                    @pl.when(i <= PACED)
                    def _():
                        tick(done + jnp.minimum(3 * i + 1, 3 * PACED - 1))

                    pass_slice(1, before, su, bu_h, gu_h)

            give(0, 0, sd, ad_h).wait_send()
            give(1, 0, su, au_h).wait_send()

        pl.run_scoped(
            first_grads, pltpu.VMEM((rows, cols), LOW), pltpu.VMEM((2, ff + att, width), F32),
            pltpu.VMEM((2, width, ff), F32), pltpu.SemaphoreType.DMA,
        )
        done2 = done + 3 * PACED

        def back_phase(dk, dv):
            for h in range(heads):
                dk[...] = jnp.zeros_like(dk)
                dv[...] = jnp.zeros_like(dv)

                @pl.loop(0, steps)
                def _(r):
                    rds, kds = at_tile(r, BLOCK), seen(r)
                    query, keys, values = q_v[h, rds, :], k_v[h, kds, :], v_v[h, kds, :]
                    d_ctx = do_v[rds, h * HS : (h + 1) * HS]
                    scores = jnp.where(allowed(r), dot_nt(query, keys) * score_scale, MASKED_SCORE)
                    probs = jnp.exp(scores - lse_v[rds, h * 64 : h * 64 + 1])
                    dv[kds, :] += dot_nn(probs.astype(LOW).T, d_ctx)
                    d_probs = dot_nt(d_ctx, values)
                    inner = jnp.sum(probs * d_probs, axis=-1, keepdims=True)
                    d_scores = (probs * (d_probs - inner)).astype(LOW)
                    d_query = dot_nn(d_scores, keys) * score_scale
                    d_query = turn(d_query, turn_tables(rot_v[rds, :]), -1).astype(LOW)
                    dq_v[rds, pl.ds(3 * h * HS, HS)] = d_query
                    dk[kds, :] += dot_nn(d_scores.T, query) * score_scale
                    there = pl.ds(3 * h * HS, HS)
                    sv_v[S_QKV : S_QKV + 1, there] += jnp.sum(d_query.astype(F32), axis=0, keepdims=True)

                if h == 0:
                    tick(done2)

                @pl.loop(0, steps)
                def _(r):
                    rds = at_tile(r, BLOCK)
                    d_key = turn(dk[rds, :], turn_tables(rot_v[rds, :]), -1).astype(LOW)
                    d_value = dv[rds, :].astype(LOW)
                    for part, got in ((1, d_key), (2, d_value)):
                        there = pl.ds((3 * h + part) * HS, HS)
                        dq_v[rds, there] = got
                        sv_v[S_QKV : S_QKV + 1, there] += jnp.sum(got.astype(F32), axis=0, keepdims=True)

                if h == 0 or h == heads - 1:
                    tick(done2 + (1 if h == 0 else 2))

        pl.run_scoped(back_phase, pltpu.VMEM((rows, HS), F32), pltpu.VMEM((rows, HS), F32))
        done3 = done2 + 3

        def norm_phase(xs, pst, xhat, rstd, m1, m2, xsem):
            load_x(0, xs, xsem).start()

            @pl.loop(0, steps)
            def _(r):
                rds = at_tile(r, BLOCK)
                xcur = xs.at[lax.rem(r, 2)]
                load_x(r, xs, xsem).wait()

                @pl.when(r + 1 < steps)
                def _():
                    load_x(r + 1, xs, xsem).start()

                @pl.loop(0, BLOCK // SUB, unroll=2)
                def _(s):
                    sds = at_tile(s, SUB)
                    xf = xcur[sds, :].astype(F32)
                    centre = xf - jnp.mean(xf, axis=-1, keepdims=True)
                    inv = lax.rsqrt(jnp.mean(centre * centre, axis=-1, keepdims=True) + EPSILON)
                    xhat[sds, :] = centre * inv
                    rstd[sds, :] = jnp.broadcast_to(inv, (SUB, 128))

                m1[...] = jnp.zeros_like(m1)
                m2[...] = jnp.zeros_like(m2)

                @pl.when(r > 1)
                def _():
                    put_p(r - 1, 1, pst).wait()

                @pl.loop(0, dtile)
                def _(j):
                    jds = at_tile(j, TILE)
                    xh = xhat[:, jds]
                    second = dot_nt(dh_v[rds, :], up_v[jds, :])
                    sv_v[S_GAIN2 : S_GAIN2 + 1, jds] += jnp.sum(second * xh, axis=0, keepdims=True)
                    sv_v[S_BIAS2 : S_BIAS2 + 1, jds] += jnp.sum(second, axis=0, keepdims=True)
                    first = dot_nt(dq_v[rds, :], qkv_v[jds, :])
                    sv_v[S_GAIN1 : S_GAIN1 + 1, jds] += jnp.sum(first * xh, axis=0, keepdims=True)
                    sv_v[S_BIAS1 : S_BIAS1 + 1, jds] += jnp.sum(first, axis=0, keepdims=True)
                    cot_tile = cot_v[rds, jds].astype(F32)
                    sv_v[S_OUT : S_OUT + 1, jds] += jnp.sum(cot_tile, axis=0, keepdims=True)
                    scaled = second * vec[V_GAIN2 : V_GAIN2 + 1, jds] + first * vec[V_GAIN1 : V_GAIN1 + 1, jds]
                    pst[:, :, jds] = scaled.reshape(PER, CH, TILE)
                    with_xh = scaled * xh
                    for q in range(TILE // 128):
                        m1[...] += scaled[:, q * 128 : (q + 1) * 128]
                        m2[...] += with_xh[:, q * 128 : (q + 1) * 128]

                tick(done3 + 2 * r)

                @pl.loop(0, PER)
                def _(s):
                    sds = at_tile(s, CH)
                    mean1 = jnp.sum(m1[sds, :], axis=-1, keepdims=True) * (1.0 / cols)
                    mean2 = jnp.sum(m2[sds, :], axis=-1, keepdims=True) * (1.0 / cols)
                    grad = rstd[sds, 0:1] * (pst[s] - mean1 - xhat[sds, :] * mean2)
                    cot_rows = cot_v[pl.ds(pl.multiple_of(r * BLOCK + s * CH, CH), CH), :].astype(F32)
                    pst[s] = grad + add_here * cot_rows

                put_p(r, 1, pst).start()

                @pl.when(r == 0)
                def _():
                    put_p(r, 1, pst).wait()

                tick(done3 + 2 * r + 1)

            put_p(steps - 1, 1, pst).wait()

        pl.run_scoped(
            norm_phase,
            pltpu.VMEM((2, BLOCK, cols), LOW), pltpu.VMEM((PER, CH, cols), F32), pltpu.VMEM((BLOCK, cols), F32),
            pltpu.VMEM((BLOCK, 128), F32), pltpu.VMEM((BLOCK, 128), F32), pltpu.VMEM((BLOCK, 128), F32),
            pltpu.SemaphoreType.DMA((2,)),
        )
        done4 = done3 + 2 * steps

        sv_v[S_STATS : S_STATS + 1, :] += (
            jnp.sum(csq_v[...]) * vec[V_CTX : V_CTX + 1, :]
            + jnp.sum(sq_v[...]) * vec[V_ACT : V_ACT + 1, :]
            + vec[V_COUNT : V_COUNT + 1, :]
        )
        svd[d] = sv_v[...]

        @pl.loop(1, ndp)
        def _(k):
            give_dp(k).start()

        def last_grads(n1_v, sq, gsem):
            load_n1 = pltpu.make_async_copy(n1_h, n1_v, gsem)
            load_n1.start()
            load_n1.wait()
            columns_of = by_columns(n1_v, dq_v)

            @pl.loop(0, half + 1)
            def _(i):
                now, before = turn_of(i), turn_of(i + half - 1)

                @pl.when(i > 0)
                def _():
                    get_slice(2, before, sq, aq_h)

                @pl.when(i < half)
                def _():
                    mate_slice(2, now, sq, aq_h, columns_of, i > 0)

                @pl.when(i < PACED)
                def _():
                    tick(done4 + jnp.maximum(2 * i - 1, 0))

                @pl.when(i > 0)
                def _():
                    own_slice(2, before, sq, aq_h, bq_h, gq_h, columns_of)

                    @pl.when(i <= PACED)
                    def _():
                        tick(done4 + jnp.minimum(2 * i, 2 * PACED - 1))

                    pass_slice(2, before, sq, bq_h, gq_h)

            give(2, 0, sq, aq_h).wait_send()

        pl.run_scoped(
            last_grads, pltpu.VMEM((rows, cols), LOW), pltpu.VMEM((2, width, qw), F32), pltpu.SemaphoreType.DMA)

    def give_dp(k):
        return pltpu.make_async_remote_copy(
            src_ref=sv_v, dst_ref=svd.at[d], send_sem=ssv.at[k], recv_sem=rsv.at[d],
            device_id=(lax.rem(d + k, ndp), t), device_id_type=MESH)

    def get_dp(k):
        other = lax.rem(d + k, ndp)
        return pltpu.make_async_remote_copy(
            src_ref=sv_v, dst_ref=svd.at[other], send_sem=ssv.at[k], recv_sem=rsv.at[other],
            device_id=(other, t), device_id_type=MESH)

    pl.run_scoped(with_inputs, pltpu.VMEM((cols, ff), LOW), pltpu.VMEM((cols, qw), LOW))
    finished = 4 * (steps - 1) + 1 + 3 * PACED + 3 + 2 * steps + 2 * PACED
    before_last = chunks + LAG - 5

    @pl.loop(finished, before_last)
    def _(k):
        tick(k)

    @pl.loop(1, ndp)
    def _(k):
        get_dp(k).wait_recv()
        give_dp(k).wait_send()

    total = svd[0]
    for i in range(1, ndp):
        total = total + svd[i]
    sv_o[0] = total
    svz[t] = total

    def give_z(k):
        return pltpu.make_async_remote_copy(
            src_ref=sv_o.at[0], dst_ref=svz.at[t], send_sem=ssz.at[k], recv_sem=rsz.at[t],
            device_id=(d, lax.rem(t + k, 4)), device_id_type=MESH)

    def get_z(k):
        other = lax.rem(t + k, 4)
        return pltpu.make_async_remote_copy(
            src_ref=sv_o.at[0], dst_ref=svz.at[other], send_sem=ssz.at[k], recv_sem=rsz.at[other],
            device_id=(d, other), device_id_type=MESH)

    for k in range(1, 4):
        give_z(k).start()

    @pl.loop(before_last, chunks + LAG)
    def _(k):
        tick(k)

    for k in range(1, 4):
        get_z(k).wait_recv()
        give_z(k).wait_send()
    sv_o[1] = svz[0] + svz[1] + svz[2] + svz[3]

    @pl.when(mid)
    def _():
        @pl.loop(chunks - HELD, chunks)
        def _(k):
            send_sum(k).wait_send()

    store(chunks - 2).wait()
    store(chunks - 1).wait()

    @pl.loop(0, half)
    def _(i):
        @pl.when(i != here)
        def _():
            for group, keep, out in ((0, bd_h, gd_h), (1, bu_h, gu_h), (2, bq_h, gq_h)):
                sent = pltpu.make_async_remote_copy(
                    src_ref=keep.at[i], dst_ref=out.at[i], send_sem=sb.at[group * half + i],
                    recv_sem=rb.at[group * half + i], device_id=(2 * i + parity, t), device_id_type=MESH)
                sent.wait_send()
                sent.wait_recv()


def layer(ndp, vec, seg, x, cot, rot, up_w, down_w, dense_w, qkv_w):
    rows, cols = x.shape
    ff, att, qw = up_w.shape[1], dense_w.shape[0], qkv_w.shape[1]
    heads = att // HS
    width, half, steps, chunks = cols // ndp, ndp // 2, rows // BLOCK, 2 * rows // CH
    any_spec = pl.BlockSpec(memory_space=pl.ANY)
    vmem_spec = pl.BlockSpec(memory_space=pltpu.VMEM)
    sem = pltpu.SemaphoreType.DMA
    slices = [
        jax.ShapeDtypeStruct((half, ff + att, width), F32),
        jax.ShapeDtypeStruct((half, width, ff), F32),
        jax.ShapeDtypeStruct((half, width, qw), F32),
    ]
    return pl.pallas_call(
        functools.partial(layer_kernel, ndp),
        out_shape=[
            jax.ShapeDtypeStruct((chunks, CH, cols), LOW),
            jax.ShapeDtypeStruct((2, SV, cols), F32),
            *slices,
            jax.ShapeDtypeStruct((chunks, CH, cols), F32),
            jax.ShapeDtypeStruct((rows, cols), LOW),
            jax.ShapeDtypeStruct((rows, cols), LOW),
            *slices,
            *slices,
        ],
        in_specs=[vmem_spec, vmem_spec] + [any_spec] * 7,
        out_specs=[any_spec, vmem_spec] + [any_spec] * 12,
        scratch_shapes=[
            pltpu.VMEM((ff + att, rows), LOW), pltpu.VMEM((rows, cols), LOW), pltpu.VMEM((rows, ff), LOW),
            pltpu.VMEM((rows, qw), LOW), pltpu.VMEM((heads, rows, HS), LOW), pltpu.VMEM((heads, rows, HS), LOW),
            pltpu.VMEM((heads, rows, HS), LOW), pltpu.VMEM((rows, att), LOW), pltpu.VMEM((rows, 64 * heads), F32),
            pltpu.VMEM((rows, 128), F32), pltpu.VMEM((SV, cols), F32),
            pltpu.VMEM((8, TILE), F32), pltpu.VMEM((8, HS), F32),
            pltpu.VMEM((ndp, SV, cols), F32), pltpu.VMEM((4, SV, cols), F32),
            pltpu.VMEM((WINDOW, CH, cols), F32), pltpu.VMEM((WINDOW, CH, cols), F32),
            pltpu.VMEM((2, CH, cols), F32), pltpu.VMEM((2, CH, cols), LOW),
            sem((WINDOW,)), sem((WINDOW,)), sem((WINDOW,)), sem((WINDOW,)), sem((2,)), sem((2,)),
            sem((steps + 1,)), sem((2 * (ff // TILE) + 2,)), sem, sem((2,)),
            sem((ndp,)), sem((ndp,)), sem((4,)), sem((4,)),
            sem((3,)), sem((3 * half,)), sem((3 * half,)), sem((3 * half,)), sem((6,)),
        ],
        compiler_params=pltpu.CompilerParams(
            collective_id=0, has_side_effects=True, vmem_limit_bytes=VMEM_ASK),
        cost_estimate=pl.CostEstimate(flops=10**11, bytes_accessed=2 * 10**8, transcendentals=0),
        name="layer",
    )(vec, seg, x, cot, rot, up_w, down_w, dense_w, qkv_w)


def turn_table(length):
    frequency = np.float32(10000.0) ** (-(np.float32(2.0) * np.arange(ROT // 2, dtype=np.float32)) / np.float32(ROT))
    angles = np.arange(length, dtype=np.float32)[:, None] * frequency.astype(np.float32)[None, :]
    angles = np.concatenate([angles, angles], axis=1).astype(np.float32)
    return np.concatenate([np.cos(angles), np.sin(angles)], axis=1).astype(np.float32)


def on_device(
    ndp,
    inputs,
    cotangent,
    segments,
    subsets,
    ln1_gain,
    ln1_bias,
    qkv_weight,
    qkv_bias,
    dense_weight,
    dense_bias,
    ln2_gain,
    ln2_bias,
    up_weight,
    up_bias,
    down_weight,
    down_bias,
):
    rows_here, model = inputs.shape
    hidden_here = up_weight.shape[1]
    lane = jnp.arange(model)
    slot_of = 3 * subsets[0]

    def row(values):
        return values if values.shape[0] == model else jnp.pad(values, (0, model - values.shape[0]))

    count = jnp.where(lax.axis_index("tensor") == 0, float(LEN), 0.0)
    blank = jnp.zeros((model,), F32)
    vec = jnp.stack(
        [
            row(up_bias), ln1_gain, ln1_bias, ln2_gain, ln2_bias, dense_bias + down_bias, row(qkv_bias),
            (lane == slot_of).astype(F32), (lane == slot_of + 1).astype(F32), jnp.where(lane == slot_of + 2, count, 0.0),
        ]
        + [blank] * (VROWS - 10)
    )
    seg = segments.astype(F32)
    done = layer(
        ndp, vec, seg, inputs, cotangent, jnp.asarray(turn_table(LEN)), up_weight, down_weight, dense_weight, qkv_weight)
    sums, small, grads_d, grads_u, grads_q = done[:5]
    sums = sums.reshape(2, rows_here, model)
    stats_total = small[1, S_STATS, : 3 * SUBSETS].reshape(SUBSETS, 3)
    widths = jnp.array([HEADS * HS, FF], jnp.float32)
    subset_rms = jnp.sqrt(
        stats_total[:, :2] / (jnp.maximum(stats_total[:, 2:3], 1.0) * widths[None, :])
    )
    bias_out = small[0, S_OUT]
    return (
        sums[0],
        sums[1],
        small[1, S_GAIN1],
        small[1, S_BIAS1],
        jnp.sum(grads_q, axis=0),
        small[0, S_QKV, : qkv_bias.shape[0]],
        jnp.sum(grads_d[:, hidden_here:], axis=0),
        bias_out,
        small[1, S_GAIN2],
        small[1, S_BIAS2],
        jnp.sum(grads_u, axis=0),
        small[0, S_UP, :hidden_here],
        jnp.sum(grads_d[:, :hidden_here], axis=0),
        bias_out,
        subset_rms,
    )


def solution(mesh):
    placed = (
        P("dp", None),
        P("dp", None),
        P("dp", None),
        P("dp"),
        P(),
        P(),
        P(None, "tensor"),
        P("tensor"),
        P("tensor", None),
        P(),
        P(),
        P(),
        P(None, "tensor"),
        P("tensor"),
        P("tensor", None),
        P(),
    )
    return jax.shard_map(
        functools.partial(on_device, mesh.shape["dp"]),
        mesh=mesh,
        in_specs=placed,
        out_specs=(
            P("dp", None),
            P("dp", None),
            P(),
            P(),
            P("dp", "tensor"),
            P("tensor"),
            P("tensor", "dp"),
            P(),
            P(),
            P(),
            P("dp", "tensor"),
            P("tensor"),
            P("tensor", "dp"),
            P(),
            P(),
        ),
        check_vma=False,
    )
```

```python
import functools

import jax
import jax.numpy as jnp
import numpy as np
from jax import lax
from jax.experimental import pallas as pl
from jax.experimental.pallas import tpu as pltpu
from jax.sharding import PartitionSpec as P

HEADS = 8
HS = 256
ROT = 64
FF = 8192
SUBSETS = 22
LEN = 1024


EPSILON = 1e-05
MASKED_SCORE = -1000000000.0


VMEM_ASK = 64 * 2**20

MESH = pl.DeviceIdType.MESH
F32 = jnp.float32
LOW = jnp.bfloat16
BLOCK = 256
REACH = 3
CH = 32
PER = BLOCK // CH
WINDOW = 8
HELD = 4
BACK = 2
LAG = 5
PACED = 4
TILE = 512
SUB = 16
RSQRT2 = 0.7071067811865476
RSQRT2PI = 0.3989422804014327
SV = 8
S_GAIN1, S_BIAS1, S_GAIN2, S_BIAS2, S_STATS, S_UP, S_QKV, S_OUT = range(SV)
VROWS = 16
V_UP, V_GAIN1, V_BIAS1, V_GAIN2, V_BIAS2, V_OUT, V_QKV, V_CTX, V_ACT, V_COUNT = range(10)


def dot_nn(left, right):
    return lax.dot_general(left, right, (((1,), (0,)), ((), ())), preferred_element_type=F32)


def dot_nt(left, right):
    return lax.dot_general(left, right, (((1,), (1,)), ((), ())), preferred_element_type=F32)


def at_tile(index, width):
    return pl.ds(pl.multiple_of(index * width, width), width)


def turn_tables(packed):
    lane = lax.broadcasted_iota(jnp.int32, packed.shape, 1)
    half_rot = ROT // 2
    sine = pltpu.roll(packed, 64, 1)
    cosine = jnp.where(lane < ROT, packed, 1.0)
    from_upper = jnp.where(lane < half_rot, -sine, 0.0)
    from_lower = jnp.where((lane >= half_rot) & (lane < ROT), sine, 0.0)
    return cosine, from_upper, from_lower


def turn(head, tables, sign):
    cosine, from_upper, from_lower = tables
    low_part = head[:, :128]
    moved = pltpu.roll(low_part, 128 - ROT // 2, 1) * from_upper + pltpu.roll(low_part, ROT // 2, 1) * from_lower
    low_part = low_part * cosine + moved if sign > 0 else low_part * cosine - moved
    return jnp.concatenate([low_part, head[:, 128:]], axis=1)


def layer_kernel(
    ndp,
    up_b, qkv_b, gain1, bias1, gain2, bias2, dense_b, down_b, seg_in, subset, x_h, cot_h, rot_h, up_h, down_h, dense_h, qkv_h,
    o_h, sv_o, down_g, dense_g, up_g, qkv_g, gd_h, gu_h, gq_h, p_h, n1_h, n2_h, ad_h, au_h, aq_h, bd_h, bu_h, bq_h,
    vec, seg, a_t, cot_v, dh_v, dq_v, q_v, k_v, v_v, do_v, lse_v, rot_v, sv_v, sq_v, csq_v, svd, svz,
    near_in, far_in, own, low,
    s1, r1, s2, r2, lp, lo, lsem, wsem, psem, nsem,
    ssv, rsv, ssz, rsz, sa, ra, sb, rb, ssem,
):
    d = lax.axis_index("dp")
    t = lax.axis_index("tensor")
    rows, cols = x_h.shape
    ff = up_h.shape[1]
    att = dense_h.shape[0]
    heads = att // HS
    qw = qkv_h.shape[1]
    width = cols // ndp
    half = ndp // 2
    steps = rows // BLOCK
    chunks = 2 * rows // CH
    near = t + 1 - 2 * lax.rem(t, 2)
    far = 3 - t
    mid = (t == 1) | (t == 2)
    end = jnp.logical_not(mid)
    parity = lax.rem(d, 2)
    mate = d + 1 - 2 * parity
    here = lax.div(d, 2)
    add_here = jnp.where(t == 1, 1.0, 0.0).astype(F32)

    bar = pltpu.get_barrier_semaphore()
    for k in range(1, 4):
        pl.semaphore_signal(bar, inc=1, device_id=(d, lax.rem(t + k, 4)), device_id_type=MESH)

    @pl.loop(1, ndp)
    def _(k):
        pl.semaphore_signal(bar, inc=1, device_id=(lax.rem(d + k, ndp), t), device_id_type=MESH)

    def slot(k):
        return lax.rem(k, WINDOW)

    def send_part(k):
        return pltpu.make_async_remote_copy(
            src_ref=p_h.at[k], dst_ref=near_in.at[slot(k)], send_sem=s1.at[slot(k)],
            recv_sem=r1.at[slot(k)], device_id=(d, near), device_id_type=MESH)

    def swap(k):
        return pltpu.make_async_remote_copy(
            src_ref=near_in.at[slot(k)], dst_ref=far_in.at[slot(k)], send_sem=s2.at[slot(k)],
            recv_sem=r2.at[slot(k)], device_id=(d, far), device_id_type=MESH)

    def send_sum(k):
        return pltpu.make_async_remote_copy(
            src_ref=far_in.at[slot(k)], dst_ref=near_in.at[slot(k)], send_sem=s1.at[slot(k)],
            recv_sem=r1.at[slot(k)], device_id=(d, near), device_id_type=MESH)

    def load_own(k):
        return pltpu.make_async_copy(p_h.at[k], own.at[lax.rem(k, 2)], lp.at[lax.rem(k, 2)])

    def store(k):
        return pltpu.make_async_copy(low.at[lax.rem(k, 2)], o_h.at[k], lo.at[lax.rem(k, 2)])

    def emit(k, ref):
        @pl.when(k >= 2)
        def _():
            store(k - 2).wait()

        low[lax.rem(k, 2)] = ref[slot(k)].astype(LOW)
        store(k).start()

    def prime():
        @pl.when(end)
        def _():
            @pl.loop(0, WINDOW)
            def _(k):
                send_part(k).start()

        @pl.when(mid)
        def _():
            load_own(0).start()
            load_own(1).start()

    def tick(k):
        @pl.when(end & (k >= LAG) & (k < chunks + LAG))
        def _():
            j = k - LAG
            send_sum(j).wait_recv()
            send_part(j).wait_send()
            emit(j, near_in)

            @pl.when(j + WINDOW < chunks)
            def _():
                send_part(j + WINDOW).start()

        @pl.when(mid & (k < chunks))
        def _():
            send_part(k).wait_recv()
            load_own(k).wait()
            near_in[slot(k)] = near_in[slot(k)] + own[lax.rem(k, 2)]

            @pl.when(k >= HELD)
            def _():
                send_sum(k - HELD).wait_send()

            swap(k).start()

            @pl.when(k + 2 < chunks)
            def _():
                load_own(k + 2).start()

        @pl.when(mid & (k >= BACK) & (k < chunks + BACK))
        def _():
            j = k - BACK
            swap(j).wait()
            far_in[slot(j)] = near_in[slot(j)] + far_in[slot(j)]
            send_sum(j).start()
            emit(j, far_in)

    ntile, dtile = ff // TILE, cols // TILE

    def load_cot(r):
        return pltpu.make_async_copy(cot_h.at[at_tile(r, BLOCK)], cot_v.at[at_tile(r, BLOCK)], lsem.at[r])

    def load_x(r, xs, xsem):
        return pltpu.make_async_copy(x_h.at[at_tile(r, BLOCK)], xs.at[lax.rem(r, 2)], xsem.at[lax.rem(r, 2)])

    def put_p(r, which, pst):
        first = pl.multiple_of(which * (chunks // 2) + r * PER, PER)
        return pltpu.make_async_copy(pst, p_h.at[pl.ds(first, PER)], psem)

    def seen(r):
        return pl.ds(pl.multiple_of(jnp.maximum(r - (REACH - 1), 0) * BLOCK, BLOCK), REACH * BLOCK)

    def allowed(r):
        keys = REACH * BLOCK
        first = jnp.maximum(r - (REACH - 1), 0) * BLOCK
        query_at = lax.broadcasted_iota(jnp.int32, (BLOCK, keys), 0) + r * BLOCK
        key_at = lax.broadcasted_iota(jnp.int32, (BLOCK, keys), 1) + first
        query_seg = jnp.broadcast_to(seg[0:1, at_tile(r, BLOCK)], (8, BLOCK)).T[:, 0:1]
        return (query_seg == seg[0:1, seen(r)]) & (key_at <= query_at)

    vec[...] = jnp.zeros_like(vec)
    for at, ref in (
        (V_UP, up_b), (V_QKV, qkv_b), (V_GAIN1, gain1), (V_BIAS1, bias1), (V_GAIN2, gain2), (V_BIAS2, bias2), (V_OUT, dense_b)
    ):
        vec[at : at + 1, pl.ds(0, ref.shape[1])] = ref[...]
    vec[V_OUT : V_OUT + 1, :] += down_b[...]
    seg[...] = seg_in[...].astype(F32)
    lane = lax.broadcasted_iota(jnp.int32, (1, cols), 1)
    first_stat = 3 * subset[0]
    vec[V_CTX : V_CTX + 1, :] = jnp.where(lane == first_stat, 1.0, 0.0)
    vec[V_ACT : V_ACT + 1, :] = jnp.where(lane == first_stat + 1, 1.0, 0.0)
    count = jnp.where(t == 0, 1.0, 0.0).astype(F32) * rows
    vec[V_COUNT : V_COUNT + 1, :] = jnp.where(lane == first_stat + 2, count, 0.0)
    sv_v[...] = jnp.zeros_like(sv_v)
    sq_v[...] = jnp.zeros_like(sq_v)
    csq_v[...] = jnp.zeros_like(csq_v)
    score_scale = HS ** (-0.5)

    def with_inputs(up_v, qkv_v):
        def load_up(j):
            return pltpu.make_async_copy(up_h.at[:, at_tile(j, TILE)], up_v.at[:, at_tile(j, TILE)], wsem.at[2 * j])

        load_qkv = pltpu.make_async_copy(qkv_h, qkv_v, wsem.at[2 * ntile + 1])
        load_rot = pltpu.make_async_copy(rot_h, rot_v, lsem.at[steps])

        def forward_phase(down_v, dense_v, xs, pst, n1c, n2c, actc, slope, ctxc, xsem):
            def load_down(j):
                return pltpu.make_async_copy(down_h.at[at_tile(j, TILE)], down_v.at[at_tile(j, TILE)], wsem.at[2 * j + 1])

            load_dense = pltpu.make_async_copy(dense_h, dense_v, wsem.at[2 * ntile])
            load_x(0, xs, xsem).start()
            load_qkv.start()
            load_rot.start()
            k_v[...] = jnp.zeros_like(k_v)
            v_v[...] = jnp.zeros_like(v_v)

            def put_n(r):
                return (
                    pltpu.make_async_copy(n1c, n1_h.at[at_tile(r, BLOCK)], nsem.at[0]),
                    pltpu.make_async_copy(n2c, n2_h.at[at_tile(r, BLOCK)], nsem.at[1]),
                )

            @pl.loop(0, steps)
            def _(r):
                rds = at_tile(r, BLOCK)
                xcur = xs.at[lax.rem(r, 2)]
                load_x(r, xs, xsem).wait()

                @pl.when(r + 1 < steps)
                def _():
                    load_x(r + 1, xs, xsem).start()

                @pl.when(r > 0)
                def _():
                    for copy in put_n(r - 1):
                        copy.wait()

                @pl.loop(0, BLOCK // SUB, unroll=2)
                def _(s):
                    sds = at_tile(s, SUB)
                    xf = xcur[sds, :].astype(F32)
                    centre = xf - jnp.mean(xf, axis=-1, keepdims=True)
                    xh = centre * lax.rsqrt(jnp.mean(centre * centre, axis=-1, keepdims=True) + EPSILON)
                    n1c[sds, :] = (xh * vec[V_GAIN1 : V_GAIN1 + 1, :] + vec[V_BIAS1 : V_BIAS1 + 1, :]).astype(LOW)
                    n2c[sds, :] = (xh * vec[V_GAIN2 : V_GAIN2 + 1, :] + vec[V_BIAS2 : V_BIAS2 + 1, :]).astype(LOW)

                for copy in put_n(r):
                    copy.start()

                @pl.when(r == 0)
                def _():
                    load_qkv.wait()
                    load_rot.wait()
                    for j in range(ntile):
                        load_up(j).start()
                    load_cot(0).start()
                    load_dense.start()
                    pl.semaphore_wait(bar, 3 + ndp - 1)

                tables = turn_tables(rot_v[rds, :])
                for h in range(heads):
                    for part in range(3):
                        at = pl.ds((3 * h + part) * HS, HS)
                        head = dot_nn(n1c[...], qkv_v[:, at]) + vec[V_QKV : V_QKV + 1, at]
                        if part < 2:
                            head = turn(head, tables, 1)
                        (q_v, k_v, v_v)[part][h, rds, :] = head.astype(LOW)

                @pl.when(r == 0)
                def _():
                    for j in range(ntile):
                        load_down(j).start()

                ok = allowed(r)
                for h in range(heads):
                    scores = dot_nt(q_v[h, rds, :], k_v[h, seen(r), :]) * score_scale
                    scores = jnp.where(ok, scores, MASKED_SCORE)
                    peak = jnp.max(scores, axis=-1, keepdims=True)
                    weights = jnp.exp(scores - peak)
                    total = jnp.sum(weights, axis=-1, keepdims=True)
                    lse_v[rds, h * 64 : h * 64 + 64] = jnp.broadcast_to(peak + jnp.log(total), (BLOCK, 64))
                    context = dot_nn((weights / total).astype(LOW), v_v[h, seen(r), :])
                    csq_v[...] += jnp.sum((context * context).reshape(BLOCK // 8, 8, HS), axis=0)
                    context = context.astype(LOW)
                    ctxc[:, h * HS : (h + 1) * HS] = context
                    a_t[pl.ds(ff + h * HS, HS), rds] = context.T

                @pl.when(r > 0)
                def _():
                    tick(4 * r - 3)

                @pl.loop(0, ntile)
                def _(j):
                    jds = at_tile(j, TILE)

                    @pl.when(r == 0)
                    def _():
                        load_up(j).wait()

                    hidden = dot_nn(n2c[...], up_v[:, jds]) + vec[V_UP : V_UP + 1, jds]
                    cum = 0.5 * (1.0 + lax.erf(hidden * RSQRT2))
                    active = hidden * cum
                    slope[:, jds] = cum + hidden * jnp.exp(-0.5 * hidden * hidden) * RSQRT2PI
                    act_low = active.astype(LOW)
                    actc[:, jds] = act_low
                    sq_v[...] += jnp.sum((active * active).reshape(BLOCK // 8, 8, TILE), axis=0)

                @pl.when(r > 0)
                def _():
                    tick(4 * r - 2)

                @pl.when(r == 0)
                def _():
                    load_dense.wait()
                    for k in range(1, steps):
                        load_cot(k).start()

                    @pl.loop(0, ntile)
                    def _(j):
                        load_down(j).wait()

                @pl.loop(0, dtile)
                def _(j):
                    jds = at_tile(j, TILE)
                    term = dot_nn(actc[...], down_v[:, jds]) + dot_nn(ctxc[...], dense_v[:, jds])
                    term = term + add_here * (xcur[:, jds].astype(F32) + vec[V_OUT : V_OUT + 1, jds])
                    pst[:, :, jds] = term.reshape(PER, CH, TILE)

                put_p(r, 0, pst).start()

                @pl.loop(0, ntile)
                def _(j):
                    jds = at_tile(j, TILE)
                    a_t[jds, rds] = actc[:, jds].T

                put_p(r, 0, pst).wait()

                @pl.when(r == 0)
                def _():
                    prime()

                @pl.when(r > 0)
                def _():
                    tick(4 * r - 1)

                load_cot(r).wait()
                do_v[rds, :] = dot_nt(cot_v[rds, :], dense_v[...]).astype(LOW)

                @pl.loop(0, ntile)
                def _(j):
                    jds = at_tile(j, TILE)
                    d_hid = (dot_nt(cot_v[rds, :], down_v[jds, :]) * slope[:, jds]).astype(LOW)
                    dh_v[rds, jds] = d_hid
                    sv_v[S_UP : S_UP + 1, jds] += jnp.sum(d_hid.astype(F32), axis=0, keepdims=True)

                tick(4 * r)

            for copy in put_n(steps - 1):
                copy.wait()

        pl.run_scoped(
            forward_phase,
            pltpu.VMEM((ff, cols), LOW), pltpu.VMEM((att, cols), LOW),
            pltpu.VMEM((2, BLOCK, cols), LOW), pltpu.VMEM((PER, CH, cols), F32),
            pltpu.VMEM((BLOCK, cols), LOW), pltpu.VMEM((BLOCK, cols), LOW), pltpu.VMEM((BLOCK, ff), LOW),
            pltpu.VMEM((BLOCK, ff), F32), pltpu.VMEM((BLOCK, att), LOW), pltpu.SemaphoreType.DMA((2,)),
        )
        done = 4 * (steps - 1) + 1

        def lanes(ref, e):
            if width % 128 == 0:
                return ref[:, at_tile(e, width)]
            pair = ref[:, at_tile(lax.div(e, 2), 2 * width)]
            odd = lax.rem(e, 2) == 1
            return jnp.where(odd, pair[:, width:].astype(F32), pair[:, :width].astype(F32)).astype(LOW)

        def by_rows(right_ref):
            def compute(e, into, add):
                right = lanes(right_ref, e)

                @pl.loop(0, (ff + att) // TILE)
                def _(j):
                    part = dot_nn(a_t[at_tile(j, TILE), :], right)
                    if add:
                        part = part + into[at_tile(j, TILE), :]
                    into[at_tile(j, TILE), :] = part

            return compute

        def by_columns(left_ref, right_ref):
            def compute(e, into, add):
                left = lanes(left_ref, e).T

                @pl.loop(0, right_ref.shape[1] // TILE)
                def _(j):
                    part = dot_nn(left, right_ref[:, at_tile(j, TILE)])
                    if add:
                        part = part + into[:, at_tile(j, TILE)]
                    into[:, at_tile(j, TILE)] = part

            return compute

        def give(group, i, buf, got):
            return pltpu.make_async_remote_copy(
                src_ref=buf.at[0], dst_ref=got.at[i], send_sem=sa.at[group], recv_sem=ra.at[group * half + i],
                device_id=(mate, t), device_id_type=MESH)

        def mate_slice(group, i, buf, got, compute, again):
            @pl.when(again)
            def _():
                give(group, i, buf, got).wait_send()

            compute(2 * i + 1 - parity, buf.at[0], False)
            give(group, i, buf, got).start()

        def fetch(group, i, buf, got):
            return pltpu.make_async_copy(got.at[i], buf.at[1], ssem.at[group])

        def get_slice(group, i, buf, got):
            give(group, i, buf, got).wait_recv()
            fetch(group, i, buf, got).start()

        def put(group, i, buf, there):
            return pltpu.make_async_copy(buf.at[1], there.at[i], ssem.at[3 + group])

        def own_slice(group, i, buf, got, keep, out, compute):
            fetch(group, i, buf, got).wait()
            compute(2 * i + parity, buf.at[1], True)

            @pl.when(i == here)
            def _():
                put(group, i, buf, out).start()

            @pl.when(i != here)
            def _():
                put(group, i, buf, keep).start()

        def pass_slice(group, i, buf, keep, out):
            put(group, i, buf, keep).wait()

            @pl.when(i != here)
            def _():
                pltpu.make_async_remote_copy(
                    src_ref=keep.at[i], dst_ref=out.at[here], send_sem=sb.at[group * half + i],
                    recv_sem=rb.at[group * half + here], device_id=(2 * i + parity, t), device_id_type=MESH).start()

        def turn_of(i):
            return lax.bitwise_xor(here, half - 1 - lax.rem(i, half))

        def first_grads(n2_v, sd, su, gsem):
            load_n2 = pltpu.make_async_copy(n2_h, n2_v, gsem)
            load_n2.start()
            rows_of, columns_of = by_rows(cot_v), by_columns(n2_v, dh_v)

            @pl.loop(0, half + 1)
            def _(i):
                now, before = turn_of(i), turn_of(i + half - 1)

                @pl.when(i > 0)
                def _():
                    get_slice(0, before, sd, ad_h)

                @pl.when(i < half)
                def _():
                    mate_slice(0, now, sd, ad_h, rows_of, i > 0)

                @pl.when(i < PACED)
                def _():
                    tick(done + jnp.maximum(3 * i - 1, 0))

                @pl.when(i > 0)
                def _():
                    own_slice(0, before, sd, ad_h, bd_h, gd_h, rows_of)
                    get_slice(1, before, su, au_h)

                @pl.when(i == 0)
                def _():
                    load_n2.wait()

                @pl.when(i < half)
                def _():
                    mate_slice(1, now, su, au_h, columns_of, i > 0)

                @pl.when(i < PACED)
                def _():
                    tick(done + jnp.maximum(3 * i, 1))

                @pl.when(i > 0)
                def _():
                    pass_slice(0, before, sd, bd_h, gd_h)
                    own_slice(1, before, su, au_h, bu_h, gu_h, columns_of)

                    @pl.when(i <= PACED)
                    def _():
                        tick(done + jnp.minimum(3 * i + 1, 3 * PACED - 1))

                    pass_slice(1, before, su, bu_h, gu_h)

            give(0, 0, sd, ad_h).wait_send()
            give(1, 0, su, au_h).wait_send()

        pl.run_scoped(
            first_grads, pltpu.VMEM((rows, cols), LOW), pltpu.VMEM((2, ff + att, width), F32),
            pltpu.VMEM((2, width, ff), F32), pltpu.SemaphoreType.DMA,
        )
        done2 = done + 3 * PACED

        def back_phase(dk, dv):
            for h in range(heads):
                dk[...] = jnp.zeros_like(dk)
                dv[...] = jnp.zeros_like(dv)

                @pl.loop(0, steps)
                def _(r):
                    rds, kds = at_tile(r, BLOCK), seen(r)
                    query, keys, values = q_v[h, rds, :], k_v[h, kds, :], v_v[h, kds, :]
                    d_ctx = do_v[rds, h * HS : (h + 1) * HS]
                    scores = jnp.where(allowed(r), dot_nt(query, keys) * score_scale, MASKED_SCORE)
                    probs = jnp.exp(scores - lse_v[rds, h * 64 : h * 64 + 1])
                    dv[kds, :] += dot_nn(probs.astype(LOW).T, d_ctx)
                    d_probs = dot_nt(d_ctx, values)
                    inner = jnp.sum(probs * d_probs, axis=-1, keepdims=True)
                    d_scores = (probs * (d_probs - inner)).astype(LOW)
                    d_query = dot_nn(d_scores, keys) * score_scale
                    d_query = turn(d_query, turn_tables(rot_v[rds, :]), -1).astype(LOW)
                    dq_v[rds, pl.ds(3 * h * HS, HS)] = d_query
                    dk[kds, :] += dot_nn(d_scores.T, query) * score_scale
                    there = pl.ds(3 * h * HS, HS)
                    sv_v[S_QKV : S_QKV + 1, there] += jnp.sum(d_query.astype(F32), axis=0, keepdims=True)

                if h == 0:
                    tick(done2)

                @pl.loop(0, steps)
                def _(r):
                    rds = at_tile(r, BLOCK)
                    d_key = turn(dk[rds, :], turn_tables(rot_v[rds, :]), -1).astype(LOW)
                    d_value = dv[rds, :].astype(LOW)
                    for part, got in ((1, d_key), (2, d_value)):
                        there = pl.ds((3 * h + part) * HS, HS)
                        dq_v[rds, there] = got
                        sv_v[S_QKV : S_QKV + 1, there] += jnp.sum(got.astype(F32), axis=0, keepdims=True)

                if h == 0 or h == heads - 1:
                    tick(done2 + (1 if h == 0 else 2))

        pl.run_scoped(back_phase, pltpu.VMEM((rows, HS), F32), pltpu.VMEM((rows, HS), F32))
        done3 = done2 + 3

        def norm_phase(n1_v, nsem1, xs, pst, xhat, rstd, m1, m2, xsem):
            load_x(0, xs, xsem).start()
            pltpu.make_async_copy(n1_h, n1_v, nsem1).start()

            @pl.loop(0, steps)
            def _(r):
                rds = at_tile(r, BLOCK)
                xcur = xs.at[lax.rem(r, 2)]
                load_x(r, xs, xsem).wait()

                @pl.when(r + 1 < steps)
                def _():
                    load_x(r + 1, xs, xsem).start()

                @pl.loop(0, BLOCK // SUB, unroll=2)
                def _(s):
                    sds = at_tile(s, SUB)
                    xf = xcur[sds, :].astype(F32)
                    centre = xf - jnp.mean(xf, axis=-1, keepdims=True)
                    inv = lax.rsqrt(jnp.mean(centre * centre, axis=-1, keepdims=True) + EPSILON)
                    xhat[sds, :] = centre * inv
                    rstd[sds, :] = jnp.broadcast_to(inv, (SUB, 128))

                m1[...] = jnp.zeros_like(m1)
                m2[...] = jnp.zeros_like(m2)

                @pl.when(r > 1)
                def _():
                    put_p(r - 1, 1, pst).wait()

                @pl.loop(0, dtile)
                def _(j):
                    jds = at_tile(j, TILE)
                    xh = xhat[:, jds]
                    second = dot_nt(dh_v[rds, :], up_v[jds, :])
                    sv_v[S_GAIN2 : S_GAIN2 + 1, jds] += jnp.sum(second * xh, axis=0, keepdims=True)
                    sv_v[S_BIAS2 : S_BIAS2 + 1, jds] += jnp.sum(second, axis=0, keepdims=True)
                    first = dot_nt(dq_v[rds, :], qkv_v[jds, :])
                    sv_v[S_GAIN1 : S_GAIN1 + 1, jds] += jnp.sum(first * xh, axis=0, keepdims=True)
                    sv_v[S_BIAS1 : S_BIAS1 + 1, jds] += jnp.sum(first, axis=0, keepdims=True)
                    cot_tile = cot_v[rds, jds].astype(F32)
                    sv_v[S_OUT : S_OUT + 1, jds] += jnp.sum(cot_tile, axis=0, keepdims=True)
                    scaled = second * vec[V_GAIN2 : V_GAIN2 + 1, jds] + first * vec[V_GAIN1 : V_GAIN1 + 1, jds]
                    pst[:, :, jds] = scaled.reshape(PER, CH, TILE)
                    with_xh = scaled * xh
                    for q in range(TILE // 128):
                        m1[...] += scaled[:, q * 128 : (q + 1) * 128]
                        m2[...] += with_xh[:, q * 128 : (q + 1) * 128]

                tick(done3 + 2 * r)

                @pl.loop(0, PER)
                def _(s):
                    sds = at_tile(s, CH)
                    mean1 = jnp.sum(m1[sds, :], axis=-1, keepdims=True) * (1.0 / cols)
                    mean2 = jnp.sum(m2[sds, :], axis=-1, keepdims=True) * (1.0 / cols)
                    grad = rstd[sds, 0:1] * (pst[s] - mean1 - xhat[sds, :] * mean2)
                    cot_rows = cot_v[pl.ds(pl.multiple_of(r * BLOCK + s * CH, CH), CH), :].astype(F32)
                    pst[s] = grad + add_here * cot_rows

                put_p(r, 1, pst).start()

                @pl.when(r == 0)
                def _():
                    put_p(r, 1, pst).wait()

                tick(done3 + 2 * r + 1)

            put_p(steps - 1, 1, pst).wait()

        done4 = done3 + 2 * steps

        def last_grads(n1_v, nsem1, sq):
            pltpu.make_async_copy(n1_h, n1_v, nsem1).wait()
            columns_of = by_columns(n1_v, dq_v)

            @pl.loop(0, half + 1)
            def _(i):
                now, before = turn_of(i), turn_of(i + half - 1)

                @pl.when(i > 0)
                def _():
                    get_slice(2, before, sq, aq_h)

                @pl.when(i < half)
                def _():
                    mate_slice(2, now, sq, aq_h, columns_of, i > 0)

                @pl.when(i < PACED)
                def _():
                    tick(done4 + jnp.maximum(2 * i - 1, 0))

                @pl.when(i > 0)
                def _():
                    own_slice(2, before, sq, aq_h, bq_h, gq_h, columns_of)

                    @pl.when(i <= PACED)
                    def _():
                        tick(done4 + jnp.minimum(2 * i, 2 * PACED - 1))

                    pass_slice(2, before, sq, bq_h, gq_h)

            give(2, 0, sq, aq_h).wait_send()

        def small_sums():
            sv_v[S_STATS : S_STATS + 1, :] += (
                jnp.sum(csq_v[...]) * vec[V_CTX : V_CTX + 1, :]
                + jnp.sum(sq_v[...]) * vec[V_ACT : V_ACT + 1, :]
                + vec[V_COUNT : V_COUNT + 1, :]
            )
            svd[d] = sv_v[...]

            @pl.loop(1, ndp)
            def _(k):
                give_dp(k).start()

        def with_n1(n1_v, nsem1):
            pl.run_scoped(
                functools.partial(norm_phase, n1_v, nsem1),
                pltpu.VMEM((2, BLOCK, cols), LOW), pltpu.VMEM((PER, CH, cols), F32), pltpu.VMEM((BLOCK, cols), F32),
                pltpu.VMEM((BLOCK, 128), F32), pltpu.VMEM((BLOCK, 128), F32), pltpu.VMEM((BLOCK, 128), F32),
                pltpu.SemaphoreType.DMA((2,)),
            )
            small_sums()
            pl.run_scoped(functools.partial(last_grads, n1_v, nsem1), pltpu.VMEM((2, width, qw), F32))

        pl.run_scoped(with_n1, pltpu.VMEM((rows, cols), LOW), pltpu.SemaphoreType.DMA)

    def give_dp(k):
        return pltpu.make_async_remote_copy(
            src_ref=sv_v, dst_ref=svd.at[d], send_sem=ssv.at[k], recv_sem=rsv.at[d],
            device_id=(lax.rem(d + k, ndp), t), device_id_type=MESH)

    def get_dp(k):
        other = lax.rem(d + k, ndp)
        return pltpu.make_async_remote_copy(
            src_ref=sv_v, dst_ref=svd.at[other], send_sem=ssv.at[k], recv_sem=rsv.at[other],
            device_id=(other, t), device_id_type=MESH)

    pl.run_scoped(with_inputs, pltpu.VMEM((cols, ff), LOW), pltpu.VMEM((cols, qw), LOW))
    finished = 4 * (steps - 1) + 1 + 3 * PACED + 3 + 2 * steps + 2 * PACED
    tiles_down, tiles_up, tiles_qkv = (ff + att) // TILE, ff // TILE, qw // TILE
    before_last = chunks - tiles_down - tiles_up - 5

    @pl.loop(finished, before_last)
    def _(k):
        tick(k)

    def give_z(k):
        return pltpu.make_async_remote_copy(
            src_ref=sv_o.at[0], dst_ref=svz.at[t], send_sem=ssz.at[k], recv_sem=rsz.at[t],
            device_id=(d, lax.rem(t + k, 4)), device_id_type=MESH)

    def get_z(k):
        other = lax.rem(t + k, 4)
        return pltpu.make_async_remote_copy(
            src_ref=sv_o.at[0], dst_ref=svz.at[other], send_sem=ssz.at[k], recv_sem=rsz.at[other],
            device_id=(d, other), device_id_type=MESH)

    def small_totals():
        @pl.loop(1, ndp)
        def _(k):
            get_dp(k).wait_recv()
            give_dp(k).wait_send()

        total = svd[0]
        for i in range(1, ndp):
            total = total + svd[i]
        sv_o[0] = total
        svz[t] = total
        for k in range(1, 4):
            give_z(k).start()

    def landed(group, keep, out):
        @pl.loop(0, half)
        def _(i):
            @pl.when(i != here)
            def _():
                sent = pltpu.make_async_remote_copy(
                    src_ref=keep.at[i], dst_ref=out.at[i], send_sem=sb.at[group * half + i],
                    recv_sem=rb.at[group * half + i], device_id=(2 * i + parity, t), device_id_type=MESH)
                sent.wait_send()
                sent.wait_recv()

    def sum_phase(tall, tall_sum, wide, wide_sum, fsem, usem):
        def tiles_d():
            for j in range((ff + att) // TILE):
                there = down_g.at[pl.ds(j * TILE, TILE)] if j < ff // TILE else dense_g.at[pl.ds(j * TILE - ff, TILE)]
                yield gd_h.at[:, pl.ds(j * TILE, TILE)], there

        def tiles_w(got, result):
            for j in range(got.shape[2] // TILE):
                yield got.at[:, :, pl.ds(j * TILE, TILE)], result.at[:, pl.ds(j * TILE, TILE)]

        def add_up(pairs, parts, total):
            pairs = list(pairs)

            def get(j):
                return pltpu.make_async_copy(pairs[j][0], parts.at[j % 2], fsem.at[j % 2])

            def put_sum(j):
                return pltpu.make_async_copy(total.at[j % 2], pairs[j][1], usem.at[j % 2])

            get(0).start()
            for j in range(len(pairs)):
                if j + 1 < len(pairs):
                    get(j + 1).start()
                get(j).wait()
                if j >= 2:
                    put_sum(j - 2).wait()
                acc = parts[j % 2, 0]
                for i in range(1, half):
                    acc = acc + parts[j % 2, i]
                total[j % 2] = acc
                put_sum(j).start()
                yield
            for j in range(max(len(pairs) - 2, 0), len(pairs)):
                put_sum(j).wait()

        at = before_last
        for group, keep, out, work in (
            (0, bd_h, gd_h, lambda: add_up(tiles_d(), tall, tall_sum)),
            (1, bu_h, gu_h, lambda: add_up(tiles_w(gu_h, up_g), wide, wide_sum)),
            (2, bq_h, gq_h, lambda: add_up(tiles_w(gq_h, qkv_g), wide, wide_sum)),
        ):
            if group == 2:
                small_totals()

                @pl.loop(at, chunks + BACK)
                def _(k):
                    tick(k)

                at = chunks + BACK
            landed(group, keep, out)
            for _ in work():
                tick(at)
                at += 1

    pl.run_scoped(
        sum_phase,
        pltpu.VMEM((2, half, TILE, width), F32), pltpu.VMEM((2, TILE, width), F32),
        pltpu.VMEM((2, half, width, TILE), F32), pltpu.VMEM((2, width, TILE), F32),
        pltpu.SemaphoreType.DMA((2,)), pltpu.SemaphoreType.DMA((2,)),
    )

    @pl.loop(chunks + BACK + tiles_qkv, chunks + LAG)
    def _(k):
        tick(k)

    for k in range(1, 4):
        get_z(k).wait_recv()
        give_z(k).wait_send()
    sv_o[1] = svz[0] + svz[1] + svz[2] + svz[3]

    @pl.when(mid)
    def _():
        @pl.loop(chunks - HELD, chunks)
        def _(k):
            send_sum(k).wait_send()

    store(chunks - 2).wait()
    store(chunks - 1).wait()


def layer(ndp, vectors, segments, subsets, x, cot, rot, up_w, down_w, dense_w, qkv_w):
    rows, cols = x.shape
    ff, att, qw = up_w.shape[1], dense_w.shape[0], qkv_w.shape[1]
    heads = att // HS
    width, half, steps, chunks = cols // ndp, ndp // 2, rows // BLOCK, 2 * rows // CH
    any_spec = pl.BlockSpec(memory_space=pl.ANY)
    vmem_spec = pl.BlockSpec(memory_space=pltpu.VMEM)
    sem = pltpu.SemaphoreType.DMA
    slices = [
        jax.ShapeDtypeStruct((half, ff + att, width), F32),
        jax.ShapeDtypeStruct((half, width, ff), F32),
        jax.ShapeDtypeStruct((half, width, qw), F32),
    ]
    return pl.pallas_call(
        functools.partial(layer_kernel, ndp),
        out_shape=[
            jax.ShapeDtypeStruct((chunks, CH, cols), LOW),
            jax.ShapeDtypeStruct((2, SV, cols), F32),
            jax.ShapeDtypeStruct((ff, width), F32),
            jax.ShapeDtypeStruct((att, width), F32),
            jax.ShapeDtypeStruct((width, ff), F32),
            jax.ShapeDtypeStruct((width, qw), F32),
            *slices,
            jax.ShapeDtypeStruct((chunks, CH, cols), F32),
            jax.ShapeDtypeStruct((rows, cols), LOW),
            jax.ShapeDtypeStruct((rows, cols), LOW),
            *slices,
            *slices,
        ],
        in_specs=[vmem_spec] * 9 + [pl.BlockSpec(memory_space=pltpu.SMEM)] + [any_spec] * 7,
        out_specs=[any_spec, vmem_spec] + [any_spec] * 16,
        scratch_shapes=[
            pltpu.VMEM((VROWS, cols), F32), pltpu.VMEM((1, rows), F32),
            pltpu.VMEM((ff + att, rows), LOW), pltpu.VMEM((rows, cols), LOW), pltpu.VMEM((rows, ff), LOW),
            pltpu.VMEM((rows, qw), LOW), pltpu.VMEM((heads, rows, HS), LOW), pltpu.VMEM((heads, rows, HS), LOW),
            pltpu.VMEM((heads, rows, HS), LOW), pltpu.VMEM((rows, att), LOW), pltpu.VMEM((rows, 64 * heads), F32),
            pltpu.VMEM((rows, 128), F32), pltpu.VMEM((SV, cols), F32),
            pltpu.VMEM((8, TILE), F32), pltpu.VMEM((8, HS), F32),
            pltpu.VMEM((ndp, SV, cols), F32), pltpu.VMEM((4, SV, cols), F32),
            pltpu.VMEM((WINDOW, CH, cols), F32), pltpu.VMEM((WINDOW, CH, cols), F32),
            pltpu.VMEM((2, CH, cols), F32), pltpu.VMEM((2, CH, cols), LOW),
            sem((WINDOW,)), sem((WINDOW,)), sem((WINDOW,)), sem((WINDOW,)), sem((2,)), sem((2,)),
            sem((steps + 1,)), sem((2 * (ff // TILE) + 2,)), sem, sem((2,)),
            sem((ndp,)), sem((ndp,)), sem((4,)), sem((4,)),
            sem((3,)), sem((3 * half,)), sem((3 * half,)), sem((3 * half,)), sem((6,)),
        ],
        compiler_params=pltpu.CompilerParams(
            collective_id=0, has_side_effects=True, vmem_limit_bytes=VMEM_ASK),
        cost_estimate=pl.CostEstimate(flops=10**11, bytes_accessed=2 * 10**8, transcendentals=0),
        name="layer",
    )(*vectors, segments, subsets, x, cot, rot, up_w, down_w, dense_w, qkv_w)


def turn_table(length):
    frequency = np.float32(10000.0) ** (-(np.float32(2.0) * np.arange(ROT // 2, dtype=np.float32)) / np.float32(ROT))
    angles = np.arange(length, dtype=np.float32)[:, None] * frequency.astype(np.float32)[None, :]
    angles = np.concatenate([angles, angles], axis=1).astype(np.float32)
    return np.concatenate([np.cos(angles), np.sin(angles)], axis=1).astype(np.float32)


def on_device(
    ndp,
    inputs,
    cotangent,
    segments,
    subsets,
    ln1_gain,
    ln1_bias,
    qkv_weight,
    qkv_bias,
    dense_weight,
    dense_bias,
    ln2_gain,
    ln2_bias,
    up_weight,
    up_bias,
    down_weight,
    down_bias,
):
    rows_here, model = inputs.shape
    hidden_here = up_weight.shape[1]
    vectors = [
        values.reshape(1, -1)
        for values in (up_bias, qkv_bias, ln1_gain, ln1_bias, ln2_gain, ln2_bias, dense_bias, down_bias)
    ]
    sums, small, down_grad, dense_grad, up_grad, qkv_grad = layer(
        ndp, vectors, segments, subsets, inputs, cotangent, jnp.asarray(turn_table(LEN)),
        up_weight, down_weight, dense_weight, qkv_weight)[:6]
    sums = sums.reshape(2, rows_here, model)
    stats_total = small[1, S_STATS, : 3 * SUBSETS].reshape(SUBSETS, 3)
    widths = jnp.array([HEADS * HS, FF], jnp.float32)
    subset_rms = jnp.sqrt(
        stats_total[:, :2] / (jnp.maximum(stats_total[:, 2:3], 1.0) * widths[None, :])
    )
    bias_out = small[0, S_OUT]
    return (
        sums[0],
        sums[1],
        small[1, S_GAIN1],
        small[1, S_BIAS1],
        qkv_grad,
        small[0, S_QKV, : qkv_bias.shape[0]],
        dense_grad,
        bias_out,
        small[1, S_GAIN2],
        small[1, S_BIAS2],
        up_grad,
        small[0, S_UP, :hidden_here],
        down_grad,
        bias_out,
        subset_rms,
    )


def solution(mesh):
    placed = (
        P("dp", None),
        P("dp", None),
        P("dp", None),
        P("dp"),
        P(),
        P(),
        P(None, "tensor"),
        P("tensor"),
        P("tensor", None),
        P(),
        P(),
        P(),
        P(None, "tensor"),
        P("tensor"),
        P("tensor", None),
        P(),
    )
    return jax.shard_map(
        functools.partial(on_device, mesh.shape["dp"]),
        mesh=mesh,
        in_specs=placed,
        out_specs=(
            P("dp", None),
            P("dp", None),
            P(),
            P(),
            P("dp", "tensor"),
            P("tensor"),
            P("tensor", "dp"),
            P(),
            P(),
            P(),
            P("dp", "tensor"),
            P("tensor"),
            P("tensor", "dp"),
            P(),
            P(),
        ),
        check_vma=False,
    )
```

```python
import functools

import jax
import jax.numpy as jnp
import numpy as np
from jax import lax
from jax.experimental import pallas as pl
from jax.experimental.pallas import tpu as pltpu
from jax.sharding import PartitionSpec as P

HEADS = 8
HS = 256
ROT = 64
FF = 8192
SUBSETS = 22
LEN = 1024


EPSILON = 1e-05
MASKED_SCORE = -1000000000.0


VMEM_ASK = 64 * 2**20

MESH = pl.DeviceIdType.MESH
F32 = jnp.float32
LOW = jnp.bfloat16
BLOCK = 256
REACH = 3
CH = 32
PER = BLOCK // CH
WINDOW = 8
HELD = 4
BACK = 2
LAG = 5
PACED = 4
TILE = 512
SUB = 16
RSQRT2 = 0.7071067811865476
RSQRT2PI = 0.3989422804014327
SV = 8
S_GAIN1, S_BIAS1, S_GAIN2, S_BIAS2, S_STATS, S_UP, S_QKV, S_OUT = range(SV)
VROWS = 16
V_UP, V_GAIN1, V_BIAS1, V_GAIN2, V_BIAS2, V_OUT, V_QKV, V_CTX, V_ACT, V_COUNT = range(10)


def dot_nn(left, right):
    return lax.dot_general(left, right, (((1,), (0,)), ((), ())), preferred_element_type=F32)


def dot_nt(left, right):
    return lax.dot_general(left, right, (((1,), (1,)), ((), ())), preferred_element_type=F32)


def at_tile(index, width):
    return pl.ds(pl.multiple_of(index * width, width), width)


def turn_tables(packed):
    lane = lax.broadcasted_iota(jnp.int32, packed.shape, 1)
    half_rot = ROT // 2
    sine = pltpu.roll(packed, 64, 1)
    cosine = jnp.where(lane < ROT, packed, 1.0)
    from_upper = jnp.where(lane < half_rot, -sine, 0.0)
    from_lower = jnp.where((lane >= half_rot) & (lane < ROT), sine, 0.0)
    return cosine, from_upper, from_lower


def turn(head, tables, sign):
    cosine, from_upper, from_lower = tables
    low_part = head[:, :128]
    moved = pltpu.roll(low_part, 128 - ROT // 2, 1) * from_upper + pltpu.roll(low_part, ROT // 2, 1) * from_lower
    low_part = low_part * cosine + moved if sign > 0 else low_part * cosine - moved
    return jnp.concatenate([low_part, head[:, 128:]], axis=1)


def layer_kernel(
    ndp,
    up_b, qkv_b, gain1, bias1, gain2, bias2, dense_b, down_b, seg_in, subset, x_h, cot_h, rot_h, up_h, down_h, dense_h, qkv_h,
    o_h, sv_o, down_g, dense_g, up_g, qkv_g, gd_h, gu_h, gq_h, p_h, n1_h, n2_h, ad_h, au_h, aq_h, bd_h, bu_h, bq_h,
    vec, seg, a_t, cot_v, dh_v, dq_v, q_v, k_v, v_v, do_v, lse_v, rot_v, sv_v, sq_v, csq_v, svd, svz,
    near_in, far_in, own, low,
    s1, r1, s2, r2, lp, lo, lsem, wsem, psem, nsem,
    ssv, rsv, ssz, rsz, sa, ra, sb, rb, ssem,
):
    d = lax.axis_index("dp")
    t = lax.axis_index("tensor")
    rows, cols = x_h.shape
    ff = up_h.shape[1]
    att = dense_h.shape[0]
    heads = att // HS
    qw = qkv_h.shape[1]
    width = cols // ndp
    half = ndp // 2
    steps = rows // BLOCK
    chunks = 2 * rows // CH
    near = t + 1 - 2 * lax.rem(t, 2)
    far = 3 - t
    mid = (t == 1) | (t == 2)
    end = jnp.logical_not(mid)
    parity = lax.rem(d, 2)
    mate = d + 1 - 2 * parity
    here = lax.div(d, 2)
    add_here = jnp.where(t == 1, 1.0, 0.0).astype(F32)

    bar = pltpu.get_barrier_semaphore()
    for k in range(1, 4):
        pl.semaphore_signal(bar, inc=1, device_id=(d, lax.rem(t + k, 4)), device_id_type=MESH)

    @pl.loop(1, ndp)
    def _(k):
        pl.semaphore_signal(bar, inc=1, device_id=(lax.rem(d + k, ndp), t), device_id_type=MESH)

    def slot(k):
        return lax.rem(k, WINDOW)

    def send_part(k):
        return pltpu.make_async_remote_copy(
            src_ref=p_h.at[k], dst_ref=near_in.at[slot(k)], send_sem=s1.at[slot(k)],
            recv_sem=r1.at[slot(k)], device_id=(d, near), device_id_type=MESH)

    def swap(k):
        return pltpu.make_async_remote_copy(
            src_ref=near_in.at[slot(k)], dst_ref=far_in.at[slot(k)], send_sem=s2.at[slot(k)],
            recv_sem=r2.at[slot(k)], device_id=(d, far), device_id_type=MESH)

    def send_sum(k):
        return pltpu.make_async_remote_copy(
            src_ref=far_in.at[slot(k)], dst_ref=near_in.at[slot(k)], send_sem=s1.at[slot(k)],
            recv_sem=r1.at[slot(k)], device_id=(d, near), device_id_type=MESH)

    def load_own(k):
        return pltpu.make_async_copy(p_h.at[k], own.at[lax.rem(k, 2)], lp.at[lax.rem(k, 2)])

    def store(k):
        return pltpu.make_async_copy(low.at[lax.rem(k, 2)], o_h.at[k], lo.at[lax.rem(k, 2)])

    def emit(k, ref):
        @pl.when(k >= 2)
        def _():
            store(k - 2).wait()

        low[lax.rem(k, 2)] = ref[slot(k)].astype(LOW)
        store(k).start()

    def prime():
        @pl.when(end)
        def _():
            @pl.loop(0, WINDOW)
            def _(k):
                send_part(k).start()

        @pl.when(mid)
        def _():
            load_own(0).start()
            load_own(1).start()

    def tick(k):
        @pl.when(end & (k >= LAG) & (k < chunks + LAG))
        def _():
            j = k - LAG
            send_sum(j).wait_recv()
            send_part(j).wait_send()
            emit(j, near_in)

            @pl.when(j + WINDOW < chunks)
            def _():
                send_part(j + WINDOW).start()

        @pl.when(mid & (k < chunks))
        def _():
            send_part(k).wait_recv()
            load_own(k).wait()
            near_in[slot(k)] = near_in[slot(k)] + own[lax.rem(k, 2)]

            @pl.when(k >= HELD)
            def _():
                send_sum(k - HELD).wait_send()

            swap(k).start()

            @pl.when(k + 2 < chunks)
            def _():
                load_own(k + 2).start()

        @pl.when(mid & (k >= BACK) & (k < chunks + BACK))
        def _():
            j = k - BACK
            swap(j).wait()
            far_in[slot(j)] = near_in[slot(j)] + far_in[slot(j)]
            send_sum(j).start()
            emit(j, far_in)

    ntile, dtile = ff // TILE, cols // TILE

    def load_cot(r):
        return pltpu.make_async_copy(cot_h.at[at_tile(r, BLOCK)], cot_v.at[at_tile(r, BLOCK)], lsem.at[r])

    def load_x(r, xs, xsem):
        return pltpu.make_async_copy(x_h.at[at_tile(r, BLOCK)], xs.at[lax.rem(r, 2)], xsem.at[lax.rem(r, 2)])

    def put_p(r, which, pst):
        first = pl.multiple_of(which * (chunks // 2) + r * PER, PER)
        return pltpu.make_async_copy(pst, p_h.at[pl.ds(first, PER)], psem)

    def seen(r):
        return pl.ds(pl.multiple_of(jnp.maximum(r - (REACH - 1), 0) * BLOCK, BLOCK), REACH * BLOCK)

    def allowed(r):
        keys = REACH * BLOCK
        first = jnp.maximum(r - (REACH - 1), 0) * BLOCK
        query_at = lax.broadcasted_iota(jnp.int32, (BLOCK, keys), 0) + r * BLOCK
        key_at = lax.broadcasted_iota(jnp.int32, (BLOCK, keys), 1) + first
        query_seg = jnp.broadcast_to(seg[0:1, at_tile(r, BLOCK)], (8, BLOCK)).T[:, 0:1]
        return (query_seg == seg[0:1, seen(r)]) & (key_at <= query_at)

    vec[...] = jnp.zeros_like(vec)
    for at, ref in (
        (V_UP, up_b), (V_QKV, qkv_b), (V_GAIN1, gain1), (V_BIAS1, bias1), (V_GAIN2, gain2), (V_BIAS2, bias2), (V_OUT, dense_b)
    ):
        vec[at : at + 1, pl.ds(0, ref.shape[-1])] = ref[...].reshape(1, ref.shape[-1])
    vec[V_OUT : V_OUT + 1, :] += down_b[...]
    seg[...] = seg_in[...].astype(F32)
    lane = lax.broadcasted_iota(jnp.int32, (1, cols), 1)
    first_stat = 3 * subset[0]
    vec[V_CTX : V_CTX + 1, :] = jnp.where(lane == first_stat, 1.0, 0.0)
    vec[V_ACT : V_ACT + 1, :] = jnp.where(lane == first_stat + 1, 1.0, 0.0)
    count = jnp.where(t == 0, 1.0, 0.0).astype(F32) * rows
    vec[V_COUNT : V_COUNT + 1, :] = jnp.where(lane == first_stat + 2, count, 0.0)
    sv_v[...] = jnp.zeros_like(sv_v)
    sq_v[...] = jnp.zeros_like(sq_v)
    csq_v[...] = jnp.zeros_like(csq_v)
    score_scale = HS ** (-0.5)

    def with_inputs(up_v, qkv_v):
        def load_up(j):
            return pltpu.make_async_copy(up_h.at[:, at_tile(j, TILE)], up_v.at[:, at_tile(j, TILE)], wsem.at[2 * j])

        load_qkv = pltpu.make_async_copy(qkv_h, qkv_v, wsem.at[2 * ntile + 1])
        load_rot = pltpu.make_async_copy(rot_h, rot_v, lsem.at[steps])

        def forward_phase(down_v, dense_v, xs, pst, n1c, n2c, actc, slope, ctxc, xsem):
            def load_down(j):
                return pltpu.make_async_copy(down_h.at[at_tile(j, TILE)], down_v.at[at_tile(j, TILE)], wsem.at[2 * j + 1])

            load_dense = pltpu.make_async_copy(dense_h, dense_v, wsem.at[2 * ntile])
            load_x(0, xs, xsem).start()
            load_qkv.start()
            load_rot.start()
            k_v[...] = jnp.zeros_like(k_v)
            v_v[...] = jnp.zeros_like(v_v)

            def put_n(r):
                return (
                    pltpu.make_async_copy(n1c, n1_h.at[at_tile(r, BLOCK)], nsem.at[0]),
                    pltpu.make_async_copy(n2c, n2_h.at[at_tile(r, BLOCK)], nsem.at[1]),
                )

            @pl.loop(0, steps)
            def _(r):
                rds = at_tile(r, BLOCK)
                xcur = xs.at[lax.rem(r, 2)]
                load_x(r, xs, xsem).wait()

                @pl.when(r + 1 < steps)
                def _():
                    load_x(r + 1, xs, xsem).start()

                @pl.when(r > 0)
                def _():
                    for copy in put_n(r - 1):
                        copy.wait()

                @pl.loop(0, BLOCK // SUB, unroll=2)
                def _(s):
                    sds = at_tile(s, SUB)
                    xf = xcur[sds, :].astype(F32)
                    centre = xf - jnp.mean(xf, axis=-1, keepdims=True)
                    xh = centre * lax.rsqrt(jnp.mean(centre * centre, axis=-1, keepdims=True) + EPSILON)
                    n1c[sds, :] = (xh * vec[V_GAIN1 : V_GAIN1 + 1, :] + vec[V_BIAS1 : V_BIAS1 + 1, :]).astype(LOW)
                    n2c[sds, :] = (xh * vec[V_GAIN2 : V_GAIN2 + 1, :] + vec[V_BIAS2 : V_BIAS2 + 1, :]).astype(LOW)

                for copy in put_n(r):
                    copy.start()

                @pl.when(r == 0)
                def _():
                    load_qkv.wait()
                    load_rot.wait()
                    for j in range(ntile):
                        load_up(j).start()
                    load_cot(0).start()
                    load_dense.start()
                    pl.semaphore_wait(bar, 3 + ndp - 1)

                tables = turn_tables(rot_v[rds, :])
                for h in range(heads):
                    for part in range(3):
                        at = pl.ds((3 * h + part) * HS, HS)
                        head = dot_nn(n1c[...], qkv_v[:, at]) + vec[V_QKV : V_QKV + 1, at]
                        if part < 2:
                            head = turn(head, tables, 1)
                        (q_v, k_v, v_v)[part][h, rds, :] = head.astype(LOW)

                @pl.when(r == 0)
                def _():
                    for j in range(ntile):
                        load_down(j).start()

                ok = allowed(r)
                for h in range(heads):
                    scores = dot_nt(q_v[h, rds, :], k_v[h, seen(r), :]) * score_scale
                    scores = jnp.where(ok, scores, MASKED_SCORE)
                    peak = jnp.max(scores, axis=-1, keepdims=True)
                    weights = jnp.exp(scores - peak)
                    total = jnp.sum(weights, axis=-1, keepdims=True)
                    lse_v[rds, h * 64 : h * 64 + 64] = jnp.broadcast_to(peak + jnp.log(total), (BLOCK, 64))
                    context = dot_nn((weights / total).astype(LOW), v_v[h, seen(r), :])
                    csq_v[...] += jnp.sum((context * context).reshape(BLOCK // 8, 8, HS), axis=0)
                    context = context.astype(LOW)
                    ctxc[:, h * HS : (h + 1) * HS] = context
                    a_t[pl.ds(ff + h * HS, HS), rds] = context.T

                @pl.when(r > 0)
                def _():
                    tick(4 * r - 3)

                @pl.loop(0, ntile)
                def _(j):
                    jds = at_tile(j, TILE)

                    @pl.when(r == 0)
                    def _():
                        load_up(j).wait()

                    hidden = dot_nn(n2c[...], up_v[:, jds]) + vec[V_UP : V_UP + 1, jds]
                    cum = 0.5 * (1.0 + lax.erf(hidden * RSQRT2))
                    active = hidden * cum
                    slope[:, jds] = cum + hidden * jnp.exp(-0.5 * hidden * hidden) * RSQRT2PI
                    act_low = active.astype(LOW)
                    actc[:, jds] = act_low
                    sq_v[...] += jnp.sum((active * active).reshape(BLOCK // 8, 8, TILE), axis=0)

                @pl.when(r > 0)
                def _():
                    tick(4 * r - 2)

                @pl.when(r == 0)
                def _():
                    load_dense.wait()
                    for k in range(1, steps):
                        load_cot(k).start()

                    @pl.loop(0, ntile)
                    def _(j):
                        load_down(j).wait()

                @pl.loop(0, dtile)
                def _(j):
                    jds = at_tile(j, TILE)
                    term = dot_nn(actc[...], down_v[:, jds]) + dot_nn(ctxc[...], dense_v[:, jds])
                    term = term + add_here * (xcur[:, jds].astype(F32) + vec[V_OUT : V_OUT + 1, jds])
                    pst[:, :, jds] = term.reshape(PER, CH, TILE)

                put_p(r, 0, pst).start()

                @pl.loop(0, ntile)
                def _(j):
                    jds = at_tile(j, TILE)
                    a_t[jds, rds] = actc[:, jds].T

                put_p(r, 0, pst).wait()

                @pl.when(r == 0)
                def _():
                    prime()

                @pl.when(r > 0)
                def _():
                    tick(4 * r - 1)

                load_cot(r).wait()
                do_v[rds, :] = dot_nt(cot_v[rds, :], dense_v[...]).astype(LOW)

                @pl.loop(0, ntile)
                def _(j):
                    jds = at_tile(j, TILE)
                    d_hid = (dot_nt(cot_v[rds, :], down_v[jds, :]) * slope[:, jds]).astype(LOW)
                    dh_v[rds, jds] = d_hid
                    sv_v[S_UP : S_UP + 1, jds] += jnp.sum(d_hid.astype(F32), axis=0, keepdims=True)

                tick(4 * r)

            for copy in put_n(steps - 1):
                copy.wait()

        pl.run_scoped(
            forward_phase,
            pltpu.VMEM((ff, cols), LOW), pltpu.VMEM((att, cols), LOW),
            pltpu.VMEM((2, BLOCK, cols), LOW), pltpu.VMEM((PER, CH, cols), F32),
            pltpu.VMEM((BLOCK, cols), LOW), pltpu.VMEM((BLOCK, cols), LOW), pltpu.VMEM((BLOCK, ff), LOW),
            pltpu.VMEM((BLOCK, ff), F32), pltpu.VMEM((BLOCK, att), LOW), pltpu.SemaphoreType.DMA((2,)),
        )
        done = 4 * (steps - 1) + 1

        def lanes(ref, e):
            if width % 128 == 0:
                return ref[:, at_tile(e, width)]
            pair = ref[:, at_tile(lax.div(e, 2), 2 * width)]
            odd = lax.rem(e, 2) == 1
            return jnp.where(odd, pair[:, width:].astype(F32), pair[:, :width].astype(F32)).astype(LOW)

        def by_rows(right_ref):
            def compute(e, into, add):
                right = lanes(right_ref, e)

                @pl.loop(0, (ff + att) // TILE)
                def _(j):
                    part = dot_nn(a_t[at_tile(j, TILE), :], right)
                    if add:
                        part = part + into[at_tile(j, TILE), :]
                    into[at_tile(j, TILE), :] = part

            return compute

        def by_columns(left_ref, right_ref):
            def compute(e, into, add):
                left = lanes(left_ref, e).T

                @pl.loop(0, right_ref.shape[1] // TILE)
                def _(j):
                    part = dot_nn(left, right_ref[:, at_tile(j, TILE)])
                    if add:
                        part = part + into[:, at_tile(j, TILE)]
                    into[:, at_tile(j, TILE)] = part

            return compute

        def give(group, i, buf, got):
            return pltpu.make_async_remote_copy(
                src_ref=buf.at[0], dst_ref=got.at[i], send_sem=sa.at[group], recv_sem=ra.at[group * half + i],
                device_id=(mate, t), device_id_type=MESH)

        def mate_slice(group, i, buf, got, compute, again):
            @pl.when(again)
            def _():
                give(group, i, buf, got).wait_send()

            compute(2 * i + 1 - parity, buf.at[0], False)
            give(group, i, buf, got).start()

        def fetch(group, i, buf, got):
            return pltpu.make_async_copy(got.at[i], buf.at[1], ssem.at[group])

        def get_slice(group, i, buf, got):
            give(group, i, buf, got).wait_recv()
            fetch(group, i, buf, got).start()

        def put(group, i, buf, there):
            return pltpu.make_async_copy(buf.at[1], there.at[i], ssem.at[3 + group])

        def own_slice(group, i, buf, got, keep, out, compute):
            fetch(group, i, buf, got).wait()
            compute(2 * i + parity, buf.at[1], True)

            @pl.when(i == here)
            def _():
                put(group, i, buf, out).start()

            @pl.when(i != here)
            def _():
                put(group, i, buf, keep).start()

        def pass_slice(group, i, buf, keep, out):
            put(group, i, buf, keep).wait()

            @pl.when(i != here)
            def _():
                pltpu.make_async_remote_copy(
                    src_ref=keep.at[i], dst_ref=out.at[here], send_sem=sb.at[group * half + i],
                    recv_sem=rb.at[group * half + here], device_id=(2 * i + parity, t), device_id_type=MESH).start()

        def turn_of(i):
            return lax.bitwise_xor(here, half - 1 - lax.rem(i, half))

        def first_grads(n2_v, sd, su, gsem):
            load_n2 = pltpu.make_async_copy(n2_h, n2_v, gsem)
            load_n2.start()
            rows_of, columns_of = by_rows(cot_v), by_columns(n2_v, dh_v)

            @pl.loop(0, half + 1)
            def _(i):
                now, before = turn_of(i), turn_of(i + half - 1)

                @pl.when(i > 0)
                def _():
                    get_slice(0, before, sd, ad_h)

                @pl.when(i < half)
                def _():
                    mate_slice(0, now, sd, ad_h, rows_of, i > 0)

                @pl.when(i < PACED)
                def _():
                    tick(done + jnp.maximum(3 * i - 1, 0))

                @pl.when(i > 0)
                def _():
                    own_slice(0, before, sd, ad_h, bd_h, gd_h, rows_of)
                    get_slice(1, before, su, au_h)

                @pl.when(i == 0)
                def _():
                    load_n2.wait()

                @pl.when(i < half)
                def _():
                    mate_slice(1, now, su, au_h, columns_of, i > 0)

                @pl.when(i < PACED)
                def _():
                    tick(done + jnp.maximum(3 * i, 1))

                @pl.when(i > 0)
                def _():
                    pass_slice(0, before, sd, bd_h, gd_h)
                    own_slice(1, before, su, au_h, bu_h, gu_h, columns_of)

                    @pl.when(i <= PACED)
                    def _():
                        tick(done + jnp.minimum(3 * i + 1, 3 * PACED - 1))

                    pass_slice(1, before, su, bu_h, gu_h)

            give(0, 0, sd, ad_h).wait_send()
            give(1, 0, su, au_h).wait_send()

        pl.run_scoped(
            first_grads, pltpu.VMEM((rows, cols), LOW), pltpu.VMEM((2, ff + att, width), F32),
            pltpu.VMEM((2, width, ff), F32), pltpu.SemaphoreType.DMA,
        )
        done2 = done + 3 * PACED

        def back_phase(dk, dv):
            for h in range(heads):
                dk[...] = jnp.zeros_like(dk)
                dv[...] = jnp.zeros_like(dv)

                @pl.loop(0, steps)
                def _(r):
                    rds, kds = at_tile(r, BLOCK), seen(r)
                    query, keys, values = q_v[h, rds, :], k_v[h, kds, :], v_v[h, kds, :]
                    d_ctx = do_v[rds, h * HS : (h + 1) * HS]
                    scores = jnp.where(allowed(r), dot_nt(query, keys) * score_scale, MASKED_SCORE)
                    probs = jnp.exp(scores - lse_v[rds, h * 64 : h * 64 + 1])
                    dv[kds, :] += dot_nn(probs.astype(LOW).T, d_ctx)
                    d_probs = dot_nt(d_ctx, values)
                    inner = jnp.sum(probs * d_probs, axis=-1, keepdims=True)
                    d_scores = (probs * (d_probs - inner)).astype(LOW)
                    d_query = dot_nn(d_scores, keys) * score_scale
                    d_query = turn(d_query, turn_tables(rot_v[rds, :]), -1).astype(LOW)
                    dq_v[rds, pl.ds(3 * h * HS, HS)] = d_query
                    dk[kds, :] += dot_nn(d_scores.T, query) * score_scale
                    there = pl.ds(3 * h * HS, HS)
                    sv_v[S_QKV : S_QKV + 1, there] += jnp.sum(d_query.astype(F32), axis=0, keepdims=True)

                if h == 0:
                    tick(done2)

                @pl.loop(0, steps)
                def _(r):
                    rds = at_tile(r, BLOCK)
                    d_key = turn(dk[rds, :], turn_tables(rot_v[rds, :]), -1).astype(LOW)
                    d_value = dv[rds, :].astype(LOW)
                    for part, got in ((1, d_key), (2, d_value)):
                        there = pl.ds((3 * h + part) * HS, HS)
                        dq_v[rds, there] = got
                        sv_v[S_QKV : S_QKV + 1, there] += jnp.sum(got.astype(F32), axis=0, keepdims=True)

                if h == 0 or h == heads - 1:
                    tick(done2 + (1 if h == 0 else 2))

        pl.run_scoped(back_phase, pltpu.VMEM((rows, HS), F32), pltpu.VMEM((rows, HS), F32))
        done3 = done2 + 3

        def norm_phase(n1_v, nsem1, xs, pst, xhat, rstd, m1, m2, xsem):
            load_x(0, xs, xsem).start()
            pltpu.make_async_copy(n1_h, n1_v, nsem1).start()

            @pl.loop(0, steps)
            def _(r):
                rds = at_tile(r, BLOCK)
                xcur = xs.at[lax.rem(r, 2)]
                load_x(r, xs, xsem).wait()

                @pl.when(r + 1 < steps)
                def _():
                    load_x(r + 1, xs, xsem).start()

                @pl.loop(0, BLOCK // SUB, unroll=2)
                def _(s):
                    sds = at_tile(s, SUB)
                    xf = xcur[sds, :].astype(F32)
                    centre = xf - jnp.mean(xf, axis=-1, keepdims=True)
                    inv = lax.rsqrt(jnp.mean(centre * centre, axis=-1, keepdims=True) + EPSILON)
                    xhat[sds, :] = centre * inv
                    rstd[sds, :] = jnp.broadcast_to(inv, (SUB, 128))

                m1[...] = jnp.zeros_like(m1)
                m2[...] = jnp.zeros_like(m2)

                @pl.when(r > 1)
                def _():
                    put_p(r - 1, 1, pst).wait()

                @pl.loop(0, dtile)
                def _(j):
                    jds = at_tile(j, TILE)
                    xh = xhat[:, jds]
                    second = dot_nt(dh_v[rds, :], up_v[jds, :])
                    sv_v[S_GAIN2 : S_GAIN2 + 1, jds] += jnp.sum(second * xh, axis=0, keepdims=True)
                    sv_v[S_BIAS2 : S_BIAS2 + 1, jds] += jnp.sum(second, axis=0, keepdims=True)
                    first = dot_nt(dq_v[rds, :], qkv_v[jds, :])
                    sv_v[S_GAIN1 : S_GAIN1 + 1, jds] += jnp.sum(first * xh, axis=0, keepdims=True)
                    sv_v[S_BIAS1 : S_BIAS1 + 1, jds] += jnp.sum(first, axis=0, keepdims=True)
                    cot_tile = cot_v[rds, jds].astype(F32)
                    sv_v[S_OUT : S_OUT + 1, jds] += jnp.sum(cot_tile, axis=0, keepdims=True)
                    scaled = second * vec[V_GAIN2 : V_GAIN2 + 1, jds] + first * vec[V_GAIN1 : V_GAIN1 + 1, jds]
                    pst[:, :, jds] = scaled.reshape(PER, CH, TILE)
                    with_xh = scaled * xh
                    for q in range(TILE // 128):
                        m1[...] += scaled[:, q * 128 : (q + 1) * 128]
                        m2[...] += with_xh[:, q * 128 : (q + 1) * 128]

                tick(done3 + 2 * r)

                @pl.loop(0, PER)
                def _(s):
                    sds = at_tile(s, CH)
                    mean1 = jnp.sum(m1[sds, :], axis=-1, keepdims=True) * (1.0 / cols)
                    mean2 = jnp.sum(m2[sds, :], axis=-1, keepdims=True) * (1.0 / cols)
                    grad = rstd[sds, 0:1] * (pst[s] - mean1 - xhat[sds, :] * mean2)
                    cot_rows = cot_v[pl.ds(pl.multiple_of(r * BLOCK + s * CH, CH), CH), :].astype(F32)
                    pst[s] = grad + add_here * cot_rows

                put_p(r, 1, pst).start()

                @pl.when(r == 0)
                def _():
                    put_p(r, 1, pst).wait()

                tick(done3 + 2 * r + 1)

            put_p(steps - 1, 1, pst).wait()

        done4 = done3 + 2 * steps

        def last_grads(n1_v, nsem1, sq):
            pltpu.make_async_copy(n1_h, n1_v, nsem1).wait()
            columns_of = by_columns(n1_v, dq_v)

            @pl.loop(0, half + 1)
            def _(i):
                now, before = turn_of(i), turn_of(i + half - 1)

                @pl.when(i > 0)
                def _():
                    get_slice(2, before, sq, aq_h)

                @pl.when(i < half)
                def _():
                    mate_slice(2, now, sq, aq_h, columns_of, i > 0)

                @pl.when(i < PACED)
                def _():
                    tick(done4 + jnp.maximum(2 * i - 1, 0))

                @pl.when(i > 0)
                def _():
                    own_slice(2, before, sq, aq_h, bq_h, gq_h, columns_of)

                    @pl.when(i <= PACED)
                    def _():
                        tick(done4 + jnp.minimum(2 * i, 2 * PACED - 1))

                    pass_slice(2, before, sq, bq_h, gq_h)

            give(2, 0, sq, aq_h).wait_send()

        def small_sums():
            sv_v[S_STATS : S_STATS + 1, :] += (
                jnp.sum(csq_v[...]) * vec[V_CTX : V_CTX + 1, :]
                + jnp.sum(sq_v[...]) * vec[V_ACT : V_ACT + 1, :]
                + vec[V_COUNT : V_COUNT + 1, :]
            )
            svd[d] = sv_v[...]

            @pl.loop(1, ndp)
            def _(k):
                give_dp(k).start()

        def with_n1(n1_v, nsem1):
            pl.run_scoped(
                functools.partial(norm_phase, n1_v, nsem1),
                pltpu.VMEM((2, BLOCK, cols), LOW), pltpu.VMEM((PER, CH, cols), F32), pltpu.VMEM((BLOCK, cols), F32),
                pltpu.VMEM((BLOCK, 128), F32), pltpu.VMEM((BLOCK, 128), F32), pltpu.VMEM((BLOCK, 128), F32),
                pltpu.SemaphoreType.DMA((2,)),
            )
            small_sums()
            pl.run_scoped(functools.partial(last_grads, n1_v, nsem1), pltpu.VMEM((2, width, qw), F32))

        pl.run_scoped(with_n1, pltpu.VMEM((rows, cols), LOW), pltpu.SemaphoreType.DMA)

    def give_dp(k):
        return pltpu.make_async_remote_copy(
            src_ref=sv_v, dst_ref=svd.at[d], send_sem=ssv.at[k], recv_sem=rsv.at[d],
            device_id=(lax.rem(d + k, ndp), t), device_id_type=MESH)

    def get_dp(k):
        other = lax.rem(d + k, ndp)
        return pltpu.make_async_remote_copy(
            src_ref=sv_v, dst_ref=svd.at[other], send_sem=ssv.at[k], recv_sem=rsv.at[other],
            device_id=(other, t), device_id_type=MESH)

    pl.run_scoped(with_inputs, pltpu.VMEM((cols, ff), LOW), pltpu.VMEM((cols, qw), LOW))
    finished = 4 * (steps - 1) + 1 + 3 * PACED + 3 + 2 * steps + 2 * PACED
    tiles_down, tiles_up, tiles_qkv = (ff + att) // TILE, ff // TILE, qw // TILE
    before_last = chunks - tiles_down - tiles_up - 5

    @pl.loop(finished, before_last)
    def _(k):
        tick(k)

    def give_z(k):
        return pltpu.make_async_remote_copy(
            src_ref=sv_o.at[0], dst_ref=svz.at[t], send_sem=ssz.at[k], recv_sem=rsz.at[t],
            device_id=(d, lax.rem(t + k, 4)), device_id_type=MESH)

    def get_z(k):
        other = lax.rem(t + k, 4)
        return pltpu.make_async_remote_copy(
            src_ref=sv_o.at[0], dst_ref=svz.at[other], send_sem=ssz.at[k], recv_sem=rsz.at[other],
            device_id=(d, other), device_id_type=MESH)

    def small_totals():
        @pl.loop(1, ndp)
        def _(k):
            get_dp(k).wait_recv()
            give_dp(k).wait_send()

        total = svd[0]
        for i in range(1, ndp):
            total = total + svd[i]
        sv_o[0] = total
        svz[t] = total
        for k in range(1, 4):
            give_z(k).start()

    def landed(group, keep, out):
        @pl.loop(0, half)
        def _(i):
            @pl.when(i != here)
            def _():
                sent = pltpu.make_async_remote_copy(
                    src_ref=keep.at[i], dst_ref=out.at[i], send_sem=sb.at[group * half + i],
                    recv_sem=rb.at[group * half + i], device_id=(2 * i + parity, t), device_id_type=MESH)
                sent.wait_send()
                sent.wait_recv()

    def sum_phase(tall, tall_sum, wide, wide_sum, fsem, usem):
        def tiles_d():
            for j in range((ff + att) // TILE):
                there = down_g.at[pl.ds(j * TILE, TILE)] if j < ff // TILE else dense_g.at[pl.ds(j * TILE - ff, TILE)]
                yield gd_h.at[:, pl.ds(j * TILE, TILE)], there

        def tiles_w(got, result):
            for j in range(got.shape[2] // TILE):
                yield got.at[:, :, pl.ds(j * TILE, TILE)], result.at[:, pl.ds(j * TILE, TILE)]

        def add_up(pairs, parts, total):
            pairs = list(pairs)

            def get(j):
                return pltpu.make_async_copy(pairs[j][0], parts.at[j % 2], fsem.at[j % 2])

            def put_sum(j):
                return pltpu.make_async_copy(total.at[j % 2], pairs[j][1], usem.at[j % 2])

            get(0).start()
            for j in range(len(pairs)):
                if j + 1 < len(pairs):
                    get(j + 1).start()
                get(j).wait()
                if j >= 2:
                    put_sum(j - 2).wait()
                acc = parts[j % 2, 0]
                for i in range(1, half):
                    acc = acc + parts[j % 2, i]
                total[j % 2] = acc
                put_sum(j).start()
                yield
            for j in range(max(len(pairs) - 2, 0), len(pairs)):
                put_sum(j).wait()

        at = before_last
        for group, keep, out, work in (
            (0, bd_h, gd_h, lambda: add_up(tiles_d(), tall, tall_sum)),
            (1, bu_h, gu_h, lambda: add_up(tiles_w(gu_h, up_g), wide, wide_sum)),
            (2, bq_h, gq_h, lambda: add_up(tiles_w(gq_h, qkv_g), wide, wide_sum)),
        ):
            if group == 2:
                small_totals()

                @pl.loop(at, chunks + BACK)
                def _(k):
                    tick(k)

                at = chunks + BACK
            landed(group, keep, out)
            for _ in work():
                tick(at)
                at += 1

    pl.run_scoped(
        sum_phase,
        pltpu.VMEM((2, half, TILE, width), F32), pltpu.VMEM((2, TILE, width), F32),
        pltpu.VMEM((2, half, width, TILE), F32), pltpu.VMEM((2, width, TILE), F32),
        pltpu.SemaphoreType.DMA((2,)), pltpu.SemaphoreType.DMA((2,)),
    )

    @pl.loop(chunks + BACK + tiles_qkv, chunks + LAG)
    def _(k):
        tick(k)

    for k in range(1, 4):
        get_z(k).wait_recv()
        give_z(k).wait_send()
    sv_o[1] = svz[0] + svz[1] + svz[2] + svz[3]

    @pl.when(mid)
    def _():
        @pl.loop(chunks - HELD, chunks)
        def _(k):
            send_sum(k).wait_send()

    store(chunks - 2).wait()
    store(chunks - 1).wait()


def layer(ndp, vectors, segments, subsets, x, cot, rot, up_w, down_w, dense_w, qkv_w):
    rows, cols = x.shape
    ff, att, qw = up_w.shape[1], dense_w.shape[0], qkv_w.shape[1]
    heads = att // HS
    width, half, steps, chunks = cols // ndp, ndp // 2, rows // BLOCK, 2 * rows // CH
    any_spec = pl.BlockSpec(memory_space=pl.ANY)
    vmem_spec = pl.BlockSpec(memory_space=pltpu.VMEM)
    sem = pltpu.SemaphoreType.DMA
    slices = [
        jax.ShapeDtypeStruct((half, ff + att, width), F32),
        jax.ShapeDtypeStruct((half, width, ff), F32),
        jax.ShapeDtypeStruct((half, width, qw), F32),
    ]
    return pl.pallas_call(
        functools.partial(layer_kernel, ndp),
        out_shape=[
            jax.ShapeDtypeStruct((chunks, CH, cols), LOW),
            jax.ShapeDtypeStruct((2, SV, cols), F32),
            jax.ShapeDtypeStruct((ff, width), F32),
            jax.ShapeDtypeStruct((att, width), F32),
            jax.ShapeDtypeStruct((width, ff), F32),
            jax.ShapeDtypeStruct((width, qw), F32),
            *slices,
            jax.ShapeDtypeStruct((chunks, CH, cols), F32),
            jax.ShapeDtypeStruct((rows, cols), LOW),
            jax.ShapeDtypeStruct((rows, cols), LOW),
            *slices,
            *slices,
        ],
        in_specs=[vmem_spec] * 9 + [pl.BlockSpec(memory_space=pltpu.SMEM)] + [any_spec] * 7,
        out_specs=[any_spec, vmem_spec] + [any_spec] * 16,
        scratch_shapes=[
            pltpu.VMEM((VROWS, cols), F32), pltpu.VMEM((1, rows), F32),
            pltpu.VMEM((ff + att, rows), LOW), pltpu.VMEM((rows, cols), LOW), pltpu.VMEM((rows, ff), LOW),
            pltpu.VMEM((rows, qw), LOW), pltpu.VMEM((heads, rows, HS), LOW), pltpu.VMEM((heads, rows, HS), LOW),
            pltpu.VMEM((heads, rows, HS), LOW), pltpu.VMEM((rows, att), LOW), pltpu.VMEM((rows, 64 * heads), F32),
            pltpu.VMEM((rows, 128), F32), pltpu.VMEM((SV, cols), F32),
            pltpu.VMEM((8, TILE), F32), pltpu.VMEM((8, HS), F32),
            pltpu.VMEM((ndp, SV, cols), F32), pltpu.VMEM((4, SV, cols), F32),
            pltpu.VMEM((WINDOW, CH, cols), F32), pltpu.VMEM((WINDOW, CH, cols), F32),
            pltpu.VMEM((2, CH, cols), F32), pltpu.VMEM((2, CH, cols), LOW),
            sem((WINDOW,)), sem((WINDOW,)), sem((WINDOW,)), sem((WINDOW,)), sem((2,)), sem((2,)),
            sem((steps + 1,)), sem((2 * (ff // TILE) + 2,)), sem, sem((2,)),
            sem((ndp,)), sem((ndp,)), sem((4,)), sem((4,)),
            sem((3,)), sem((3 * half,)), sem((3 * half,)), sem((3 * half,)), sem((6,)),
        ],
        compiler_params=pltpu.CompilerParams(
            collective_id=0, has_side_effects=True, vmem_limit_bytes=VMEM_ASK),
        cost_estimate=pl.CostEstimate(flops=10**11, bytes_accessed=2 * 10**8, transcendentals=0),
        name="layer",
    )(*vectors, segments, subsets, x, cot, rot, up_w, down_w, dense_w, qkv_w)


def flat_shape(size):
    return (1, size) if size % 1024 == 0 else (size,)


SMALL_ROWS = ((1, S_GAIN1), (1, S_BIAS1), (0, S_QKV), (0, S_OUT), (1, S_GAIN2), (1, S_BIAS2), (0, S_UP), (0, S_OUT))


def finish_kernel(o_h, down_h, dense_h, up_h, qkv_h, small, *rest):
    out, grad, down_g, dense_g, up_g, qkv_g = rest[:6]
    row_refs, rms, held, sems_in, sems_out = rest[6:14], rest[14], rest[15:21], rest[21], rest[22]
    half_chunks = out.shape[0]
    copies = []
    for index, (source, target) in enumerate((
        (o_h.at[pl.ds(0, half_chunks)], out), (o_h.at[pl.ds(half_chunks, half_chunks)], grad),
        (down_h, down_g), (dense_h, dense_g), (up_h, up_g), (qkv_h, qkv_g),
    )):
        count = source.shape[0] // PIECES
        for piece in range(PIECES):
            at = pl.ds(piece * count, count)
            buf, sem = held[index].at[at], PIECES * index + piece
            copies.append((
                pltpu.make_async_copy(source.at[at], buf, sems_in.at[sem]),
                pltpu.make_async_copy(buf, target.at[at], sems_out.at[sem]),
            ))
    for load, _ in copies:
        load.start()
    for (which, row), ref in zip(SMALL_ROWS, row_refs):
        if len(ref.shape) == 1:
            ref[...] = small[which, row, pl.ds(0, ref.shape[0])]
        else:
            ref[...] = small[which, row : row + 1, pl.ds(0, ref.shape[1])]
    lane = lax.broadcasted_iota(jnp.int32, (128, 128), 1)
    place = lax.broadcasted_iota(jnp.int32, (128, 128), 0)
    stats = jnp.broadcast_to(small[1, S_STATS : S_STATS + 1, :128], (8, 128)).T[:, 0:1]
    context, active, count = (
        jnp.sum(jnp.where(place == 3 * lane + part, stats, 0.0), axis=0, keepdims=True) for part in range(3)
    )
    count = jnp.maximum(count, 1.0)
    rms[0:1, :] = jnp.sqrt(context / (count * (HEADS * HS)))[:, :SUBSETS]
    rms[1:2, :] = jnp.sqrt(active / (count * FF))[:, :SUBSETS]
    for load, save in copies:
        load.wait()
        save.start()
    for _, save in copies:
        save.wait()


PIECES = 4


def finish(sums, small, down_grad, dense_grad, up_grad, qkv_grad):
    chunks, per, cols = sums.shape
    grads = (down_grad, dense_grad, up_grad, qkv_grad)
    qw, ff = qkv_grad.shape[1], up_grad.shape[1]
    any_spec = pl.BlockSpec(memory_space=pl.ANY)
    vmem_spec = pl.BlockSpec(memory_space=pltpu.VMEM)
    row_widths = [cols, cols, qw, cols, cols, cols, ff, cols]
    return pl.pallas_call(
        finish_kernel,
        out_shape=[jax.ShapeDtypeStruct((chunks // 2, per, cols), LOW)] * 2
        + [jax.ShapeDtypeStruct(grad.shape, F32) for grad in grads]
        + [jax.ShapeDtypeStruct(flat_shape(row_width), F32) for row_width in row_widths]
        + [jax.ShapeDtypeStruct((2, SUBSETS), F32)],
        in_specs=[any_spec] * 5 + [vmem_spec],
        out_specs=[any_spec] * 6 + [vmem_spec] * 9,
        scratch_shapes=[pltpu.VMEM((chunks // 2, per, cols), LOW)] * 2
        + [pltpu.VMEM(grad.shape, F32) for grad in grads]
        + [pltpu.SemaphoreType.DMA((6 * PIECES,))] * 2,
        compiler_params=pltpu.CompilerParams(vmem_limit_bytes=VMEM_ASK),
        name="finish",
    )(sums, *grads, small)


def turn_table(length):
    frequency = np.float32(10000.0) ** (-(np.float32(2.0) * np.arange(ROT // 2, dtype=np.float32)) / np.float32(ROT))
    angles = np.arange(length, dtype=np.float32)[:, None] * frequency.astype(np.float32)[None, :]
    angles = np.concatenate([angles, angles], axis=1).astype(np.float32)
    return np.concatenate([np.cos(angles), np.sin(angles)], axis=1).astype(np.float32)


def on_device(
    ndp,
    inputs,
    cotangent,
    segments,
    subsets,
    ln1_gain,
    ln1_bias,
    qkv_weight,
    qkv_bias,
    dense_weight,
    dense_bias,
    ln2_gain,
    ln2_bias,
    up_weight,
    up_bias,
    down_weight,
    down_bias,
):
    rows_here, model = inputs.shape
    vectors = [
        values.reshape(flat_shape(values.shape[0]))
        for values in (up_bias, qkv_bias, ln1_gain, ln1_bias, ln2_gain, ln2_bias, dense_bias, down_bias)
    ]
    held = layer(
        ndp, vectors, segments, subsets, inputs, cotangent, jnp.asarray(turn_table(LEN)),
        up_weight, down_weight, dense_weight, qkv_weight)[:6]
    done = finish(*held)
    out, input_grad, down_grad, dense_grad, up_grad, qkv_grad = done[:6]
    gain1, bias1, qkv_bias_grad, bias_out, gain2, bias2, up_bias_grad, bias_out_again = (
        row.reshape(-1) for row in done[6:14]
    )
    return (
        out.reshape(rows_here, model),
        input_grad.reshape(rows_here, model),
        gain1,
        bias1,
        qkv_grad,
        qkv_bias_grad,
        dense_grad,
        bias_out,
        gain2,
        bias2,
        up_grad,
        up_bias_grad,
        down_grad,
        bias_out_again,
        done[14].T,
    )


def solution(mesh):
    placed = (
        P("dp", None),
        P("dp", None),
        P("dp", None),
        P("dp"),
        P(),
        P(),
        P(None, "tensor"),
        P("tensor"),
        P("tensor", None),
        P(),
        P(),
        P(),
        P(None, "tensor"),
        P("tensor"),
        P("tensor", None),
        P(),
    )
    return jax.shard_map(
        functools.partial(on_device, mesh.shape["dp"]),
        mesh=mesh,
        in_specs=placed,
        out_specs=(
            P("dp", None),
            P("dp", None),
            P(),
            P(),
            P("dp", "tensor"),
            P("tensor"),
            P("tensor", "dp"),
            P(),
            P(),
            P(),
            P("dp", "tensor"),
            P("tensor"),
            P("tensor", "dp"),
            P(),
            P(),
        ),
        check_vma=False,
    )
```

```python
import functools

import jax
import jax.numpy as jnp
import numpy as np
from jax import lax
from jax.experimental import pallas as pl
from jax.experimental.pallas import tpu as pltpu
from jax.sharding import PartitionSpec as P

HEADS = 8
HS = 256
ROT = 64
FF = 8192
SUBSETS = 22
LEN = 1024


EPSILON = 1e-05
MASKED_SCORE = -1000000000.0


VMEM_ASK = 64 * 2**20

MESH = pl.DeviceIdType.MESH
F32 = jnp.float32
LOW = jnp.bfloat16
BLOCK = 256
REACH = 3
CH = 32
PER = BLOCK // CH
WINDOW = 8
HELD = 4
BACK = 2
LAG = 5
PACED = 4
TILE = 512
SUB = 16
RSQRT2 = 0.7071067811865476
RSQRT2PI = 0.3989422804014327
SV = 8
S_GAIN1, S_BIAS1, S_GAIN2, S_BIAS2, S_STATS, S_UP, S_QKV, S_OUT = range(SV)
VROWS = 16
V_UP, V_GAIN1, V_BIAS1, V_GAIN2, V_BIAS2, V_OUT, V_QKV, V_CTX, V_ACT, V_COUNT = range(10)


def dot_nn(left, right):
    return lax.dot_general(left, right, (((1,), (0,)), ((), ())), preferred_element_type=F32)


def dot_nt(left, right):
    return lax.dot_general(left, right, (((1,), (1,)), ((), ())), preferred_element_type=F32)


def at_tile(index, width):
    return pl.ds(pl.multiple_of(index * width, width), width)


def turn_tables(packed):
    lane = lax.broadcasted_iota(jnp.int32, packed.shape, 1)
    half_rot = ROT // 2
    sine = pltpu.roll(packed, 64, 1)
    cosine = jnp.where(lane < ROT, packed, 1.0)
    from_upper = jnp.where(lane < half_rot, -sine, 0.0)
    from_lower = jnp.where((lane >= half_rot) & (lane < ROT), sine, 0.0)
    return cosine, from_upper, from_lower


def turn(head, tables, sign):
    cosine, from_upper, from_lower = tables
    low_part = head[:, :128]
    moved = pltpu.roll(low_part, 128 - ROT // 2, 1) * from_upper + pltpu.roll(low_part, ROT // 2, 1) * from_lower
    low_part = low_part * cosine + moved if sign > 0 else low_part * cosine - moved
    return jnp.concatenate([low_part, head[:, 128:]], axis=1)


def layer_kernel(
    ndp,
    up_b, qkv_b, gain1, bias1, gain2, bias2, dense_b, down_b, seg_in, subset, x_h, cot_h, rot_h, up_h, down_h, dense_h, qkv_h,
    o_h, sv_o, down_g, dense_g, up_g, qkv_g, gd_h, gu_h, gq_h, p_h, n1_h, n2_h, ad_h, au_h, aq_h, bd_h, bu_h, bq_h,
    vec, seg, a_t, cot_v, dh_v, dq_v, q_v, k_v, v_v, do_v, lse_v, rot_v, sv_v, sq_v, csq_v, svd, svz,
    near_in, far_in, own, low,
    s1, r1, s2, r2, lp, lo, lsem, wsem, psem, nsem,
    ssv, rsv, ssz, rsz, sa, ra, sb, rb, ssem,
):
    d = lax.axis_index("dp")
    t = lax.axis_index("tensor")
    rows, cols = x_h.shape
    ff = up_h.shape[1]
    att = dense_h.shape[0]
    heads = att // HS
    qw = qkv_h.shape[1]
    width = cols // ndp
    half = ndp // 2
    steps = rows // BLOCK
    chunks = 2 * rows // CH
    near = t + 1 - 2 * lax.rem(t, 2)
    far = 3 - t
    mid = (t == 1) | (t == 2)
    end = jnp.logical_not(mid)
    parity = lax.rem(d, 2)
    mate = d + 1 - 2 * parity
    here = lax.div(d, 2)
    add_here = jnp.where(t == 1, 1.0, 0.0).astype(F32)

    bar = pltpu.get_barrier_semaphore()
    for k in range(1, 4):
        pl.semaphore_signal(bar, inc=1, device_id=(d, lax.rem(t + k, 4)), device_id_type=MESH)

    @pl.loop(1, ndp)
    def _(k):
        pl.semaphore_signal(bar, inc=1, device_id=(lax.rem(d + k, ndp), t), device_id_type=MESH)

    def slot(k):
        return lax.rem(k, WINDOW)

    def send_part(k):
        return pltpu.make_async_remote_copy(
            src_ref=p_h.at[k], dst_ref=near_in.at[slot(k)], send_sem=s1.at[slot(k)],
            recv_sem=r1.at[slot(k)], device_id=(d, near), device_id_type=MESH)

    def swap(k):
        return pltpu.make_async_remote_copy(
            src_ref=near_in.at[slot(k)], dst_ref=far_in.at[slot(k)], send_sem=s2.at[slot(k)],
            recv_sem=r2.at[slot(k)], device_id=(d, far), device_id_type=MESH)

    def send_sum(k):
        return pltpu.make_async_remote_copy(
            src_ref=far_in.at[slot(k)], dst_ref=near_in.at[slot(k)], send_sem=s1.at[slot(k)],
            recv_sem=r1.at[slot(k)], device_id=(d, near), device_id_type=MESH)

    def load_own(k):
        return pltpu.make_async_copy(p_h.at[k], own.at[lax.rem(k, 2)], lp.at[lax.rem(k, 2)])

    def store(k):
        return pltpu.make_async_copy(low.at[lax.rem(k, 2)], o_h.at[k], lo.at[lax.rem(k, 2)])

    def emit(k, ref):
        @pl.when(k >= 2)
        def _():
            store(k - 2).wait()

        low[lax.rem(k, 2)] = ref[slot(k)].astype(LOW)
        store(k).start()

    def prime():
        @pl.when(end)
        def _():
            @pl.loop(0, WINDOW)
            def _(k):
                send_part(k).start()

        @pl.when(mid)
        def _():
            load_own(0).start()
            load_own(1).start()

    def tick(k):
        @pl.when(end & (k >= LAG) & (k < chunks + LAG))
        def _():
            j = k - LAG
            send_sum(j).wait_recv()
            send_part(j).wait_send()
            emit(j, near_in)

            @pl.when(j + WINDOW < chunks)
            def _():
                send_part(j + WINDOW).start()

        @pl.when(mid & (k < chunks))
        def _():
            send_part(k).wait_recv()
            load_own(k).wait()
            near_in[slot(k)] = near_in[slot(k)] + own[lax.rem(k, 2)]

            @pl.when(k >= HELD)
            def _():
                send_sum(k - HELD).wait_send()

            swap(k).start()

            @pl.when(k + 2 < chunks)
            def _():
                load_own(k + 2).start()

        @pl.when(mid & (k >= BACK) & (k < chunks + BACK))
        def _():
            j = k - BACK
            swap(j).wait()
            far_in[slot(j)] = near_in[slot(j)] + far_in[slot(j)]
            send_sum(j).start()
            emit(j, far_in)

    ntile, dtile = ff // TILE, cols // TILE

    def load_cot(r):
        return pltpu.make_async_copy(cot_h.at[at_tile(r, BLOCK)], cot_v.at[at_tile(r, BLOCK)], lsem.at[r])

    def load_x(r, xs, xsem):
        return pltpu.make_async_copy(x_h.at[at_tile(r, BLOCK)], xs.at[lax.rem(r, 2)], xsem.at[lax.rem(r, 2)])

    def put_p(r, which, pst):
        first = pl.multiple_of(which * (chunks // 2) + r * PER, PER)
        return pltpu.make_async_copy(pst, p_h.at[pl.ds(first, PER)], psem)

    def seen(r):
        return pl.ds(pl.multiple_of(jnp.maximum(r - (REACH - 1), 0) * BLOCK, BLOCK), REACH * BLOCK)

    def allowed(r):
        keys = REACH * BLOCK
        first = jnp.maximum(r - (REACH - 1), 0) * BLOCK
        query_at = lax.broadcasted_iota(jnp.int32, (BLOCK, keys), 0) + r * BLOCK
        key_at = lax.broadcasted_iota(jnp.int32, (BLOCK, keys), 1) + first
        query_seg = jnp.broadcast_to(seg[0:1, at_tile(r, BLOCK)], (8, BLOCK)).T[:, 0:1]
        return (query_seg == seg[0:1, seen(r)]) & (key_at <= query_at)

    vec[...] = jnp.zeros_like(vec)
    for at, ref in (
        (V_UP, up_b), (V_QKV, qkv_b), (V_GAIN1, gain1), (V_BIAS1, bias1), (V_GAIN2, gain2), (V_BIAS2, bias2), (V_OUT, dense_b)
    ):
        vec[at : at + 1, pl.ds(0, ref.shape[-1])] = ref[...].reshape(1, ref.shape[-1])
    vec[V_OUT : V_OUT + 1, :] += down_b[...]
    seg[...] = seg_in[...].astype(F32)
    lane = lax.broadcasted_iota(jnp.int32, (1, cols), 1)
    first_stat = 3 * subset[0]
    vec[V_CTX : V_CTX + 1, :] = jnp.where(lane == first_stat, 1.0, 0.0)
    vec[V_ACT : V_ACT + 1, :] = jnp.where(lane == first_stat + 1, 1.0, 0.0)
    count = jnp.where(t == 0, 1.0, 0.0).astype(F32) * rows
    vec[V_COUNT : V_COUNT + 1, :] = jnp.where(lane == first_stat + 2, count, 0.0)
    sv_v[...] = jnp.zeros_like(sv_v)
    sq_v[...] = jnp.zeros_like(sq_v)
    csq_v[...] = jnp.zeros_like(csq_v)
    score_scale = HS ** (-0.5)

    def with_inputs(up_v, qkv_v):
        def load_up(j):
            return pltpu.make_async_copy(up_h.at[:, at_tile(j, TILE)], up_v.at[:, at_tile(j, TILE)], wsem.at[2 * j])

        load_qkv = pltpu.make_async_copy(qkv_h, qkv_v, wsem.at[2 * ntile + 1])
        load_rot = pltpu.make_async_copy(rot_h, rot_v, lsem.at[steps])

        def forward_phase(down_v, dense_v, xs, pst, n1c, n2c, actc, slope, ctxc, xsem):
            def load_down(j):
                return pltpu.make_async_copy(down_h.at[at_tile(j, TILE)], down_v.at[at_tile(j, TILE)], wsem.at[2 * j + 1])

            load_dense = pltpu.make_async_copy(dense_h, dense_v, wsem.at[2 * ntile])
            load_x(0, xs, xsem).start()
            load_qkv.start()
            load_rot.start()
            k_v[...] = jnp.zeros_like(k_v)
            v_v[...] = jnp.zeros_like(v_v)

            def put_n(r):
                return (
                    pltpu.make_async_copy(n1c, n1_h.at[at_tile(r, BLOCK)], nsem.at[0]),
                    pltpu.make_async_copy(n2c, n2_h.at[at_tile(r, BLOCK)], nsem.at[1]),
                )

            @pl.loop(0, steps)
            def _(r):
                rds = at_tile(r, BLOCK)
                xcur = xs.at[lax.rem(r, 2)]
                load_x(r, xs, xsem).wait()

                @pl.when(r == 0)
                def _():
                    for j in range(ntile):
                        load_up(j).start()

                @pl.when(r + 1 < steps)
                def _():
                    load_x(r + 1, xs, xsem).start()

                @pl.when(r > 0)
                def _():
                    for copy in put_n(r - 1):
                        copy.wait()

                @pl.loop(0, BLOCK // SUB, unroll=2)
                def _(s):
                    sds = at_tile(s, SUB)
                    xf = xcur[sds, :].astype(F32)
                    centre = xf - jnp.mean(xf, axis=-1, keepdims=True)
                    xh = centre * lax.rsqrt(jnp.mean(centre * centre, axis=-1, keepdims=True) + EPSILON)
                    n1c[sds, :] = (xh * vec[V_GAIN1 : V_GAIN1 + 1, :] + vec[V_BIAS1 : V_BIAS1 + 1, :]).astype(LOW)
                    n2c[sds, :] = (xh * vec[V_GAIN2 : V_GAIN2 + 1, :] + vec[V_BIAS2 : V_BIAS2 + 1, :]).astype(LOW)

                for copy in put_n(r):
                    copy.start()

                @pl.when(r == 0)
                def _():
                    load_qkv.wait()
                    load_rot.wait()
                    load_dense.start()
                    for j in range(ntile):
                        load_down(j).start()
                    load_cot(0).start()
                    pl.semaphore_wait(bar, 3 + ndp - 1)

                tables = turn_tables(rot_v[rds, :])
                for h in range(heads):
                    for part in range(3):
                        at = pl.ds((3 * h + part) * HS, HS)
                        head = dot_nn(n1c[...], qkv_v[:, at]) + vec[V_QKV : V_QKV + 1, at]
                        if part < 2:
                            head = turn(head, tables, 1)
                        (q_v, k_v, v_v)[part][h, rds, :] = head.astype(LOW)

                ok = allowed(r)
                for h in range(heads):
                    scores = dot_nt(q_v[h, rds, :], k_v[h, seen(r), :]) * score_scale
                    scores = jnp.where(ok, scores, MASKED_SCORE)
                    peak = jnp.max(scores, axis=-1, keepdims=True)
                    weights = jnp.exp(scores - peak)
                    total = jnp.sum(weights, axis=-1, keepdims=True)
                    lse_v[rds, h * 64 : h * 64 + 64] = jnp.broadcast_to(peak + jnp.log(total), (BLOCK, 64))
                    context = dot_nn((weights / total).astype(LOW), v_v[h, seen(r), :])
                    csq_v[...] += jnp.sum((context * context).reshape(BLOCK // 8, 8, HS), axis=0)
                    context = context.astype(LOW)
                    ctxc[:, h * HS : (h + 1) * HS] = context
                    a_t[pl.ds(ff + h * HS, HS), rds] = context.T

                @pl.when(r > 0)
                def _():
                    tick(4 * r - 3)

                @pl.loop(0, ntile)
                def _(j):
                    jds = at_tile(j, TILE)

                    @pl.when(r == 0)
                    def _():
                        load_up(j).wait()

                    hidden = dot_nn(n2c[...], up_v[:, jds]) + vec[V_UP : V_UP + 1, jds]
                    cum = 0.5 * (1.0 + lax.erf(hidden * RSQRT2))
                    active = hidden * cum
                    slope[:, jds] = cum + hidden * jnp.exp(-0.5 * hidden * hidden) * RSQRT2PI
                    act_low = active.astype(LOW)
                    actc[:, jds] = act_low
                    sq_v[...] += jnp.sum((active * active).reshape(BLOCK // 8, 8, TILE), axis=0)

                @pl.when(r > 0)
                def _():
                    tick(4 * r - 2)

                @pl.when(r == 0)
                def _():
                    load_dense.wait()
                    for k in range(1, steps):
                        load_cot(k).start()

                    @pl.loop(0, ntile)
                    def _(j):
                        load_down(j).wait()

                @pl.loop(0, dtile)
                def _(j):
                    jds = at_tile(j, TILE)
                    term = dot_nn(actc[...], down_v[:, jds]) + dot_nn(ctxc[...], dense_v[:, jds])
                    term = term + add_here * (xcur[:, jds].astype(F32) + vec[V_OUT : V_OUT + 1, jds])
                    pst[:, :, jds] = term.reshape(PER, CH, TILE)

                put_p(r, 0, pst).start()

                @pl.loop(0, ntile)
                def _(j):
                    jds = at_tile(j, TILE)
                    a_t[jds, rds] = actc[:, jds].T

                put_p(r, 0, pst).wait()

                @pl.when(r == 0)
                def _():
                    prime()

                @pl.when(r > 0)
                def _():
                    tick(4 * r - 1)

                load_cot(r).wait()
                do_v[rds, :] = dot_nt(cot_v[rds, :], dense_v[...]).astype(LOW)

                @pl.loop(0, ntile)
                def _(j):
                    jds = at_tile(j, TILE)
                    d_hid = (dot_nt(cot_v[rds, :], down_v[jds, :]) * slope[:, jds]).astype(LOW)
                    dh_v[rds, jds] = d_hid
                    sv_v[S_UP : S_UP + 1, jds] += jnp.sum(d_hid.astype(F32), axis=0, keepdims=True)

                tick(4 * r)

            for copy in put_n(steps - 1):
                copy.wait()

        pl.run_scoped(
            forward_phase,
            pltpu.VMEM((ff, cols), LOW), pltpu.VMEM((att, cols), LOW),
            pltpu.VMEM((2, BLOCK, cols), LOW), pltpu.VMEM((PER, CH, cols), F32),
            pltpu.VMEM((BLOCK, cols), LOW), pltpu.VMEM((BLOCK, cols), LOW), pltpu.VMEM((BLOCK, ff), LOW),
            pltpu.VMEM((BLOCK, ff), F32), pltpu.VMEM((BLOCK, att), LOW), pltpu.SemaphoreType.DMA((2,)),
        )
        done = 4 * (steps - 1) + 1

        def lanes(ref, e):
            if width % 128 == 0:
                return ref[:, at_tile(e, width)]
            pair = ref[:, at_tile(lax.div(e, 2), 2 * width)]
            odd = lax.rem(e, 2) == 1
            return jnp.where(odd, pair[:, width:].astype(F32), pair[:, :width].astype(F32)).astype(LOW)

        def by_rows(right_ref):
            def compute(e, into, add):
                right = lanes(right_ref, e)

                @pl.loop(0, (ff + att) // TILE)
                def _(j):
                    part = dot_nn(a_t[at_tile(j, TILE), :], right)
                    if add:
                        part = part + into[at_tile(j, TILE), :]
                    into[at_tile(j, TILE), :] = part

            return compute

        def by_columns(left_ref, right_ref):
            def compute(e, into, add):
                left = lanes(left_ref, e).T

                @pl.loop(0, right_ref.shape[1] // TILE)
                def _(j):
                    part = dot_nn(left, right_ref[:, at_tile(j, TILE)])
                    if add:
                        part = part + into[:, at_tile(j, TILE)]
                    into[:, at_tile(j, TILE)] = part

            return compute

        def give(group, i, buf, got):
            return pltpu.make_async_remote_copy(
                src_ref=buf.at[0], dst_ref=got.at[i], send_sem=sa.at[group], recv_sem=ra.at[group * half + i],
                device_id=(mate, t), device_id_type=MESH)

        def mate_slice(group, i, buf, got, compute, again):
            @pl.when(again)
            def _():
                give(group, i, buf, got).wait_send()

            compute(2 * i + 1 - parity, buf.at[0], False)
            give(group, i, buf, got).start()

        def fetch(group, i, buf, got):
            return pltpu.make_async_copy(got.at[i], buf.at[1], ssem.at[group])

        def get_slice(group, i, buf, got):
            give(group, i, buf, got).wait_recv()
            fetch(group, i, buf, got).start()

        def put(group, i, buf, there):
            return pltpu.make_async_copy(buf.at[1], there.at[i], ssem.at[3 + group])

        def own_slice(group, i, buf, got, keep, out, compute):
            fetch(group, i, buf, got).wait()
            compute(2 * i + parity, buf.at[1], True)

            @pl.when(i == here)
            def _():
                put(group, i, buf, out).start()

            @pl.when(i != here)
            def _():
                put(group, i, buf, keep).start()

        def pass_slice(group, i, buf, keep, out):
            put(group, i, buf, keep).wait()

            @pl.when(i != here)
            def _():
                pltpu.make_async_remote_copy(
                    src_ref=keep.at[i], dst_ref=out.at[here], send_sem=sb.at[group * half + i],
                    recv_sem=rb.at[group * half + here], device_id=(2 * i + parity, t), device_id_type=MESH).start()

        def turn_of(i):
            return lax.bitwise_xor(here, half - 1 - lax.rem(i, half))

        def first_grads(n2_v, sd, su, gsem):
            load_n2 = pltpu.make_async_copy(n2_h, n2_v, gsem)
            load_n2.start()
            rows_of, columns_of = by_rows(cot_v), by_columns(n2_v, dh_v)

            @pl.loop(0, half + 1)
            def _(i):
                now, before = turn_of(i), turn_of(i + half - 1)

                @pl.when(i > 0)
                def _():
                    get_slice(0, before, sd, ad_h)

                @pl.when(i < half)
                def _():
                    mate_slice(0, now, sd, ad_h, rows_of, i > 0)

                @pl.when(i < PACED)
                def _():
                    tick(done + jnp.maximum(3 * i - 1, 0))

                @pl.when(i > 0)
                def _():
                    own_slice(0, before, sd, ad_h, bd_h, gd_h, rows_of)
                    get_slice(1, before, su, au_h)

                @pl.when(i == 0)
                def _():
                    load_n2.wait()

                @pl.when(i < half)
                def _():
                    mate_slice(1, now, su, au_h, columns_of, i > 0)

                @pl.when(i < PACED)
                def _():
                    tick(done + jnp.maximum(3 * i, 1))

                @pl.when(i > 0)
                def _():
                    pass_slice(0, before, sd, bd_h, gd_h)
                    own_slice(1, before, su, au_h, bu_h, gu_h, columns_of)

                    @pl.when(i <= PACED)
                    def _():
                        tick(done + jnp.minimum(3 * i + 1, 3 * PACED - 1))

                    pass_slice(1, before, su, bu_h, gu_h)

            give(0, 0, sd, ad_h).wait_send()
            give(1, 0, su, au_h).wait_send()

        pl.run_scoped(
            first_grads, pltpu.VMEM((rows, cols), LOW), pltpu.VMEM((2, ff + att, width), F32),
            pltpu.VMEM((2, width, ff), F32), pltpu.SemaphoreType.DMA,
        )
        done2 = done + 3 * PACED

        def back_phase(dk, dv):
            for h in range(heads):
                dk[...] = jnp.zeros_like(dk)
                dv[...] = jnp.zeros_like(dv)

                @pl.loop(0, steps)
                def _(r):
                    rds, kds = at_tile(r, BLOCK), seen(r)
                    query, keys, values = q_v[h, rds, :], k_v[h, kds, :], v_v[h, kds, :]
                    d_ctx = do_v[rds, h * HS : (h + 1) * HS]
                    scores = jnp.where(allowed(r), dot_nt(query, keys) * score_scale, MASKED_SCORE)
                    probs = jnp.exp(scores - lse_v[rds, h * 64 : h * 64 + 1])
                    dv[kds, :] += dot_nn(probs.astype(LOW).T, d_ctx)
                    d_probs = dot_nt(d_ctx, values)
                    inner = jnp.sum(probs * d_probs, axis=-1, keepdims=True)
                    d_scores = (probs * (d_probs - inner)).astype(LOW)
                    d_query = dot_nn(d_scores, keys) * score_scale
                    d_query = turn(d_query, turn_tables(rot_v[rds, :]), -1).astype(LOW)
                    dq_v[rds, pl.ds(3 * h * HS, HS)] = d_query
                    dk[kds, :] += dot_nn(d_scores.T, query) * score_scale
                    there = pl.ds(3 * h * HS, HS)
                    sv_v[S_QKV : S_QKV + 1, there] += jnp.sum(d_query.astype(F32), axis=0, keepdims=True)

                if h == 0:
                    tick(done2)

                @pl.loop(0, steps)
                def _(r):
                    rds = at_tile(r, BLOCK)
                    d_key = turn(dk[rds, :], turn_tables(rot_v[rds, :]), -1).astype(LOW)
                    d_value = dv[rds, :].astype(LOW)
                    for part, got in ((1, d_key), (2, d_value)):
                        there = pl.ds((3 * h + part) * HS, HS)
                        dq_v[rds, there] = got
                        sv_v[S_QKV : S_QKV + 1, there] += jnp.sum(got.astype(F32), axis=0, keepdims=True)

                if h == 0 or h == heads - 1:
                    tick(done2 + (1 if h == 0 else 2))

        pl.run_scoped(back_phase, pltpu.VMEM((rows, HS), F32), pltpu.VMEM((rows, HS), F32))
        done3 = done2 + 3

        def norm_phase(n1_v, nsem1, xs, pst, xhat, rstd, m1, m2, xsem):
            load_x(0, xs, xsem).start()
            pltpu.make_async_copy(n1_h, n1_v, nsem1).start()

            @pl.loop(0, steps)
            def _(r):
                rds = at_tile(r, BLOCK)
                xcur = xs.at[lax.rem(r, 2)]
                load_x(r, xs, xsem).wait()

                @pl.when(r + 1 < steps)
                def _():
                    load_x(r + 1, xs, xsem).start()

                @pl.loop(0, BLOCK // SUB, unroll=2)
                def _(s):
                    sds = at_tile(s, SUB)
                    xf = xcur[sds, :].astype(F32)
                    centre = xf - jnp.mean(xf, axis=-1, keepdims=True)
                    inv = lax.rsqrt(jnp.mean(centre * centre, axis=-1, keepdims=True) + EPSILON)
                    xhat[sds, :] = centre * inv
                    rstd[sds, :] = jnp.broadcast_to(inv, (SUB, 128))

                m1[...] = jnp.zeros_like(m1)
                m2[...] = jnp.zeros_like(m2)

                @pl.when(r > 1)
                def _():
                    put_p(r - 1, 1, pst).wait()

                @pl.loop(0, dtile)
                def _(j):
                    jds = at_tile(j, TILE)
                    xh = xhat[:, jds]
                    second = dot_nt(dh_v[rds, :], up_v[jds, :])
                    sv_v[S_GAIN2 : S_GAIN2 + 1, jds] += jnp.sum(second * xh, axis=0, keepdims=True)
                    sv_v[S_BIAS2 : S_BIAS2 + 1, jds] += jnp.sum(second, axis=0, keepdims=True)
                    first = dot_nt(dq_v[rds, :], qkv_v[jds, :])
                    sv_v[S_GAIN1 : S_GAIN1 + 1, jds] += jnp.sum(first * xh, axis=0, keepdims=True)
                    sv_v[S_BIAS1 : S_BIAS1 + 1, jds] += jnp.sum(first, axis=0, keepdims=True)
                    cot_tile = cot_v[rds, jds].astype(F32)
                    sv_v[S_OUT : S_OUT + 1, jds] += jnp.sum(cot_tile, axis=0, keepdims=True)
                    scaled = second * vec[V_GAIN2 : V_GAIN2 + 1, jds] + first * vec[V_GAIN1 : V_GAIN1 + 1, jds]
                    pst[:, :, jds] = scaled.reshape(PER, CH, TILE)
                    with_xh = scaled * xh
                    for q in range(TILE // 128):
                        m1[...] += scaled[:, q * 128 : (q + 1) * 128]
                        m2[...] += with_xh[:, q * 128 : (q + 1) * 128]

                tick(done3 + 2 * r)

                @pl.loop(0, PER)
                def _(s):
                    sds = at_tile(s, CH)
                    mean1 = jnp.sum(m1[sds, :], axis=-1, keepdims=True) * (1.0 / cols)
                    mean2 = jnp.sum(m2[sds, :], axis=-1, keepdims=True) * (1.0 / cols)
                    grad = rstd[sds, 0:1] * (pst[s] - mean1 - xhat[sds, :] * mean2)
                    cot_rows = cot_v[pl.ds(pl.multiple_of(r * BLOCK + s * CH, CH), CH), :].astype(F32)
                    pst[s] = grad + add_here * cot_rows

                put_p(r, 1, pst).start()

                @pl.when(r == 0)
                def _():
                    put_p(r, 1, pst).wait()

                tick(done3 + 2 * r + 1)

            put_p(steps - 1, 1, pst).wait()

        done4 = done3 + 2 * steps

        def last_grads(n1_v, nsem1, sq):
            pltpu.make_async_copy(n1_h, n1_v, nsem1).wait()
            columns_of = by_columns(n1_v, dq_v)

            @pl.loop(0, half + 1)
            def _(i):
                now, before = turn_of(i), turn_of(i + half - 1)

                @pl.when(i > 0)
                def _():
                    get_slice(2, before, sq, aq_h)

                @pl.when(i < half)
                def _():
                    mate_slice(2, now, sq, aq_h, columns_of, i > 0)

                @pl.when(i < PACED)
                def _():
                    tick(done4 + jnp.maximum(2 * i - 1, 0))

                @pl.when(i > 0)
                def _():
                    own_slice(2, before, sq, aq_h, bq_h, gq_h, columns_of)

                    @pl.when(i <= PACED)
                    def _():
                        tick(done4 + jnp.minimum(2 * i, 2 * PACED - 1))

                    pass_slice(2, before, sq, bq_h, gq_h)

            give(2, 0, sq, aq_h).wait_send()

        def small_sums():
            sv_v[S_STATS : S_STATS + 1, :] += (
                jnp.sum(csq_v[...]) * vec[V_CTX : V_CTX + 1, :]
                + jnp.sum(sq_v[...]) * vec[V_ACT : V_ACT + 1, :]
                + vec[V_COUNT : V_COUNT + 1, :]
            )
            svd[d] = sv_v[...]

            @pl.loop(1, ndp)
            def _(k):
                give_dp(k).start()

        def with_n1(n1_v, nsem1):
            pl.run_scoped(
                functools.partial(norm_phase, n1_v, nsem1),
                pltpu.VMEM((2, BLOCK, cols), LOW), pltpu.VMEM((PER, CH, cols), F32), pltpu.VMEM((BLOCK, cols), F32),
                pltpu.VMEM((BLOCK, 128), F32), pltpu.VMEM((BLOCK, 128), F32), pltpu.VMEM((BLOCK, 128), F32),
                pltpu.SemaphoreType.DMA((2,)),
            )
            small_sums()
            pl.run_scoped(functools.partial(last_grads, n1_v, nsem1), pltpu.VMEM((2, width, qw), F32))

        pl.run_scoped(with_n1, pltpu.VMEM((rows, cols), LOW), pltpu.SemaphoreType.DMA)

    def give_dp(k):
        return pltpu.make_async_remote_copy(
            src_ref=sv_v, dst_ref=svd.at[d], send_sem=ssv.at[k], recv_sem=rsv.at[d],
            device_id=(lax.rem(d + k, ndp), t), device_id_type=MESH)

    def get_dp(k):
        other = lax.rem(d + k, ndp)
        return pltpu.make_async_remote_copy(
            src_ref=sv_v, dst_ref=svd.at[other], send_sem=ssv.at[k], recv_sem=rsv.at[other],
            device_id=(other, t), device_id_type=MESH)

    pl.run_scoped(with_inputs, pltpu.VMEM((cols, ff), LOW), pltpu.VMEM((cols, qw), LOW))
    finished = 4 * (steps - 1) + 1 + 3 * PACED + 3 + 2 * steps + 2 * PACED
    tiles_down, tiles_up, tiles_qkv = (ff + att) // TILE, ff // TILE, qw // TILE
    before_last = chunks - tiles_down - tiles_up - 5

    @pl.loop(finished, before_last)
    def _(k):
        tick(k)

    def give_z(k):
        return pltpu.make_async_remote_copy(
            src_ref=sv_o.at[0], dst_ref=svz.at[t], send_sem=ssz.at[k], recv_sem=rsz.at[t],
            device_id=(d, lax.rem(t + k, 4)), device_id_type=MESH)

    def get_z(k):
        other = lax.rem(t + k, 4)
        return pltpu.make_async_remote_copy(
            src_ref=sv_o.at[0], dst_ref=svz.at[other], send_sem=ssz.at[k], recv_sem=rsz.at[other],
            device_id=(d, other), device_id_type=MESH)

    def small_totals():
        @pl.loop(1, ndp)
        def _(k):
            get_dp(k).wait_recv()
            give_dp(k).wait_send()

        total = svd[0]
        for i in range(1, ndp):
            total = total + svd[i]
        sv_o[0] = total
        svz[t] = total
        for k in range(1, 4):
            give_z(k).start()

    def landed(group, keep, out):
        @pl.loop(0, half)
        def _(i):
            @pl.when(i != here)
            def _():
                sent = pltpu.make_async_remote_copy(
                    src_ref=keep.at[i], dst_ref=out.at[i], send_sem=sb.at[group * half + i],
                    recv_sem=rb.at[group * half + i], device_id=(2 * i + parity, t), device_id_type=MESH)
                sent.wait_send()
                sent.wait_recv()

    def sum_phase(tall, tall_sum, wide, wide_sum, fsem, usem):
        def tiles_d():
            for j in range((ff + att) // TILE):
                there = down_g.at[pl.ds(j * TILE, TILE)] if j < ff // TILE else dense_g.at[pl.ds(j * TILE - ff, TILE)]
                yield gd_h.at[:, pl.ds(j * TILE, TILE)], there

        def tiles_w(got, result):
            for j in range(got.shape[2] // TILE):
                yield got.at[:, :, pl.ds(j * TILE, TILE)], result.at[:, pl.ds(j * TILE, TILE)]

        def add_up(pairs, parts, total):
            pairs = list(pairs)

            def get(j):
                return pltpu.make_async_copy(pairs[j][0], parts.at[j % 2], fsem.at[j % 2])

            def put_sum(j):
                return pltpu.make_async_copy(total.at[j % 2], pairs[j][1], usem.at[j % 2])

            get(0).start()
            for j in range(len(pairs)):
                if j + 1 < len(pairs):
                    get(j + 1).start()
                get(j).wait()
                if j >= 2:
                    put_sum(j - 2).wait()
                acc = parts[j % 2, 0]
                for i in range(1, half):
                    acc = acc + parts[j % 2, i]
                total[j % 2] = acc
                put_sum(j).start()
                yield
            for j in range(max(len(pairs) - 2, 0), len(pairs)):
                put_sum(j).wait()

        at = before_last
        for group, keep, out, work in (
            (0, bd_h, gd_h, lambda: add_up(tiles_d(), tall, tall_sum)),
            (1, bu_h, gu_h, lambda: add_up(tiles_w(gu_h, up_g), wide, wide_sum)),
            (2, bq_h, gq_h, lambda: add_up(tiles_w(gq_h, qkv_g), wide, wide_sum)),
        ):
            if group == 2:
                small_totals()

                @pl.loop(at, chunks + BACK)
                def _(k):
                    tick(k)

                at = chunks + BACK
            landed(group, keep, out)
            for _ in work():
                tick(at)
                at += 1

    pl.run_scoped(
        sum_phase,
        pltpu.VMEM((2, half, TILE, width), F32), pltpu.VMEM((2, TILE, width), F32),
        pltpu.VMEM((2, half, width, TILE), F32), pltpu.VMEM((2, width, TILE), F32),
        pltpu.SemaphoreType.DMA((2,)), pltpu.SemaphoreType.DMA((2,)),
    )

    @pl.loop(chunks + BACK + tiles_qkv, chunks + LAG)
    def _(k):
        tick(k)

    for k in range(1, 4):
        get_z(k).wait_recv()
        give_z(k).wait_send()
    sv_o[1] = svz[0] + svz[1] + svz[2] + svz[3]

    @pl.when(mid)
    def _():
        @pl.loop(chunks - HELD, chunks)
        def _(k):
            send_sum(k).wait_send()

    store(chunks - 2).wait()
    store(chunks - 1).wait()


def layer(ndp, vectors, segments, subsets, x, cot, rot, up_w, down_w, dense_w, qkv_w):
    rows, cols = x.shape
    ff, att, qw = up_w.shape[1], dense_w.shape[0], qkv_w.shape[1]
    heads = att // HS
    width, half, steps, chunks = cols // ndp, ndp // 2, rows // BLOCK, 2 * rows // CH
    any_spec = pl.BlockSpec(memory_space=pl.ANY)
    vmem_spec = pl.BlockSpec(memory_space=pltpu.VMEM)
    sem = pltpu.SemaphoreType.DMA
    slices = [
        jax.ShapeDtypeStruct((half, ff + att, width), F32),
        jax.ShapeDtypeStruct((half, width, ff), F32),
        jax.ShapeDtypeStruct((half, width, qw), F32),
    ]
    return pl.pallas_call(
        functools.partial(layer_kernel, ndp),
        out_shape=[
            jax.ShapeDtypeStruct((chunks, CH, cols), LOW),
            jax.ShapeDtypeStruct((2, SV, cols), F32),
            jax.ShapeDtypeStruct((ff, width), F32),
            jax.ShapeDtypeStruct((att, width), F32),
            jax.ShapeDtypeStruct((width, ff), F32),
            jax.ShapeDtypeStruct((width, qw), F32),
            *slices,
            jax.ShapeDtypeStruct((chunks, CH, cols), F32),
            jax.ShapeDtypeStruct((rows, cols), LOW),
            jax.ShapeDtypeStruct((rows, cols), LOW),
            *slices,
            *slices,
        ],
        in_specs=[vmem_spec] * 9 + [pl.BlockSpec(memory_space=pltpu.SMEM)] + [any_spec] * 7,
        out_specs=[any_spec, vmem_spec] + [any_spec] * 16,
        scratch_shapes=[
            pltpu.VMEM((VROWS, cols), F32), pltpu.VMEM((1, rows), F32),
            pltpu.VMEM((ff + att, rows), LOW), pltpu.VMEM((rows, cols), LOW), pltpu.VMEM((rows, ff), LOW),
            pltpu.VMEM((rows, qw), LOW), pltpu.VMEM((heads, rows, HS), LOW), pltpu.VMEM((heads, rows, HS), LOW),
            pltpu.VMEM((heads, rows, HS), LOW), pltpu.VMEM((rows, att), LOW), pltpu.VMEM((rows, 64 * heads), F32),
            pltpu.VMEM((rows, 128), F32), pltpu.VMEM((SV, cols), F32),
            pltpu.VMEM((8, TILE), F32), pltpu.VMEM((8, HS), F32),
            pltpu.VMEM((ndp, SV, cols), F32), pltpu.VMEM((4, SV, cols), F32),
            pltpu.VMEM((WINDOW, CH, cols), F32), pltpu.VMEM((WINDOW, CH, cols), F32),
            pltpu.VMEM((2, CH, cols), F32), pltpu.VMEM((2, CH, cols), LOW),
            sem((WINDOW,)), sem((WINDOW,)), sem((WINDOW,)), sem((WINDOW,)), sem((2,)), sem((2,)),
            sem((steps + 1,)), sem((2 * (ff // TILE) + 2,)), sem, sem((2,)),
            sem((ndp,)), sem((ndp,)), sem((4,)), sem((4,)),
            sem((3,)), sem((3 * half,)), sem((3 * half,)), sem((3 * half,)), sem((6,)),
        ],
        compiler_params=pltpu.CompilerParams(
            collective_id=0, has_side_effects=True, vmem_limit_bytes=VMEM_ASK),
        cost_estimate=pl.CostEstimate(flops=10**11, bytes_accessed=2 * 10**8, transcendentals=0),
        name="layer",
    )(*vectors, segments, subsets, x, cot, rot, up_w, down_w, dense_w, qkv_w)


def flat_shape(size):
    return (1, size) if size % 1024 == 0 else (size,)


SMALL_ROWS = ((1, S_GAIN1), (1, S_BIAS1), (0, S_QKV), (0, S_OUT), (1, S_GAIN2), (1, S_BIAS2), (0, S_UP), (0, S_OUT))


def finish_kernel(o_h, down_h, dense_h, up_h, qkv_h, small, *rest):
    out, grad, down_g, dense_g, up_g, qkv_g = rest[:6]
    row_refs, rms, held, sems_in, sems_out = rest[6:14], rest[14], rest[15:21], rest[21], rest[22]
    half_chunks = out.shape[0]
    copies = []
    for index, (source, target) in enumerate((
        (o_h.at[pl.ds(0, half_chunks)], out), (o_h.at[pl.ds(half_chunks, half_chunks)], grad),
        (down_h, down_g), (dense_h, dense_g), (up_h, up_g), (qkv_h, qkv_g),
    )):
        count = source.shape[0] // PIECES
        for piece in range(PIECES):
            at = pl.ds(piece * count, count)
            buf, sem = held[index].at[at], PIECES * index + piece
            copies.append((
                pltpu.make_async_copy(source.at[at], buf, sems_in.at[sem]),
                pltpu.make_async_copy(buf, target.at[at], sems_out.at[sem]),
            ))
    for load, _ in copies[:DEPTH]:
        load.start()
    for (which, row), ref in zip(SMALL_ROWS, row_refs):
        if len(ref.shape) == 1:
            ref[...] = small[which, row, pl.ds(0, ref.shape[0])]
        else:
            ref[...] = small[which, row : row + 1, pl.ds(0, ref.shape[1])]
    lane = lax.broadcasted_iota(jnp.int32, (128, 128), 1)
    place = lax.broadcasted_iota(jnp.int32, (128, 128), 0)
    stats = jnp.broadcast_to(small[1, S_STATS : S_STATS + 1, :128], (8, 128)).T[:, 0:1]
    context, active, count = (
        jnp.sum(jnp.where(place == 3 * lane + part, stats, 0.0), axis=0, keepdims=True) for part in range(3)
    )
    count = jnp.maximum(count, 1.0)
    rms[0:1, :] = jnp.sqrt(context / (count * (HEADS * HS)))[:, :SUBSETS]
    rms[1:2, :] = jnp.sqrt(active / (count * FF))[:, :SUBSETS]
    for index, (load, save) in enumerate(copies):
        load.wait()
        save.start()
        if index + DEPTH < len(copies):
            copies[index + DEPTH][0].start()
    for _, save in copies:
        save.wait()


PIECES = 4
DEPTH = 8


def finish(sums, small, down_grad, dense_grad, up_grad, qkv_grad):
    chunks, per, cols = sums.shape
    grads = (down_grad, dense_grad, up_grad, qkv_grad)
    qw, ff = qkv_grad.shape[1], up_grad.shape[1]
    any_spec = pl.BlockSpec(memory_space=pl.ANY)
    vmem_spec = pl.BlockSpec(memory_space=pltpu.VMEM)
    row_widths = [cols, cols, qw, cols, cols, cols, ff, cols]
    return pl.pallas_call(
        finish_kernel,
        out_shape=[jax.ShapeDtypeStruct((chunks // 2, per, cols), LOW)] * 2
        + [jax.ShapeDtypeStruct(grad.shape, F32) for grad in grads]
        + [jax.ShapeDtypeStruct(flat_shape(row_width), F32) for row_width in row_widths]
        + [jax.ShapeDtypeStruct((2, SUBSETS), F32)],
        in_specs=[any_spec] * 5 + [vmem_spec],
        out_specs=[any_spec] * 6 + [vmem_spec] * 9,
        scratch_shapes=[pltpu.VMEM((chunks // 2, per, cols), LOW)] * 2
        + [pltpu.VMEM(grad.shape, F32) for grad in grads]
        + [pltpu.SemaphoreType.DMA((6 * PIECES,))] * 2,
        compiler_params=pltpu.CompilerParams(vmem_limit_bytes=VMEM_ASK),
        name="finish",
    )(sums, *grads, small)


def turn_table(length):
    frequency = np.float32(10000.0) ** (-(np.float32(2.0) * np.arange(ROT // 2, dtype=np.float32)) / np.float32(ROT))
    angles = np.arange(length, dtype=np.float32)[:, None] * frequency.astype(np.float32)[None, :]
    angles = np.concatenate([angles, angles], axis=1).astype(np.float32)
    return np.concatenate([np.cos(angles), np.sin(angles)], axis=1).astype(np.float32)


def on_device(
    ndp,
    inputs,
    cotangent,
    segments,
    subsets,
    ln1_gain,
    ln1_bias,
    qkv_weight,
    qkv_bias,
    dense_weight,
    dense_bias,
    ln2_gain,
    ln2_bias,
    up_weight,
    up_bias,
    down_weight,
    down_bias,
):
    rows_here, model = inputs.shape
    vectors = [
        values.reshape(flat_shape(values.shape[0]))
        for values in (up_bias, qkv_bias, ln1_gain, ln1_bias, ln2_gain, ln2_bias, dense_bias, down_bias)
    ]
    held = layer(
        ndp, vectors, segments, subsets, inputs, cotangent, jnp.asarray(turn_table(LEN)),
        up_weight, down_weight, dense_weight, qkv_weight)[:6]
    done = finish(*held)
    out, input_grad, down_grad, dense_grad, up_grad, qkv_grad = done[:6]
    gain1, bias1, qkv_bias_grad, bias_out, gain2, bias2, up_bias_grad, bias_out_again = (
        row.reshape(-1) for row in done[6:14]
    )
    return (
        out.reshape(rows_here, model),
        input_grad.reshape(rows_here, model),
        gain1,
        bias1,
        qkv_grad,
        qkv_bias_grad,
        dense_grad,
        bias_out,
        gain2,
        bias2,
        up_grad,
        up_bias_grad,
        down_grad,
        bias_out_again,
        done[14].T,
    )


def solution(mesh):
    placed = (
        P("dp", None),
        P("dp", None),
        P("dp", None),
        P("dp"),
        P(),
        P(),
        P(None, "tensor"),
        P("tensor"),
        P("tensor", None),
        P(),
        P(),
        P(),
        P(None, "tensor"),
        P("tensor"),
        P("tensor", None),
        P(),
    )
    return jax.shard_map(
        functools.partial(on_device, mesh.shape["dp"]),
        mesh=mesh,
        in_specs=placed,
        out_specs=(
            P("dp", None),
            P("dp", None),
            P(),
            P(),
            P("dp", "tensor"),
            P("tensor"),
            P("tensor", "dp"),
            P(),
            P(),
            P(),
            P("dp", "tensor"),
            P("tensor"),
            P("tensor", "dp"),
            P(),
            P(),
        ),
        check_vma=False,
    )
```
